128 devices in a mesh: row: 8 (over z, y_lo), col: 16 (over y_hi, x, core).
Axes of the slice: x: 4, y: 4 (y_hi: 2, y_lo: 2; y = y_hi * 2 + y_lo), z: 4, core: 2. Of those that a mesh axis runs over, the one named last changes fastest.
Arguments:
- layer_input: bfloat16 [16, 1024, 1024], P('col', 'row'), may hold values from -6 to 6
- prenorm: float32 [1024], replicated, may hold values from 0.25 to 1.75
- query_proj: bfloat16 [1024, 1024], P('col', 'row'), may hold values from -0.1875 to 0.1875
- key_proj: bfloat16 [1024, 512], P('col', 'row'), may hold values from -0.1875 to 0.1875
- value_proj: bfloat16 [1024, 512], P('col', 'row'), may hold values from -0.1875 to 0.1875
- querynorm: float32 [64], replicated, may hold values from 0.5 to 2
- keynorm: float32 [64], replicated, may hold values from 0.5 to 2
- out_proj: bfloat16 [1024, 1024], P('row', 'col'), may hold values from -3 to 3
- midnorm: float32 [1024], replicated, may hold values from 0.25 to 1.75
- router: bfloat16 [1024, 32], P('col'), may hold values from -0.09375 to 0.09375
- gate_proj: bfloat16 [32, 1024, 512], P('row', 'col'), may hold values from -0.1875 to 0.1875
- up_proj: bfloat16 [32, 1024, 512], P('row', 'col'), may hold values from -0.1875 to 0.1875
- down_proj: bfloat16 [32, 512, 1024], P('row', None, 'col'), may hold values from -6 to 6
- routes: int32 [16, 1024, 8], P('col'), may hold values from 0 to 31, as said below
- slot_ids: int32 [16, 1024, 8], P('col'), may hold values from 0 to 447, as said below
- prefix: int32 [16], P('col'), may hold values from 1 to 1024
- cotangent: bfloat16 [16, 1024, 1024], P('col', 'row'), may hold values from -6 to 6
Outputs:
- layer_output: bfloat16 [16, 1024, 1024], P('col', 'row')
- input_grad: float32 [16, 1024, 1024], P('col', 'row')
- prenorm_grad: float32 [1024], replicated
- query_grad: float32 [1024, 1024], P('col', 'row')
- key_grad: float32 [1024, 512], P('col', 'row')
- value_grad: float32 [1024, 512], P('col', 'row')
- querynorm_grad: float32 [64], replicated
- keynorm_grad: float32 [64], replicated
- out_grad: float32 [1024, 1024], P('row', 'col')
- midnorm_grad: float32 [1024], replicated
- router_grad: float32 [1024, 32], P('col')
- gate_grad: float32 [32, 1024, 512], P('row', 'col')
- up_grad: float32 [32, 1024, 512], P('row', 'col')
- down_grad: float32 [32, 512, 1024], P('row', None, 'col')
The draws below stay inside these ranges and needn't reach their ends.
Inputs may be any that keep to these rules, and one draw needn't show every extreme that they name: `routes`: each token names 8 different experts. In each group of 1 sequence (those of one index of col), every expert is named by at least one and at most 448 tokens, and some expert by exactly 448. `slot_ids`: for each choice of a token, a slot of that expert's 448 slots for the token's group of 1 sequence; within a group no two choices share both expert and slot.
All inputs are finite; a program needn't handle non-finite values.
Results may differ from the reference program's by a relative error of at most 0.023.
Values may be sent and summed in bfloat16 or wider, within the bound.
No kernel may reach another device: no remote copies, remote signals or barrier semaphores. Data moves between devices by JAX's collectives and lax.ppermute only.
A program may use at most 128 MiB of HBM per device.

```python
import math
import jax
import jax.numpy as jnp
from jax import lax

D = 1024
H = 16
KV = 8
HD = 64
E = 32
FF = 512
TOP = 8
SEQ = 1024
SEQS = 1
NSEQ = 16
CAP = 448


def group_routes(key):
    tokens = SEQS * SEQ
    assigned = tokens * TOP
    mean_load = assigned // E
    spread = CAP - mean_load
    key_loads, key_labels, key_slots, key_tokens = jax.random.split(key, 4)
    pair_ids = jnp.arange(E // 2, dtype=jnp.int32)
    offsets = spread - 2 * spread * pair_ids // (E - 1)
    head_room = (spread - offsets) // 2 + 1
    jitter = jax.random.randint(key_loads, (E // 2,), 0, head_room)
    jitter = jnp.where(pair_ids == 0, 0, jitter)
    upper_half = mean_load + offsets + jitter
    lower_half = mean_load - offsets - jitter
    run_loads = jnp.concatenate([upper_half, lower_half[::-1]]).astype(jnp.int32)
    run_ends = jnp.cumsum(run_loads)
    run_starts = run_ends - run_loads
    positions = jnp.arange(assigned, dtype=jnp.int32)
    run_ids = jnp.sum((positions[:, None] >= run_ends[None, :]).astype(jnp.int32), axis=1)
    run_rank = positions - run_starts[run_ids]
    labels = jax.random.permutation(key_labels, E).astype(jnp.int32)
    order_keys = jax.random.randint(key_slots, (E, CAP), 0, 1 << 16) * CAP + jnp.arange(CAP, dtype=jnp.int32)[None, :]
    slot_orders = jnp.argsort(order_keys, axis=1).astype(jnp.int32)
    token_order = jax.random.permutation(key_tokens, tokens).astype(jnp.int32)
    token_ids = token_order[positions % tokens]
    pick_ids = positions // tokens
    routes_group = jnp.zeros((tokens, TOP), jnp.int32).at[token_ids, pick_ids].set(labels[run_ids])
    slots_group = jnp.zeros((tokens, TOP), jnp.int32).at[token_ids, pick_ids].set(slot_orders[run_ids, run_rank])
    return (routes_group, slots_group)


def route_parts(key):
    group_keys = jax.random.split(key, NSEQ // SEQS)
    routes_all, slots_all = jax.vmap(group_routes)(group_keys)
    return (routes_all.reshape(NSEQ, SEQ, TOP), slots_all.reshape(NSEQ, SEQ, TOP))


def draw_routes(key, part):
    return route_parts(key)[0]


def draw_slot_ids(key, part):
    return route_parts(key)[1]


def set_ends(drawn, stream_key, least, largest):
    extent = drawn.shape
    spot = [jax.random.randint(jax.random.fold_in(stream_key, axis), (), 0, extent[axis]) for axis in range(len(extent))]
    drawn = drawn.at[tuple(spot)].set(least)
    longest = extent.index(max(extent))
    spot[longest] = (spot[longest] + 1) % extent[longest]
    return drawn.at[tuple(spot)].set(largest)


def block_levels(stream_key, dims, pieces, least, high):
    gain = 1.0
    for position, shards_of in pieces:
        steps = jax.random.uniform(jax.random.fold_in(jax.random.fold_in(stream_key, 6), position), (shards_of,), jnp.float32, least / len(pieces), high / len(pieces))
        gain = gain * jnp.repeat(jnp.exp(steps), dims[position] // shards_of).reshape((-1,) + (1,) * (len(dims) - 1 - position))
    return gain


def gaussian(own_key, extent, scale, bound, cuts=(), kind=jnp.bfloat16):
    values = scale * jax.random.normal(own_key, extent, jnp.float32)
    if cuts:
        values = values * block_levels(own_key, extent, cuts, -0.22, 0.18)
    return jnp.clip(values, -bound, bound).astype(kind)


def setup_inputs(seed: int = 0) -> dict:
    seeds = jax.random.split(jax.random.key(seed), 18)
    return {
        "layer_input": gaussian(seeds[0], (NSEQ, SEQ, D), 1.0, 6.0, ((0, 16), (1, 8))),
        "prenorm": jnp.clip(1.0 + 0.15 * jax.random.normal(seeds[1], (D,), jnp.float32), 0.25, 1.75),
        "query_proj": gaussian(seeds[2], (D, H * HD), D ** -0.5, 0.1875, ((0, 16), (1, 8))),
        "key_proj": gaussian(seeds[3], (D, KV * HD), D ** -0.5, 0.1875, ((0, 16), (1, 8))),
        "value_proj": gaussian(seeds[4], (D, KV * HD), D ** -0.5, 0.1875, ((0, 16), (1, 8))),
        "querynorm": jnp.clip(jnp.exp(jax.random.uniform(seeds[5], (HD,), jnp.float32, math.log(0.5), math.log(2.0))), 0.5, 2.0),
        "keynorm": jnp.clip(jnp.exp(jax.random.uniform(seeds[6], (HD,), jnp.float32, math.log(0.5), math.log(2.0))), 0.5, 2.0),
        "out_proj": gaussian(seeds[7], (H * HD, D), (H * HD * 4 // SEQ) ** -0.5, 3.0, ((0, 8), (1, 16))),
        "midnorm": jnp.clip(1.0 + 0.15 * jax.random.normal(seeds[8], (D,), jnp.float32), 0.25, 1.75),
        "router": gaussian(seeds[9], (D, E), (4 * D) ** -0.5, 0.09375, ((0, 16),)),
        "gate_proj": gaussian(seeds[10], (E, D, FF), D ** -0.5, 0.1875, ((0, 8), (1, 16))),
        "up_proj": gaussian(seeds[11], (E, D, FF), D ** -0.5, 0.1875, ((0, 8), (1, 16))),
        "down_proj": gaussian(seeds[12], (E, FF, D), (max(1, TOP * FF // (3 * E * E))) ** -0.5, 6.0, ((0, 8), (2, 16))),
        "routes": draw_routes(jax.random.fold_in(seeds[17], 71), 0),
        "slot_ids": draw_slot_ids(jax.random.fold_in(seeds[17], 71), 0),
        "prefix": set_ends(jax.random.randint(seeds[15], (NSEQ,), 1, SEQ + 1), jax.random.fold_in(seeds[15], 1), 1, SEQ).astype(jnp.int32),
        "cotangent": gaussian(seeds[16], (NSEQ, SEQ, D), 1.0, 6.0, ((0, 16), (1, 8))),
    }


epsilon = 1e-06
rope_base = 10000.0
masked_score = -1e+30
highest = lax.Precision.HIGHEST

@jax.custom_vjp
def low(v):
    return lax.optimization_barrier(v.astype(jnp.bfloat16)).astype(jnp.float32)

@jax.custom_vjp
def low_back(v):
    return v

def low_keep(v):
    return (low(v), None)

def low_pass(kept, grad):
    return (grad,)

def back_keep(v):
    return (v, None)

def back_low(kept, grad):
    return (low(grad),)
low.defvjp(low_keep, low_pass)
low_back.defvjp(back_keep, back_low)

def rms_scale(values):
    return lax.rsqrt(lax.optimization_barrier(jnp.mean(values * values, axis=-1, keepdims=True)) + epsilon)

def rope_tables(length, head_width):
    frequency = rope_base ** (-2.0 * jnp.arange(head_width // 2, dtype=jnp.float32) / head_width)
    angles = jnp.arange(length, dtype=jnp.float32)[:, None] * frequency[None, :]
    return (jnp.cos(angles), jnp.sin(angles))

def rotate(values, cosine_table, sine_table):
    half_width = values.shape[-1] // 2
    front_half = values[..., :half_width]
    back_half = values[..., half_width:]
    cosine_table = cosine_table[:, None, :]
    sine_table = sine_table[:, None, :]
    return jnp.concatenate([front_half * cosine_table - back_half * sine_table, back_half * cosine_table + front_half * sine_table], axis=-1)

def attend(query_pre, key_in, value_in, prefix_len, querynorm, keynorm):
    length = query_pre.shape[0]
    query_heads = query_pre.reshape(length, H, HD)
    key_heads = key_in.reshape(length, KV, HD)
    value_heads = value_in.reshape(length, KV, HD)
    cosine_table, sine_table = rope_tables(length, HD)
    query_rot = low(rotate(query_heads * rms_scale(query_heads) * querynorm, cosine_table, sine_table))
    key_rot = low(rotate(key_heads * rms_scale(key_heads) * keynorm, cosine_table, sine_table))
    query_rot = query_rot.reshape(length, KV, H // KV, HD)
    raw_scores = jnp.einsum('qkgd,skd->kgqs', query_rot, key_rot, precision=highest)
    scores = low_back(raw_scores * HD ** (-0.5))
    row_ids = jnp.arange(length, dtype=jnp.int32)[:, None]
    col_ids = jnp.arange(length, dtype=jnp.int32)[None, :]
    visible = (col_ids <= row_ids) | (col_ids < prefix_len)
    scores = jnp.where(visible, scores, masked_score)
    row_max = lax.optimization_barrier(jnp.max(scores, axis=-1, keepdims=True))
    exp_scores = jnp.exp(scores - row_max)
    attn_probs = exp_scores / lax.optimization_barrier(jnp.sum(exp_scores, axis=-1, keepdims=True))
    mixed_out = jnp.einsum('kgqs,skd->qkgd', low(attn_probs), value_heads, precision=highest)
    return mixed_out.reshape(length, H * HD)

def experts(normed, gate_vals, routes, slot_ids, gate_proj, up_proj, down_proj):
    tokens = normed.shape[0]
    target = (routes * CAP + slot_ids).reshape(-1)
    token_ids = jnp.broadcast_to(jnp.arange(tokens, dtype=jnp.int32)[:, None], routes.shape).reshape(-1)
    slot_owner = jnp.full((E * CAP,), tokens, dtype=jnp.int32).at[target].set(token_ids)
    padded = jnp.concatenate([normed, jnp.zeros((1, normed.shape[1]), dtype=jnp.float32)], axis=0)
    buffer = padded[slot_owner].reshape(E, CAP, normed.shape[1])
    gate_pre = low_back(jnp.einsum('ecd,edf->ecf', buffer, gate_proj, precision=highest))
    up_pre = low_back(jnp.einsum('ecd,edf->ecf', buffer, up_proj, precision=highest))
    activation = low(jax.nn.silu(gate_pre) * up_pre)
    expert_out = low_back(jnp.einsum('ecf,efd->ecd', activation, down_proj, precision=highest))
    picked = expert_out.reshape(E * CAP, normed.shape[1])[target].reshape(tokens, TOP, normed.shape[1])
    return lax.optimization_barrier(jnp.sum(gate_vals[:, :, None] * picked, axis=1))

def forward(layer_input, prenorm, query_proj, key_proj, value_proj, querynorm, keynorm, out_proj, midnorm, router, gate_proj, up_proj, down_proj, routes, slot_ids, prefix):
    normed_one = low(layer_input * rms_scale(layer_input) * prenorm)
    query_pre = low_back(jnp.einsum('nsd,df->nsf', normed_one, query_proj, precision=highest))
    key_all = low_back(jnp.einsum('nsd,df->nsf', normed_one, key_proj, precision=highest))
    value_all = low(low_back(jnp.einsum('nsd,df->nsf', normed_one, value_proj, precision=highest)))

    def attend_one(inputs):
        return jax.checkpoint(attend)(inputs[0], inputs[1], inputs[2], inputs[3], querynorm, keynorm)
    attended = low(low_back(lax.map(attend_one, (query_pre, key_all, value_all, prefix))))
    middle = layer_input + low_back(jnp.einsum('nsf,fd->nsd', attended, out_proj, precision=highest))
    normed_two = low(middle * rms_scale(middle) * midnorm)
    logits = jnp.einsum('nsd,de->nse', normed_two, router, precision=highest)
    row_max = lax.optimization_barrier(jnp.max(logits, axis=-1, keepdims=True))
    exp_logits = jnp.exp(logits - row_max)
    gate_probs = exp_logits / lax.optimization_barrier(jnp.sum(exp_logits, axis=-1, keepdims=True))
    choose = routes[..., None] == jnp.arange(E, dtype=jnp.int32)
    gate_vals = low(lax.optimization_barrier(jnp.sum(jnp.where(choose, gate_probs[:, :, None, :], 0.0), axis=-1)))
    groups = NSEQ // SEQS

    def expert_group(inputs):
        return jax.checkpoint(experts)(inputs[0], inputs[1], inputs[2], inputs[3], gate_proj, up_proj, down_proj)
    expert_mix = lax.map(expert_group, (normed_two.reshape(groups, SEQS * SEQ, D), gate_vals.reshape(groups, SEQS * SEQ, TOP), routes.reshape(groups, SEQS * SEQ, TOP), slot_ids.reshape(groups, SEQS * SEQ, TOP)))
    return middle + low_back(expert_mix.reshape(NSEQ, SEQ, D))

def reference(layer_input, prenorm, query_proj, key_proj, value_proj, querynorm, keynorm, out_proj, midnorm, router, gate_proj, up_proj, down_proj, routes, slot_ids, prefix, cotangent):
    floats = [array.astype(jnp.float32) for array in (layer_input, prenorm, query_proj, key_proj, value_proj, querynorm, keynorm, out_proj, midnorm, router, gate_proj, up_proj, down_proj)]

    def forward_all(*params):
        return forward(*params, routes, slot_ids, prefix)
    block_out, pullback = jax.vjp(forward_all, *floats)
    gradients = pullback(cotangent.astype(jnp.float32))
    return (block_out.astype(jnp.bfloat16), gradients[0], gradients[1], gradients[2], gradients[3], gradients[4], gradients[5], gradients[6], gradients[7], gradients[8], gradients[9], gradients[10], gradients[11], gradients[12])
```

```python
import functools

import jax
import jax.numpy as jnp
from jax import lax
from jax.experimental import pallas as pl
from jax.experimental.pallas import tpu as pltpu
from jax.sharding import PartitionSpec as P

HD = 64
CAP = 448
PAD = 512
ROWS = 8
COLS = 16
BLK = 128
LEN = ROWS * BLK
LOCAL = 4
EXPERTS = 32
EPS = 1e-06
BF = jnp.bfloat16
F32 = jnp.float32
VM = pl.BlockSpec(memory_space=pltpu.VMEM)
SM = pl.BlockSpec(memory_space=pltpu.SMEM)
MIB = 1 << 20


def dot(a, b):
    return lax.dot_general(a, b, (((1,), (0,)), ((), ())), preferred_element_type=F32)


def dot_nt(a, b):
    return lax.dot_general(a, b, (((1,), (1,)), ((), ())), preferred_element_type=F32)


def shape(dims, kind):
    return jax.ShapeDtypeStruct(dims, kind)


def call(body, outs, ins, *args, scratch=(), flops=0, moved=0, limit=40, **kwargs):
    return pl.pallas_call(
        body,
        out_shape=outs,
        in_specs=ins,
        scratch_shapes=list(scratch),
        compiler_params=pltpu.CompilerParams(vmem_limit_bytes=limit * MIB),
        cost_estimate=pl.CostEstimate(flops=flops, bytes_accessed=moved, transcendentals=0),
        **kwargs,
    )(*args)


def row_gather(own):
    return [own] + [
        lax.ppermute(own, "row", [(i, (i - k) % ROWS) for i in range(ROWS)])
        for k in range(1, ROWS)
    ]


def row_send(blocks):
    return [blocks[0]] + [
        lax.ppermute(blocks[k], "row", [(i, (i + k) % ROWS) for i in range(ROWS)])
        for k in range(1, ROWS)
    ]


def total(values):
    for axis, count in (("col", COLS), ("row", ROWS)):
        step = 1
        while step < count:
            values = values + lax.ppermute(
                values, axis, [(i, i ^ step) for i in range(count)]
            )
            step *= 2
    return values


def lane_ids(rows):
    return lax.broadcasted_iota(jnp.int32, (rows, 2 * HD), 1)


def half_mean(values, lanes):
    low = jnp.sum(jnp.where(lanes < HD, values, 0.0), axis=-1, keepdims=True)
    high = jnp.sum(jnp.where(lanes < HD, 0.0, values), axis=-1, keepdims=True)
    return jnp.where(lanes < HD, low, high) * (1.0 / HD)


def turn(values, cosine, sine, lanes):
    swapped = jnp.where(
        (lanes & (HD - 1)) < HD // 2,
        pltpu.roll(values, 2 * HD - HD // 2, 1),
        pltpu.roll(values, HD // 2, 1),
    )
    return values * cosine + swapped * sine


def attend_kernel(*refs):
    place = refs[0]
    tokens = refs[1 : 1 + ROWS]
    weight, query_gain, key_gain, cosine, sine = refs[1 + ROWS : 6 + ROWS]
    pre, query, keyval, out = refs[6 + ROWS : 10 + ROWS]
    key_low, key_high, val_low, val_high = refs[10 + ROWS :]
    lanes = lane_ids(BLK)
    for j in range(ROWS):
        rows = pl.ds(j * BLK, BLK)
        block = dot(tokens[j][...], weight[...])
        pre[rows, :] = block
        cos_rows, sin_rows = cosine[rows, :], sine[rows, :]
        q_pre, kv_pre = block[:, : 2 * HD], block[:, 2 * HD :]
        q_scale = lax.rsqrt(half_mean(q_pre * q_pre, lanes) + EPS)
        turned = turn(q_pre * q_scale * query_gain[...], cos_rows, sin_rows, lanes)
        query[rows, :] = turned.astype(BF) * HD ** (-0.5)
        k_scale = lax.rsqrt(half_mean(kv_pre * kv_pre, lanes) + EPS)
        turned = turn(kv_pre * k_scale * key_gain[...], cos_rows, sin_rows, lanes)
        key = jnp.where(lanes < HD, turned, 0.0)
        val = jnp.where(lanes < HD, 0.0, kv_pre)
        keyval[rows, :] = (key + val).astype(BF)
        key_low[rows, :] = key.astype(BF)
        key_high[rows, :] = pltpu.roll(key, HD, 1).astype(BF)
        val_low[rows, :] = pltpu.roll(val, HD, 1).astype(BF)
        val_high[rows, :] = val.astype(BF)
    start, prefix = place[0], place[1]
    size = 2 * BLK
    key_at = (lax.broadcasted_iota(jnp.int32, (size, LEN), 1) + start) & (LEN - 1)

    def step(index, carry):
        rows = pl.ds(pl.multiple_of(index * size, size), size)
        q_rows = query[rows, :]
        at = (lax.broadcasted_iota(jnp.int32, (size, 1), 0) + index * size + start) & (LEN - 1)
        visible = key_at < jnp.maximum(at + 1, prefix)
        mixed = jnp.zeros((size, 2 * HD), F32)
        for keys, vals in ((key_low, val_low), (key_high, val_high)):
            weights = jnp.where(visible, jnp.exp(dot_nt(q_rows, keys[...])), 0.0)
            inverse = 1.0 / jnp.sum(weights, axis=-1, keepdims=True)
            mixed += dot((weights * inverse).astype(BF), vals[...])
        out[rows, :] = mixed.astype(BF)
        return carry

    lax.fori_loop(0, LEN // size, step, 0)


def attend_back_kernel(*refs):
    place = refs[0]
    grads = refs[1 : 1 + ROWS]
    tokens = refs[1 + ROWS : 1 + 2 * ROWS]
    weight, query_gain, key_gain, cosine, sine, pre, query, keyval = refs[
        1 + 2 * ROWS : 9 + 2 * ROWS
    ]
    low, part, pre_sum, gain_sum = refs[9 + 2 * ROWS : 13 + 2 * ROWS]
    key_low, key_high, val_low, val_high, key_t, grad_all, q_grad, kv_grad = refs[13 + 2 * ROWS :]
    lanes = lane_ids(BLK)
    for j in range(ROWS):
        rows = pl.ds(j * BLK, BLK)
        both = keyval[rows, :].astype(F32)
        key = jnp.where(lanes < HD, both, 0.0)
        val = jnp.where(lanes < HD, 0.0, both)
        key_two = pltpu.roll(key, HD, 1)
        key_low[rows, :] = key.astype(BF)
        key_high[rows, :] = key_two.astype(BF)
        val_low[rows, :] = pltpu.roll(val, HD, 1).astype(BF)
        val_high[rows, :] = val.astype(BF)
        key_t[:, j * BLK : (j + 1) * BLK] = (key + key_two).T.astype(BF)
        grad_all[rows, :] = grads[j][...]
    kv_grad[...] = jnp.zeros_like(kv_grad)
    start, prefix = place[0], place[1]
    size = 2 * BLK
    key_at = (lax.broadcasted_iota(jnp.int32, (LEN, size), 0) + start) & (LEN - 1)
    wide = lane_ids(size)

    def step(index, carry):
        rows = pl.ds(pl.multiple_of(index * size, size), size)
        q_rows, g_rows = query[rows, :], grad_all[rows, :]
        q_wide, g_wide = q_rows.astype(F32), g_rows.astype(F32)
        at = (lax.broadcasted_iota(jnp.int32, (1, size), 1) + index * size + start) & (LEN - 1)
        visible = key_at < jnp.maximum(at + 1, prefix)
        q_t = []
        for head, (keys, vals) in enumerate(((key_low, val_low), (key_high, val_high))):
            weights = jnp.where(visible, jnp.exp(dot_nt(keys[...], q_rows)), 0.0)
            probs = weights * (1.0 / jnp.sum(weights, axis=0, keepdims=True))
            back = dot_nt(vals[...], g_rows)
            delta = jnp.sum(probs * back, axis=0, keepdims=True)
            score = (probs * (back - delta)).astype(BF)
            q_t.append(dot(key_t[head * HD : (head + 1) * HD, :], score))
            q_side = q_wide if head == 0 else pltpu.roll(q_wide, HD, 1)
            g_side = pltpu.roll(g_wide, HD, 1) if head == 0 else g_wide
            q_side = jnp.where(wide < HD, q_side, 0.0).astype(BF)
            g_side = jnp.where(wide < HD, 0.0, g_side).astype(BF)
            kv_grad[...] += dot(score, q_side) + dot(probs.astype(BF), g_side)
        q_grad[rows, :] = jnp.concatenate(q_t, axis=0).T * HD ** (-0.5)
        return carry

    lax.fori_loop(0, LEN // size, step, 0)
    q_gain, k_gain = query_gain[...], key_gain[...]
    q_terms = jnp.zeros((1, 2 * HD), F32)
    k_terms = jnp.zeros((1, 2 * HD), F32)
    column = jnp.zeros((1, tokens[0].shape[1]), F32)
    for j in range(ROWS):
        rows = pl.ds(j * BLK, BLK)
        cos_rows, sin_rows = cosine[rows, :], -sine[rows, :]
        block = pre[rows, :]
        q_pre, kv_pre = block[:, : 2 * HD], block[:, 2 * HD :]
        q_scale = lax.rsqrt(half_mean(q_pre * q_pre, lanes) + EPS)
        q_hat = q_pre * q_scale
        turned = turn(q_grad[rows, :], cos_rows, sin_rows, lanes)
        q_terms += jnp.sum(q_hat * turned, axis=0, keepdims=True)
        inner = turned * q_gain
        q_back = q_scale * (inner - q_hat * half_mean(inner * q_hat, lanes))
        low[rows, : 2 * HD] = q_back.astype(BF)
        k_scale = lax.rsqrt(half_mean(kv_pre * kv_pre, lanes) + EPS)
        k_hat = kv_pre * k_scale
        both = kv_grad[rows, :]
        turned = turn(both, cos_rows, sin_rows, lanes)
        k_terms += jnp.sum(k_hat * turned, axis=0, keepdims=True)
        inner = turned * k_gain
        k_back = k_scale * (inner - k_hat * half_mean(inner * k_hat, lanes))
        low[rows, 2 * HD :] = jnp.where(lanes < HD, k_back, both).astype(BF)
        share = dot_nt(low[rows, :], weight[...])
        part[j] = share.astype(BF)
        column += jnp.sum(tokens[j][...].astype(F32) * share, axis=0, keepdims=True)
    pre_sum[...] = column
    gain_sum[...] = jnp.concatenate([q_terms, k_terms], axis=0)


def middle_kernel(*refs):
    x_in, gain = refs[:2]
    heads = refs[2 : 2 + ROWS]
    weights = refs[2 + ROWS : 2 + 2 * ROWS]
    middle, normed = refs[2 + 2 * ROWS :]
    value = x_in[...].astype(F32)
    for k in range(ROWS):
        value += dot_nt(heads[k][...], weights[(ROWS - k) % ROWS][...])
    middle[...] = value
    scale = lax.rsqrt(jnp.mean(value * value, axis=-1, keepdims=True) + EPS)
    normed[...] = (value * scale * gain[...]).astype(BF)


def middle_back_kernel(*refs):
    middle_in, gain, upstream = refs[:3]
    parts = refs[3 : 3 + ROWS]
    weights = refs[3 + ROWS : 3 + 2 * ROWS]
    grad, grad_low, heads, gain_sum = refs[3 + 2 * ROWS :]
    value = middle_in[...]
    back = parts[0][...].astype(F32)
    for k in range(1, ROWS):
        back += parts[k][...].astype(F32)
    scale = lax.rsqrt(jnp.mean(value * value, axis=-1, keepdims=True) + EPS)
    hat = value * scale
    gain_sum[...] = jnp.sum(hat * back, axis=0, keepdims=True)
    inner = back * gain[...]
    result = upstream[...].astype(F32) + scale * (
        inner - hat * jnp.mean(inner * hat, axis=-1, keepdims=True)
    )
    grad[...] = result
    rounded = result.astype(BF)
    grad_low[...] = rounded
    for k in range(ROWS):
        heads[k] = dot(rounded, weights[k][...]).astype(BF)


def pick_rows(slot_rows, expert):
    slots = slot_rows[pl.ds(expert, 1), :]
    return (lax.broadcasted_iota(jnp.int32, (CAP, LEN), 0) == slots).astype(BF)


def pick_tokens(slot_cols, rows):
    slots = slot_cols[rows, :]
    ids = lax.broadcasted_iota(jnp.int32, (BLK, PAD), 1)
    return jnp.concatenate(
        [(ids == slots[:, e : e + 1]).astype(BF) for e in range(LOCAL)], axis=1
    )


def upstream_kernel(slot_rows, *refs):
    tokens = refs[:ROWS]
    down, slot_up, act_back, held = refs[ROWS:]
    expert = pl.program_id(0)

    @pl.when(expert == 0)
    def _():
        for j in range(ROWS):
            held[pl.ds(j * BLK, BLK), :] = tokens[j][...]

    picked = dot(pick_rows(slot_rows, expert), held[...]).astype(BF)
    slot_up[0] = picked
    act_back[0] = dot(picked, down[0, 0])


def expert_kernel(slot_rows, slot_cols, *refs):
    tokens = refs[:ROWS]
    (
        router,
        router_t,
        weights,
        act_back,
        buffer,
        act_gated,
        gate_grad,
        up_grad,
        part,
        logit_grad,
        held,
        probs,
        grads,
        gates,
    ) = refs[ROWS:]
    step = pl.program_id(0)

    @pl.when(step == 0)
    def _():
        for j in range(ROWS):
            held[pl.ds(j * BLK, BLK), :] = tokens[j][...]
        lanes = lax.broadcasted_iota(jnp.int32, (LEN, BLK), 1)
        logits = jnp.where(lanes < EXPERTS, dot(held[...], router[...]), -1e30)
        exps = jnp.exp(logits - jnp.max(logits, axis=-1, keepdims=True))
        probs[...] = exps / jnp.sum(exps, axis=-1, keepdims=True)
        grads[...] = jnp.zeros_like(grads)
        gates[...] = jnp.zeros_like(gates)

    @pl.when(step < LOCAL)
    def _():
        choose = pick_rows(slot_rows, step)
        picked = dot(choose, held[...]).astype(BF)
        buffer[0] = picked
        lanes = lax.broadcasted_iota(jnp.int32, (CAP, BLK), 1)
        slot_probs = dot(choose, probs[...].astype(BF))
        gate = jnp.sum(jnp.where(lanes == step, slot_probs, 0.0), axis=-1, keepdims=True)
        gate_pre = dot(picked, weights[0, 0])
        up_pre = dot(picked, weights[0, 1])
        sigma = 1.0 / (1.0 + jnp.exp(-gate_pre))
        silu = gate_pre * sigma
        act = (silu * up_pre).astype(BF).astype(F32)
        raw = act_back[0]
        gate_back = jnp.sum(act * raw, axis=-1, keepdims=True)
        act_gated[0] = (act * gate).astype(BF)
        act_grad = raw * gate
        d_gate = (act_grad * up_pre * sigma * (1.0 + gate_pre * (1.0 - sigma))).astype(BF)
        d_up = (act_grad * silu).astype(BF)
        gate_grad[0] = d_gate
        up_grad[0] = d_up
        rows = pl.ds(pl.multiple_of(step * PAD, PAD), CAP)
        grads[rows, :] = (dot_nt(d_gate, weights[0, 0]) + dot_nt(d_up, weights[0, 1])).astype(BF)
        gates[rows, :] = jnp.where(lanes == step, gate_back, 0.0).astype(BF)

    @pl.when(step == LOCAL)
    def _():
        def block(j, carry):
            rows = pl.ds(pl.multiple_of(j * BLK, BLK), BLK)
            choose = pick_tokens(slot_cols, rows)
            gate_back = dot(choose, gates[...])
            own = probs[rows, :]
            weighted = own * gate_back
            logit = weighted - own * jnp.sum(weighted, axis=-1, keepdims=True)
            high = logit.astype(BF).astype(F32)
            both = (high + pltpu.roll(logit - high, EXPERTS, 1)).astype(BF)
            logit_grad[rows, :] = both
            part[j] = (dot(choose, grads[...]) + dot(both, router_t[...])).astype(BF)
            return carry

        lax.fori_loop(0, ROWS, block, 0)


def expert_sums_kernel(slot_cols, *refs):
    tokens = refs[:ROWS]
    (
        logit_grad,
        weights,
        slot_up,
        buffer,
        act_gated,
        gate_grad,
        up_grad,
        sums,
        mix,
        router_sum,
        held,
    ) = refs[ROWS:]
    step = pl.program_id(0)

    @pl.when(step == 0)
    def _():
        held[...] = jnp.zeros_like(held)
        result = jnp.zeros((BLK, tokens[0].shape[1]), F32)
        for j in range(ROWS):
            turned = logit_grad[pl.ds(j * BLK, BLK), :].astype(F32).T.astype(BF)
            result += dot(turned, tokens[j][...])
        router_sum[...] = result

    @pl.when(step < LOCAL)
    def _():
        turned = buffer[0].T
        sums[0, 0] = dot(turned, gate_grad[0]).astype(BF)
        sums[0, 1] = dot(turned, up_grad[0]).astype(BF)
        sums[0, 2] = dot(slot_up[0].T, act_gated[0]).astype(BF)
        rows = pl.ds(pl.multiple_of(step * PAD, PAD), CAP)
        held[rows, :] = dot_nt(act_gated[0], weights[0, 0]).astype(BF)

    @pl.when(step == LOCAL)
    def _():
        def block(j, carry):
            rows = pl.ds(pl.multiple_of(j * BLK, BLK), BLK)
            mix[j] = dot(pick_tokens(slot_cols, rows), held[...]).astype(BF)
            return carry

        lax.fori_loop(0, ROWS, block, 0)


def shards(
    layer_input,
    prenorm,
    query_proj,
    key_proj,
    value_proj,
    querynorm,
    keynorm,
    out_proj,
    midnorm,
    router,
    gate_proj,
    up_proj,
    down_proj,
    routes,
    slot_ids,
    prefix,
    cotangent,
):
    width = layer_input.shape[-1]
    inner = gate_proj.shape[-1]
    row = lax.axis_index("row")
    col = lax.axis_index("col")
    col_rows = width // COLS

    experts = lax.all_gather(
        jnp.stack([gate_proj, up_proj, down_proj.transpose(0, 2, 1)], axis=1),
        "col",
        axis=2,
        tiled=True,
    )
    small = lax.all_gather(
        jnp.concatenate([query_proj, key_proj, value_proj, out_proj.T, router], axis=1),
        "col",
        axis=0,
        tiled=True,
    )
    qkv_weight = small[:, : 4 * HD]
    out_weight = small[:, 4 * HD : 6 * HD]
    router_all = small[:, 6 * HD :]
    router_rel = lax.dynamic_slice_in_dim(
        jnp.concatenate([router_all, router_all], axis=1), row * LOCAL, EXPERTS, 1
    )
    router_pad = jnp.pad(router_rel, ((0, 0), (0, BLK - EXPERTS)))
    router_t = jnp.pad(
        jnp.concatenate([router_rel.T, router_rel.T], axis=0), ((0, BLK - 2 * EXPERTS), (0, 0))
    )

    x_low = layer_input[0]
    x = x_low.astype(F32)
    scale_one = lax.rsqrt(jnp.mean(x * x, axis=-1, keepdims=True) + EPS)
    normed_one = (x * scale_one * prenorm).astype(BF)
    tokens_one = row_gather(normed_one)
    place = jnp.stack([row * BLK, prefix[0]]).astype(jnp.int32)
    frequency = 10000.0 ** (-2.0 * jnp.arange(HD // 2, dtype=F32) / HD)
    at = (jnp.arange(LEN, dtype=jnp.int32) + row * BLK) & (LEN - 1)
    angles = at.astype(F32)[:, None] * frequency[None, :]
    cos_half, sin_half = jnp.cos(angles), jnp.sin(angles)
    cosine = jnp.concatenate([cos_half] * 4, axis=1)
    sine = jnp.concatenate([-sin_half, sin_half] * 2, axis=1)
    query_gain = jnp.concatenate([querynorm, querynorm])[None, :]
    key_gain = jnp.concatenate([keynorm, keynorm])[None, :]
    side = pltpu.VMEM((LEN, 2 * HD), BF)
    pre, query, keyval, attended = call(
        attend_kernel,
        (
            shape((LEN, 4 * HD), F32),
            shape((LEN, 2 * HD), BF),
            shape((LEN, 2 * HD), BF),
            shape((LEN, 2 * HD), BF),
        ),
        [SM] + [VM] * (ROWS + 5),
        place,
        *tokens_one,
        qkv_weight,
        query_gain,
        key_gain,
        cosine,
        sine,
        scratch=[side] * 4,
        flops=4 << 30,
        moved=6 * MIB,
    )
    heads_out = row_send([attended[k * BLK : (k + 1) * BLK] for k in range(ROWS)])
    out_weights = row_gather(out_weight)
    middle, normed_two = call(
        middle_kernel,
        (shape((BLK, width), F32), shape((BLK, width), BF)),
        [VM] * (2 + 2 * ROWS),
        x_low,
        midnorm[None, :],
        *heads_out,
        *out_weights,
        flops=1 << 28,
        moved=3 * MIB,
    )

    turned_routes = lax.dynamic_slice_in_dim(
        jnp.concatenate([routes[0], routes[0]], axis=0), row * BLK, LEN, 0
    )
    turned_slots = lax.dynamic_slice_in_dim(
        jnp.concatenate([slot_ids[0], slot_ids[0]], axis=0), row * BLK, LEN, 0
    )
    mine = turned_routes[:, :, None] == row * LOCAL + jnp.arange(2 * LOCAL, dtype=jnp.int32)
    mine = mine & (jnp.arange(2 * LOCAL) < LOCAL)
    slot_cols = jnp.sum(jnp.where(mine, turned_slots[:, :, None] + 1, 0), axis=1) - 1
    slot_rows = slot_cols.T
    upstream = row_gather(cotangent[0])
    whole = lambda *dims: pl.BlockSpec(dims, lambda e: (0,) * len(dims))
    last = lambda e: jnp.minimum(e, LOCAL - 1)
    one = lambda *dims: pl.BlockSpec((1,) + dims, lambda e: (last(e),) + (0,) * len(dims))
    slot_up, act_back = call(
        upstream_kernel,
        (shape((LOCAL, CAP, width), BF), shape((LOCAL, CAP, inner), F32)),
        [whole(2 * LOCAL, LEN)]
        + [whole(BLK, width)] * ROWS
        + [pl.BlockSpec((1, 1, width, inner), lambda e: (e, 2, 0, 0))],
        slot_rows,
        *upstream,
        experts,
        grid=(LOCAL,),
        out_specs=(one(CAP, width), one(CAP, inner)),
        scratch=[pltpu.VMEM((LEN, width), BF)],
        flops=6 << 30,
        moved=16 * MIB,
    )
    tokens_two = row_gather(normed_two)
    buffer, act_gated, gate_low, up_low, part, logit_grad = call(
        expert_kernel,
        (
            shape((LOCAL, CAP, width), BF),
            shape((LOCAL, CAP, inner), BF),
            shape((LOCAL, CAP, inner), BF),
            shape((LOCAL, CAP, inner), BF),
            shape((ROWS, BLK, width), BF),
            shape((LEN, BLK), BF),
        ),
        [whole(2 * LOCAL, LEN), whole(LEN, 2 * LOCAL)]
        + [whole(BLK, width)] * ROWS
        + [
            whole(width, BLK),
            whole(BLK, width),
            pl.BlockSpec((1, 2, width, inner), lambda e: (last(e), 0, 0, 0)),
            one(CAP, inner),
        ],
        slot_rows,
        slot_cols,
        *tokens_two,
        router_pad,
        router_t,
        experts,
        act_back,
        grid=(LOCAL + 1,),
        out_specs=(
            one(CAP, width),
            one(CAP, inner),
            one(CAP, inner),
            one(CAP, inner),
            whole(ROWS, BLK, width),
            whole(LEN, BLK),
        ),
        scratch=[
            pltpu.VMEM((LEN, width), BF),
            pltpu.VMEM((LEN, BLK), F32),
            pltpu.VMEM((LOCAL * PAD, width), BF),
            pltpu.VMEM((LOCAL * PAD, BLK), BF),
        ],
        flops=16 << 30,
        moved=24 * MIB,
        limit=48,
    )
    parts_two = row_send([part[k] for k in range(ROWS)])
    sums, mix, router_sum = call(
        expert_sums_kernel,
        (
            shape((LOCAL, 3, width, inner), BF),
            shape((ROWS, BLK, width), BF),
            shape((BLK, width), F32),
        ),
        [whole(LEN, 2 * LOCAL)]
        + [whole(BLK, width)] * ROWS
        + [
            whole(LEN, BLK),
            pl.BlockSpec((1, 1, width, inner), lambda e: (last(e), 2, 0, 0)),
            one(CAP, width),
            one(CAP, width),
            one(CAP, inner),
            one(CAP, inner),
            one(CAP, inner),
        ],
        slot_cols,
        *tokens_two,
        logit_grad,
        experts,
        slot_up,
        buffer,
        act_gated,
        gate_low,
        up_low,
        grid=(LOCAL + 1,),
        out_specs=(one(3, width, inner), whole(ROWS, BLK, width), whole(BLK, width)),
        scratch=[pltpu.VMEM((LOCAL * PAD, width), BF)],
        flops=12 << 30,
        moved=32 * MIB,
        limit=48,
    )
    expert_grads = lax.psum_scatter(sums, "col", scatter_dimension=2, tiled=True).astype(F32)
    mixed = row_send([mix[k] for k in range(ROWS)])
    output = middle
    for piece in mixed:
        output = output + piece.astype(F32)
    layer_output = output.astype(BF)[None]

    middle_grad, middle_low, heads_grad, midnorm_part = call(
        middle_back_kernel,
        (
            shape((BLK, width), F32),
            shape((BLK, width), BF),
            shape((ROWS, BLK, 2 * HD), BF),
            shape((1, width), F32),
        ),
        [VM] * (3 + 2 * ROWS),
        middle,
        midnorm[None, :],
        cotangent[0],
        *parts_two,
        *out_weights,
        flops=1 << 28,
        moved=5 * MIB,
    )
    sent = row_send([heads_grad[k] for k in range(ROWS)])
    grads_in = [sent[(ROWS - k) % ROWS] for k in range(ROWS)]
    group_mid = row_gather(middle_low)
    low, part_one, prenorm_part, gain_part = call(
        attend_back_kernel,
        (
            shape((LEN, 4 * HD), BF),
            shape((ROWS, BLK, width), BF),
            shape((1, width), F32),
            shape((2, 2 * HD), F32),
        ),
        [SM] + [VM] * (2 * ROWS + 8),
        place,
        *grads_in,
        *tokens_one,
        qkv_weight,
        query_gain,
        key_gain,
        cosine,
        sine,
        pre,
        query,
        keyval,
        scratch=[side] * 4
        + [
            pltpu.VMEM((2 * HD, LEN), BF),
            side,
            pltpu.VMEM((LEN, 2 * HD), F32),
            pltpu.VMEM((LEN, 2 * HD), F32),
        ],
        flops=8 << 30,
        moved=8 * MIB,
    )
    parts_one = row_send([part_one[k] for k in range(ROWS)])
    normed_one_grad = parts_one[0].astype(F32)
    for piece in parts_one[1:]:
        normed_one_grad = normed_one_grad + piece.astype(F32)
    hat = x * scale_one
    weighted = normed_one_grad * prenorm
    input_grad = middle_grad + scale_one * (
        weighted - hat * jnp.mean(weighted * hat, axis=-1, keepdims=True)
    )

    qkv_sum = jnp.einsum(
        "td,tf->df", jnp.concatenate(tokens_one, axis=0), low, preferred_element_type=F32
    )
    out_sum = jnp.einsum(
        "td,tf->df", jnp.concatenate(group_mid, axis=0), attended, preferred_element_type=F32
    )
    attention_sums = jnp.concatenate([qkv_sum.astype(BF), out_sum.astype(BF)], axis=1)
    swapped = lax.all_to_all(attention_sums, "col", 0, 0, tiled=True)
    attention_grads = jnp.sum(
        swapped.reshape(COLS, col_rows, 6 * HD).astype(F32), axis=0
    )
    router_rows = router_sum[:EXPERTS] + router_sum[EXPERTS : 2 * EXPERTS]
    router_rows = lax.dynamic_slice_in_dim(
        jnp.concatenate([router_rows, router_rows], axis=0), EXPERTS - row * LOCAL, EXPERTS, 0
    )
    early = total(jnp.concatenate([router_rows, midnorm_part], axis=0))
    router_grad = lax.dynamic_slice_in_dim(
        early[:EXPERTS], col * col_rows, col_rows, 1
    ).T
    late = total(
        jnp.concatenate([(prenorm_part[0] / prenorm).reshape(-1, 2 * HD), gain_part], axis=0)
    )
    prenorm_grad = late[: width // (2 * HD)].reshape(width)
    query_terms, key_terms = late[-2], late[-1]
    return (
        layer_output,
        input_grad[None],
        prenorm_grad,
        attention_grads[:, : 2 * HD],
        attention_grads[:, 2 * HD : 3 * HD],
        attention_grads[:, 3 * HD : 4 * HD],
        query_terms[:HD] + query_terms[HD:],
        key_terms[:HD],
        attention_grads[:, 4 * HD :].T,
        early[EXPERTS],
        router_grad,
        expert_grads[:, 0],
        expert_grads[:, 1],
        expert_grads[:, 2].transpose(0, 2, 1),
    )


def solution(mesh):
    return jax.shard_map(
        shards,
        mesh=mesh,
        in_specs=(
            P("col", "row", None),
            P(),
            P("col", "row"),
            P("col", "row"),
            P("col", "row"),
            P(),
            P(),
            P("row", "col"),
            P(),
            P("col", None),
            P("row", "col", None),
            P("row", "col", None),
            P("row", None, "col"),
            P("col", None, None),
            P("col", None, None),
            P("col"),
            P("col", "row", None),
        ),
        out_specs=(
            P("col", "row", None),
            P("col", "row", None),
            P(),
            P("col", "row"),
            P("col", "row"),
            P("col", "row"),
            P(),
            P(),
            P("row", "col"),
            P(),
            P("col", None),
            P("row", "col", None),
            P("row", "col", None),
            P("row", None, "col"),
        ),
        check_vma=False,
    )
```

```python
import jax
import jax.numpy as jnp
import numpy as np
from jax import lax
from jax.experimental import pallas as pl
from jax.experimental.layout import Layout, with_layout_constraint
from jax.experimental.pallas import tpu as pltpu
from jax.sharding import PartitionSpec as P

HD = 64
CAP = 448
PAD = 512
ROWS = 8
COLS = 16
BLK = 128
LEN = ROWS * BLK
LOCAL = 4
EXPERTS = 32
EPS = 1e-06
BF = jnp.bfloat16
F32 = jnp.float32
SM = pl.BlockSpec(memory_space=pltpu.SMEM)
MIB = 1 << 20


def dot(a, b):
    return lax.dot_general(a, b, (((1,), (0,)), ((), ())), preferred_element_type=F32)


def dot_nt(a, b):
    return lax.dot_general(a, b, (((1,), (1,)), ((), ())), preferred_element_type=F32)


def shape(dims, kind):
    return jax.ShapeDtypeStruct(dims, kind)


def whole(value):
    dims = value.shape
    return pl.BlockSpec(dims, lambda i: (0,) * len(dims))


def call(body, outs, *args, grid=1, ins=None, out_specs=None, scratch=()):
    ins, out_specs = ins or {}, out_specs or {}
    return pl.pallas_call(
        body,
        grid=(grid,),
        out_shape=outs,
        in_specs=[ins.get(i, whole(value)) for i, value in enumerate(args)],
        out_specs=[out_specs.get(i, whole(value)) for i, value in enumerate(outs)],
        scratch_shapes=list(scratch),
        compiler_params=pltpu.CompilerParams(vmem_limit_bytes=56 * MIB),
        cost_estimate=pl.CostEstimate(flops=0, bytes_accessed=0, transcendentals=0),
    )(*args)


ROW = ("z", "y_lo")
COL = ("y_hi", "x", "core")


SWAP = [(0, 1), (1, 0)]


def together(*values):
    return lax.optimization_barrier(values)


def send(blocks, axes):
    return lax.all_to_all(blocks, axes, 0, 0)


def gather(own, axes, count):
    return send(jnp.broadcast_to(own[None], (count,) + own.shape), axes)


def shift(values, axis, step):
    return lax.ppermute(values, axis, [(i, (i - step) % 4) for i in range(4)])


def in_order(own, other, axis):
    first = lax.axis_index(axis) == 0
    return jnp.where(first, jnp.stack([own, other]), jnp.stack([other, own]))


def swap_halves(values, axis):
    first = lax.axis_index(axis) == 0
    kept = jnp.where(first, values[0], values[1])
    given = jnp.where(first, values[1], values[0])
    return kept.astype(F32) + lax.ppermute(given, axis, SWAP).astype(F32)


def ring_sum(blocks, axis):
    result = blocks[0].astype(F32)
    for k in range(1, 4):
        result = result + shift(blocks[k], axis, -k).astype(F32)
    return result


def from_here(values, axis, dim):
    here = lax.axis_index(axis)
    return [lax.dynamic_index_in_dim(values, (here + k) % 4, dim, False) for k in range(4)]


def beside(values, whole_sums):
    lines = values.reshape(-1, values.shape[-1])
    high = whole_sums.astype(BF)
    return jnp.concatenate([lines, high, (whole_sums - high.astype(F32)).astype(BF)], axis=0)


def apart(message, dims):
    count = 1
    for size in dims[:-1]:
        count *= size
    rest = message[count:]
    half = rest.shape[0] // 2
    return message[:count].reshape(dims), rest[:half] + rest[half:]


def swap_both(values, sums, axis):
    first = lax.axis_index(axis) == 0
    kept = jnp.where(first, values[0], values[1])
    given = jnp.where(first, values[1], values[0])
    got = lax.ppermute(beside(given, sums), axis, SWAP).astype(F32)
    got, more = apart(got, kept.shape)
    return kept.astype(F32) + got, sums + more


def ring_both(blocks, sums, axis):
    result, dims = blocks[0].astype(F32), blocks[0].shape
    added = sums
    for k in range(1, 4):
        got, more = apart(shift(beside(blocks[k], sums), axis, -k).astype(F32), dims)
        result, added = result + got, added + more
    return result, added


def swapped(own, axis):
    return in_order(own, lax.ppermute(own, axis, SWAP), axis)


def lane_ids(rows):
    return lax.broadcasted_iota(jnp.int32, (rows, 2 * HD), 1)


def half_mean(values, lanes):
    low = jnp.sum(jnp.where(lanes < HD, values, 0.0), axis=-1, keepdims=True)
    high = jnp.sum(jnp.where(lanes < HD, 0.0, values), axis=-1, keepdims=True)
    return jnp.where(lanes < HD, low, high) * (1.0 / HD)


def turn(values, cosine, sine, lanes):
    swapped = jnp.where(
        (lanes & (HD - 1)) < HD // 2,
        pltpu.roll(values, 2 * HD - HD // 2, 1),
        pltpu.roll(values, HD // 2, 1),
    )
    return values * cosine + swapped * sine


def turn_tables():
    frequency = np.float32(10000.0) ** (np.arange(HD // 2, dtype=np.float32) * np.float32(-2 / HD))
    angles = np.arange(LEN, dtype=np.float32)[:, None] * frequency[None, :].astype(np.float32)
    cosine, sine = np.cos(angles), np.sin(angles)
    return (
        np.concatenate([cosine] * 4, axis=1).astype(np.float32),
        np.concatenate([-sine, sine] * 2, axis=1).astype(np.float32),
    )


def attend_kernel(*refs):
    place, tokens, here, there, query_gain, key_gain, cosine, sine = refs[:8]
    pre, query, keyval, out, part, weight, out_weight, router = refs[8:16]
    key_low, key_high, val_low, val_high = refs[16:]
    size = here.shape[2]
    for core, ring in enumerate((here, there)):
        for k in range(4):
            for y in range(2):
                block = y * 8 + ((place[1] + k) & 3) * 2 + (place[2] ^ core)
                rows = pl.ds(pl.multiple_of(block * size, size), size)
                weight[rows, :] = ring[k, y, :, : 4 * HD]
                out_weight[rows, :] = ring[k, y, :, 4 * HD : 6 * HD]
                router[rows, :] = ring[k, y, :, 6 * HD :]
    lanes = lane_ids(BLK)
    for j in range(ROWS):
        rows = pl.ds(j * BLK, BLK)
        block = dot(tokens[j], weight[...])
        pre[rows, :] = block
        cos_rows, sin_rows = cosine[rows, :], sine[rows, :]
        q_pre, kv_pre = block[:, : 2 * HD], block[:, 2 * HD :]
        q_scale = lax.rsqrt(half_mean(q_pre * q_pre, lanes) + EPS)
        turned = turn(q_pre * q_scale * query_gain[...], cos_rows, sin_rows, lanes)
        query[rows, :] = turned.astype(BF) * HD ** (-0.5)
        k_scale = lax.rsqrt(half_mean(kv_pre * kv_pre, lanes) + EPS)
        turned = turn(kv_pre * k_scale * key_gain[...], cos_rows, sin_rows, lanes)
        key = jnp.where(lanes < HD, turned, 0.0)
        val = jnp.where(lanes < HD, 0.0, kv_pre)
        keyval[rows, :] = (key + val).astype(BF)
        key_low[rows, :] = key.astype(BF)
        key_high[rows, :] = pltpu.roll(key, HD, 1).astype(BF)
        val_low[rows, :] = pltpu.roll(val, HD, 1).astype(BF)
        val_high[rows, :] = val.astype(BF)
    prefix = place[0]
    size = 2 * BLK
    key_at = lax.broadcasted_iota(jnp.int32, (size, LEN), 1)

    def step(index, carry):
        rows = pl.ds(pl.multiple_of(index * size, size), size)
        q_rows = query[rows, :]
        at = lax.broadcasted_iota(jnp.int32, (size, 1), 0) + index * size
        visible = key_at < jnp.maximum(at + 1, prefix)
        mixed = jnp.zeros((size, 2 * HD), F32)
        for keys, vals in ((key_low, val_low), (key_high, val_high)):
            weights = jnp.where(visible, jnp.exp(dot_nt(q_rows, keys[...])), 0.0)
            inverse = 1.0 / jnp.sum(weights, axis=-1, keepdims=True)
            mixed += dot((weights * inverse).astype(BF), vals[...])
        mixed = mixed.astype(BF)
        out[rows, :] = mixed
        share = dot_nt(mixed, out_weight[...]).astype(BF)
        part[pl.ds(index * 2, 2)] = share.reshape(2, BLK, -1)
        return carry

    lax.fori_loop(0, LEN // size, step, 0)


def attend_back_kernel(*refs):
    place, middle, out_weight, tokens, weight, query_gain, key_gain, cosine, sine = refs[:9]
    pre, query, keyval = refs[9:12]
    low, part, pre_sum, gain_sum = refs[12:16]
    key_low, key_high, val_low, val_high, key_t, grads, q_grad, kv_grad = refs[16:]
    lanes = lane_ids(BLK)
    for j in range(ROWS):
        rows = pl.ds(j * BLK, BLK)
        both = keyval[rows, :].astype(F32)
        key = jnp.where(lanes < HD, both, 0.0)
        val = jnp.where(lanes < HD, 0.0, both)
        key_two = pltpu.roll(key, HD, 1)
        key_low[rows, :] = key.astype(BF)
        key_high[rows, :] = key_two.astype(BF)
        val_low[rows, :] = pltpu.roll(val, HD, 1).astype(BF)
        val_high[rows, :] = val.astype(BF)
        key_t[:, j * BLK : (j + 1) * BLK] = (key + key_two).T.astype(BF)
        grads[rows, :] = dot(middle[j], out_weight[...]).astype(BF)
    kv_grad[...] = jnp.zeros_like(kv_grad)
    prefix = place[0]
    size = 2 * BLK
    key_at = lax.broadcasted_iota(jnp.int32, (LEN, size), 0)
    wide = lane_ids(size)

    def step(index, carry):
        rows = pl.ds(pl.multiple_of(index * size, size), size)
        q_rows, g_rows = query[rows, :], grads[rows, :]
        q_wide, g_wide = q_rows.astype(F32), g_rows.astype(F32)
        row_at = lax.broadcasted_iota(jnp.int32, (1, size), 1) + index * size
        visible = key_at < jnp.maximum(row_at + 1, prefix)
        q_t = []
        for head, (keys, vals) in enumerate(((key_low, val_low), (key_high, val_high))):
            weights = jnp.where(visible, jnp.exp(dot_nt(keys[...], q_rows)), 0.0)
            probs = weights * (1.0 / jnp.sum(weights, axis=0, keepdims=True))
            back = dot_nt(vals[...], g_rows)
            delta = jnp.sum(probs * back, axis=0, keepdims=True)
            score = (probs * (back - delta)).astype(BF)
            q_t.append(dot(key_t[head * HD : (head + 1) * HD, :], score))
            q_side = q_wide if head == 0 else pltpu.roll(q_wide, HD, 1)
            g_side = pltpu.roll(g_wide, HD, 1) if head == 0 else g_wide
            q_side = jnp.where(wide < HD, q_side, 0.0).astype(BF)
            g_side = jnp.where(wide < HD, 0.0, g_side).astype(BF)
            kv_grad[...] += dot(score, q_side) + dot(probs.astype(BF), g_side)
        q_grad[rows, :] = jnp.concatenate(q_t, axis=0).T * HD ** (-0.5)
        return carry

    lax.fori_loop(0, LEN // size, step, 0)
    q_gain, k_gain = query_gain[...], key_gain[...]
    q_terms = jnp.zeros((1, 2 * HD), F32)
    k_terms = jnp.zeros((1, 2 * HD), F32)
    column = jnp.zeros((1, tokens.shape[2]), F32)
    for j in range(ROWS):
        rows = pl.ds(j * BLK, BLK)
        cos_rows, sin_rows = cosine[rows, :], -sine[rows, :]
        block = pre[rows, :]
        q_pre, kv_pre = block[:, : 2 * HD], block[:, 2 * HD :]
        q_scale = lax.rsqrt(half_mean(q_pre * q_pre, lanes) + EPS)
        q_hat = q_pre * q_scale
        turned = turn(q_grad[rows, :], cos_rows, sin_rows, lanes)
        q_terms += jnp.sum(q_hat * turned, axis=0, keepdims=True)
        inner = turned * q_gain
        q_back = q_scale * (inner - q_hat * half_mean(inner * q_hat, lanes))
        low[rows, : 2 * HD] = q_back.astype(BF)
        k_scale = lax.rsqrt(half_mean(kv_pre * kv_pre, lanes) + EPS)
        k_hat = kv_pre * k_scale
        both = kv_grad[rows, :]
        turned = turn(both, cos_rows, sin_rows, lanes)
        k_terms += jnp.sum(k_hat * turned, axis=0, keepdims=True)
        inner = turned * k_gain
        k_back = k_scale * (inner - k_hat * half_mean(inner * k_hat, lanes))
        low[rows, 2 * HD :] = jnp.where(lanes < HD, k_back, both).astype(BF)
        share = dot_nt(low[rows, :], weight[...])
        part[j // 2, j % 2] = share.astype(BF)
        column += jnp.sum(tokens[j].astype(F32) * share, axis=0, keepdims=True)
    pre_sum[...] = column
    gain_sum[...] = jnp.concatenate([q_terms, k_terms], axis=0)


def norm_kernel(x_in, gain, copies):
    value = x_in[...].astype(F32)
    scale = lax.rsqrt(jnp.mean(value * value, axis=-1, keepdims=True) + EPS)
    normed = (value * scale * gain[...]).astype(BF)
    for k in range(ROWS):
        copies[k] = normed


def middle_kernel(x_in, gain, parts, middle, copies):
    value = x_in[...].astype(F32)
    for k in range(ROWS):
        value += parts[k].astype(F32)
    middle[...] = value
    scale = lax.rsqrt(jnp.mean(value * value, axis=-1, keepdims=True) + EPS)
    normed = (value * scale * gain[...]).astype(BF)
    for k in range(ROWS):
        copies[k] = normed


def middle_back_kernel(middle_in, gain, upstream, parts, grad, copies, gain_sum):
    value = middle_in[...]
    back = parts[0].astype(F32)
    for k in range(1, ROWS):
        back += parts[k].astype(F32)
    scale = lax.rsqrt(jnp.mean(value * value, axis=-1, keepdims=True) + EPS)
    hat = value * scale
    gain_sum[...] = jnp.sum(hat * back, axis=0, keepdims=True)
    inner = back * gain[...]
    result = upstream[...].astype(F32) + scale * (
        inner - hat * jnp.mean(inner * hat, axis=-1, keepdims=True)
    )
    grad[...] = result
    rounded = result.astype(BF)
    for k in range(ROWS):
        copies[k] = rounded


def put_blocks(sums, which, value):
    size = value.shape[0] // COLS
    for block in range(COLS):
        sums[block % 2, which, block // 8, block // 2 % 4] = value[block * size : (block + 1) * size]


def attention_sums_kernel(tokens, low, middle, heads, router_sums, sums):
    tall = tokens[...].reshape(LEN, -1)
    for k in range(2):
        turned = low[:, 2 * HD * k : 2 * HD * (k + 1)].astype(F32).T.astype(BF)
        put_blocks(sums, k, dot(turned, tall).T.astype(BF))
    turned = heads[...].astype(F32).T.astype(BF)
    put_blocks(sums, 2, dot(turned, middle[...].reshape(LEN, -1)).T.astype(BF))
    put_blocks(sums, 3, router_sums[...])


def pick_rows(slot_rows, expert):
    slots = slot_rows[pl.ds(expert, 1), :]
    return (lax.broadcasted_iota(jnp.int32, (CAP, LEN), 0) == slots).astype(BF)


def pick_tokens(slot_cols, rows):
    slots = slot_cols[rows, :]
    ids = lax.broadcasted_iota(jnp.int32, (BLK, PAD), 1)
    return jnp.concatenate(
        [(ids == slots[:, e : e + 1]).astype(BF) for e in range(LOCAL)], axis=1
    )


def upstream_kernel(slot_rows, t_0, t_1, t_2, t_3, slot_up):
    choose = pick_rows(slot_rows, pl.program_id(0))
    size = 2 * BLK
    picked = jnp.zeros((CAP, t_0.shape[-1]), F32)
    for k, tokens in enumerate((t_0, t_1, t_2, t_3)):
        picked += dot(choose[:, k * size : (k + 1) * size], tokens[...].reshape(size, -1))
    slot_up[0] = picked.astype(BF)


def expert_kernel(
    slot_rows,
    slot_cols,
    tokens,
    router,
    router_t,
    weights,
    slot_up,
    buffer,
    act_gated,
    gate_grad,
    up_grad,
    part,
    logit_grad,
    probs,
    grads,
    gates,
):
    step = pl.program_id(0)

    @pl.when(step == 0)
    def _():
        lanes = lax.broadcasted_iota(jnp.int32, (LEN, BLK), 1)
        logits = jnp.where(lanes < EXPERTS, dot(tokens[...], router[...]), -1e30)
        exps = jnp.exp(logits - jnp.max(logits, axis=-1, keepdims=True))
        probs[...] = exps / jnp.sum(exps, axis=-1, keepdims=True)
        grads[...] = jnp.zeros_like(grads)
        gates[...] = jnp.zeros_like(gates)

    @pl.when(step < LOCAL)
    def _():
        choose = pick_rows(slot_rows, step)
        picked = dot(choose, tokens[...]).astype(BF)
        buffer[0] = picked
        lanes = lax.broadcasted_iota(jnp.int32, (CAP, BLK), 1)
        slot_probs = dot(choose, probs[...].astype(BF))
        gate = jnp.sum(jnp.where(lanes == step, slot_probs, 0.0), axis=-1, keepdims=True)
        gate_pre = dot(picked, weights[0, 0])
        up_pre = dot(picked, weights[0, 1])
        sigma = 1.0 / (1.0 + jnp.exp(-gate_pre))
        silu = gate_pre * sigma
        act = (silu * up_pre).astype(BF).astype(F32)
        raw = dot(slot_up[0], weights[0, 2])
        gate_back = jnp.sum(act * raw, axis=-1, keepdims=True)
        act_gated[0] = (act * gate).astype(BF)
        act_grad = raw * gate
        d_gate = (act_grad * up_pre * sigma * (1.0 + gate_pre * (1.0 - sigma))).astype(BF)
        d_up = (act_grad * silu).astype(BF)
        gate_grad[0] = d_gate
        up_grad[0] = d_up
        rows = pl.ds(pl.multiple_of(step * PAD, PAD), CAP)
        grads[rows, :] = (dot_nt(d_gate, weights[0, 0]) + dot_nt(d_up, weights[0, 1])).astype(BF)
        gates[rows, :] = jnp.where(lanes == step, gate_back, 0.0).astype(BF)

    @pl.when(step == LOCAL)
    def _():
        def block(j, carry):
            rows = pl.ds(pl.multiple_of(j * BLK, BLK), BLK)
            choose = pick_tokens(slot_cols, rows)
            gate_back = dot(choose, gates[...])
            own = probs[rows, :]
            weighted = own * gate_back
            logit = weighted - own * jnp.sum(weighted, axis=-1, keepdims=True)
            high = logit.astype(BF).astype(F32)
            both = (high + pltpu.roll(logit - high, EXPERTS, 1)).astype(BF)
            logit_grad[rows, :] = both
            part[j] = (dot(choose, grads[...]) + dot(both, router_t[...])).astype(BF)
            return carry

        lax.fori_loop(0, ROWS, block, 0)


def expert_sums_kernel(slot_up, buffer, act_gated, gate_grad, up_grad, sums):
    def put(which, value):
        for y in range(2):
            for place in range(COLS // 2):
                at = (y * (COLS // 2) + place) * value.shape[0] // COLS
                sums[place, y, 0, which] = value[at : at + value.shape[0] // COLS].astype(BF)

    turned = buffer[0].T
    put(0, dot(turned, gate_grad[0]))
    put(1, dot(turned, up_grad[0]))
    put(2, dot(slot_up[0].T, act_gated[0]))


def mix_kernel(
    at, slot_cols, tokens, logit_grad, weights, act_gated, m_0, m_1, m_2, m_3, router_sum, held
):
    step = pl.program_id(0)

    @pl.when(step == 0)
    def _():
        held[...] = jnp.zeros_like(held)
        router_sum[...] = dot(logit_grad[...].astype(F32).T.astype(BF), tokens[...])

    @pl.when(step < LOCAL)
    def _():
        rows = pl.ds(pl.multiple_of(step * PAD, PAD), CAP)
        held[rows, :] = dot_nt(act_gated[0], weights[0, 0]).astype(BF)

    @pl.when(step == LOCAL)
    def _():
        for k, mix in enumerate((m_0, m_1, m_2, m_3)):
            for y in range(2):
                place = (2 * at[0] + 2 * k + y) & (ROWS - 1)
                rows = pl.ds(pl.multiple_of(place * BLK, BLK), BLK)
                mix[y] = dot(pick_tokens(slot_cols, rows), held[...]).astype(BF)


def shards(
    layer_input,
    prenorm,
    query_proj,
    key_proj,
    value_proj,
    querynorm,
    keynorm,
    out_proj,
    midnorm,
    router,
    gate_proj,
    up_proj,
    down_proj,
    routes,
    slot_ids,
    prefix,
    cotangent,
):
    width = layer_input.shape[-1]
    inner = gate_proj.shape[-1]
    row = lax.axis_index(ROW)
    z = lax.axis_index("z")
    at = z.reshape(1)
    col_rows = width // COLS

    x_low = layer_input[0]
    x = x_low.astype(F32)
    scale_one = lax.rsqrt(jnp.mean(x * x, axis=-1, keepdims=True) + EPS)
    copied = shape((ROWS, BLK, width), BF)
    (copies,) = call(norm_kernel, (copied,), x_low, prenorm[None, :])
    router_own = jnp.pad(router, ((0, 0), (0, BLK - EXPERTS)))
    small = swapped(
        jnp.concatenate([query_proj, key_proj, value_proj, out_proj.T, router_own], axis=1), "y_hi"
    )
    upstream = swapped(cotangent[0], "y_lo")
    copies, upstream, small = together(copies, upstream, small)
    upstream = [upstream] + [shift(upstream, "z", k) for k in range(1, 4)]
    tokens_one = send(copies, ROW)
    experts = lax.all_gather(
        jnp.stack([gate_proj, up_proj, down_proj.transpose(0, 2, 1)], axis=1),
        COL,
        axis=2,
        tiled=True,
    )
    small = jnp.stack([small] + [shift(small, "x", k) for k in range(1, 4)])
    small_there = lax.ppermute(small, "core", SWAP)

    cosine, sine = turn_tables()
    query_gain = jnp.concatenate([querynorm, querynorm])[None, :]
    key_gain = jnp.concatenate([keynorm, keynorm])[None, :]
    side = pltpu.VMEM((LEN, 2 * HD), BF)
    place = jnp.stack([prefix[0], lax.axis_index("x"), lax.axis_index("core")]).astype(jnp.int32)
    pre, query, keyval, attended, part_out, qkv_weight, out_weight, router_all = call(
        attend_kernel,
        (
            shape((LEN, 4 * HD), F32),
            shape((LEN, 2 * HD), BF),
            shape((LEN, 2 * HD), BF),
            shape((LEN, 2 * HD), BF),
            copied,
            shape((width, 4 * HD), BF),
            shape((width, 2 * HD), BF),
            shape((width, BLK), BF),
        ),
        place,
        tokens_one,
        small,
        small_there,
        query_gain,
        key_gain,
        cosine,
        sine,
        ins={0: SM},
        scratch=[side] * 4,
    )
    router_rel = lax.dynamic_slice_in_dim(
        jnp.concatenate([router_all[:, :EXPERTS]] * 2, axis=1), row * LOCAL, EXPERTS, 1
    )
    router_pad = jnp.pad(router_rel, ((0, 0), (0, BLK - EXPERTS)))
    router_t = jnp.pad(
        jnp.concatenate([router_rel.T, router_rel.T], axis=0), ((0, BLK - 2 * EXPERTS), (0, 0))
    )
    part_out, *upstream = together(part_out, *upstream)
    parts_out = send(part_out, ROW)
    middle, copies_two = call(
        middle_kernel,
        (shape((BLK, width), F32), copied),
        x_low,
        midnorm[None, :],
        parts_out,
    )

    ids = row * LOCAL + jnp.arange(2 * LOCAL, dtype=jnp.int32)
    mine = (routes[0][:, :, None] == ids) & (jnp.arange(2 * LOCAL) < LOCAL)
    slot_cols = jnp.sum(jnp.where(mine, slot_ids[0][:, :, None] + 1, 0), axis=1) - 1
    slot_rows = slot_cols.T
    turned_rows = lax.dynamic_slice_in_dim(
        jnp.concatenate([slot_rows, slot_rows], axis=1), z * 2 * BLK, LEN, 1
    )
    last = lambda e: jnp.minimum(e, LOCAL - 1)
    one = lambda *dims: pl.BlockSpec((1,) + dims, lambda e: (last(e),) + (0,) * len(dims))
    down_block = pl.BlockSpec((1, 1, width, inner), lambda e: (last(e), 2, 0, 0))
    tokens_two = send(copies_two, ROW).reshape(LEN, width)
    (slot_up,) = call(
        upstream_kernel,
        (shape((LOCAL, CAP, width), BF),),
        turned_rows,
        *upstream,
        grid=LOCAL,
        out_specs={0: one(CAP, width)},
    )
    buffer, act_gated, gate_low, up_low, part, logit_grad = call(
        expert_kernel,
        (
            shape((LOCAL, CAP, width), BF),
            shape((LOCAL, CAP, inner), BF),
            shape((LOCAL, CAP, inner), BF),
            shape((LOCAL, CAP, inner), BF),
            shape((ROWS, BLK, width), BF),
            shape((LEN, BLK), BF),
        ),
        slot_rows,
        slot_cols,
        tokens_two,
        router_pad,
        router_t,
        experts,
        slot_up,
        ins={5: one(3, width, inner), 6: one(CAP, width)},
        grid=LOCAL + 1,
        out_specs={0: one(CAP, width)} | {i: one(CAP, inner) for i in (1, 2, 3)},
        scratch=[
            pltpu.VMEM((LEN, BLK), F32),
            pltpu.VMEM((LOCAL * PAD, width), BF),
            pltpu.VMEM((LOCAL * PAD, BLK), BF),
        ],
    )
    parts_two = send(part, ROW)
    (sums,) = call(
        expert_sums_kernel,
        (shape((COLS // 2, 2, LOCAL, 3, col_rows, inner), BF),),
        slot_up,
        buffer,
        act_gated,
        gate_low,
        up_low,
        ins={0: one(CAP, width), 1: one(CAP, width)} | {i: one(CAP, inner) for i in (2, 3, 4)},
        grid=LOCAL,
        out_specs={
            0: pl.BlockSpec(
                (COLS // 2, 2, 1, 3, col_rows, inner), lambda e: (0, 0, e, 0, 0, 0)
            )
        },
    )
    *mix, router_sum = call(
        mix_kernel,
        (*[shape((2, BLK, width), BF)] * 4, shape((BLK, width), F32)),
        at,
        slot_cols,
        tokens_two,
        logit_grad,
        experts,
        act_gated,
        ins={0: SM, 4: down_block, 5: one(CAP, inner)},
        grid=LOCAL + 1,
        scratch=[pltpu.VMEM((LOCAL * PAD, width), BF)],
    )
    halves = lax.psum_scatter(sums, ("x", "core"), scatter_dimension=0, tiled=False)
    router_rows = router_sum[:EXPERTS] + router_sum[EXPERTS : 2 * EXPERTS]
    router_rows = lax.dynamic_slice_in_dim(
        jnp.concatenate([router_rows, router_rows], axis=0), EXPERTS - row * LOCAL, EXPERTS, 0
    )
    router_sums = jnp.pad(router_rows, ((0, BLK - EXPERTS), (0, 0))).T.astype(BF)

    middle_grad, copies_mid, midnorm_part = call(
        middle_back_kernel,
        (shape((BLK, width), F32), copied, shape((1, width), F32)),
        middle,
        midnorm[None, :],
        cotangent[0],
        parts_two,
    )
    group_mid = send(copies_mid, ROW)
    group_mid, halves, *mix = together(group_mid, halves, *mix)
    mixed = ring_sum(mix, "z").astype(BF)
    expert_grads = swap_halves(halves, "y_hi")
    low, part_one, prenorm_part, gain_part = call(
        attend_back_kernel,
        (
            shape((LEN, 4 * HD), BF),
            shape((4, 2, BLK, width), BF),
            shape((1, width), F32),
            shape((2, 2 * HD), F32),
        ),
        prefix,
        group_mid,
        out_weight,
        tokens_one,
        qkv_weight,
        query_gain,
        key_gain,
        cosine,
        sine,
        pre,
        query,
        keyval,
        ins={0: SM},
        scratch=[side] * 4
        + [
            pltpu.VMEM((2 * HD, LEN), BF),
            side,
            pltpu.VMEM((LEN, 2 * HD), F32),
            pltpu.VMEM((LEN, 2 * HD), F32),
        ],
    )
    part_one, low, mixed, expert_grads = together(part_one, low, mixed, expert_grads)
    parts_one = lax.all_to_all(part_one, "z", 0, 0)
    parts_one = jnp.sum(parts_one.astype(F32), axis=0).astype(BF)
    normed_one_grad = swap_halves(parts_one, "y_lo")

    (sums_one,) = call(
        attention_sums_kernel,
        (shape((2, 4, 2, 4, col_rows, 2 * HD), BF),),
        tokens_one,
        low,
        group_mid,
        attended,
        router_sums,
    )
    lines = width // (2 * HD)
    late = jnp.concatenate(
        [
            (prenorm_part / prenorm).reshape(-1, 2 * HD),
            midnorm_part.reshape(-1, 2 * HD),
            gain_part,
            jnp.zeros((6, 2 * HD), F32),
        ],
        axis=0,
    )
    sums_one, late = swap_both(sums_one, late, "core")
    sums_one, late = ring_both(from_here(sums_one.astype(BF), "x", 2), late, "x")
    layer_output = (middle + swap_halves(mixed, "y_lo")).astype(BF)[None]
    sums_one, late = swap_both(jnp.moveaxis(sums_one.astype(BF), 1, 0), late, "y_hi")
    router_part = sums_one[3].astype(BF)
    router_part, late = swap_both(jnp.stack([router_part] * 2), late, "y_lo")
    router_part, late = ring_both([router_part.astype(BF)] * 4, late, "z")
    hat = x * scale_one
    weighted = normed_one_grad * prenorm
    input_grad = middle_grad + scale_one * (
        weighted - hat * jnp.mean(weighted * hat, axis=-1, keepdims=True)
    )
    query_terms, key_terms = late[2 * lines], late[2 * lines + 1]
    return (
        layer_output,
        input_grad[None],
        late[:lines].reshape(width),
        sums_one[0],
        sums_one[1][:, :HD],
        sums_one[1][:, HD:],
        query_terms[:HD] + query_terms[HD:],
        key_terms[:HD],
        sums_one[2].T,
        late[lines : 2 * lines].reshape(width),
        router_part[:, :EXPERTS],
        expert_grads[:, 0],
        expert_grads[:, 1],
        expert_grads[:, 2].transpose(0, 2, 1),
    )


def solution(mesh):
    axes = ("z", "y_lo", "y_hi", "x", "core")
    return jax.shard_map(
        shards,
        mesh=jax.sharding.Mesh(mesh.devices.reshape(4, 2, 2, 4, 2), axes),
        in_specs=(
            P(COL, ROW, None),
            P(),
            P(COL, ROW),
            P(COL, ROW),
            P(COL, ROW),
            P(),
            P(),
            P(ROW, COL),
            P(),
            P(COL, None),
            P(ROW, COL, None),
            P(ROW, COL, None),
            P(ROW, None, COL),
            P(COL, None, None),
            P(COL, None, None),
            P(COL),
            P(COL, ROW, None),
        ),
        out_specs=(
            P(COL, ROW, None),
            P(COL, ROW, None),
            P(),
            P(COL, ROW),
            P(COL, ROW),
            P(COL, ROW),
            P(),
            P(),
            P(ROW, COL),
            P(),
            P(COL, None),
            P(ROW, COL, None),
            P(ROW, COL, None),
            P(ROW, None, COL),
        ),
        check_vma=False,
    )
```

```python
import jax
import jax.numpy as jnp
import numpy as np
from jax import lax
from jax.experimental import pallas as pl
from jax.experimental.layout import Layout, with_layout_constraint
from jax.experimental.pallas import tpu as pltpu
from jax.sharding import PartitionSpec as P

HD = 64
CAP = 448
ROWS = 8
COLS = 16
BLK = 128
LEN = ROWS * BLK
LOCAL = 4
EXPERTS = 32
EPS = 1e-06
BF = jnp.bfloat16
F32 = jnp.float32
SM = pl.BlockSpec(memory_space=pltpu.SMEM)
MIB = 1 << 20


def dot(a, b):
    return lax.dot_general(a, b, (((1,), (0,)), ((), ())), preferred_element_type=F32)


def dot_nt(a, b):
    return lax.dot_general(a, b, (((1,), (1,)), ((), ())), preferred_element_type=F32)


def dot_tn(a, b):
    return lax.dot_general(a, b, (((0,), (0,)), ((), ())), preferred_element_type=F32)


def shape(dims, kind):
    return jax.ShapeDtypeStruct(dims, kind)


def whole(value):
    dims = value.shape
    return pl.BlockSpec(dims, lambda i: (0,) * len(dims))


def call(body, outs, *args, grid=1, ins=None, out_specs=None, scratch=()):
    ins, out_specs = ins or {}, out_specs or {}
    return pl.pallas_call(
        body,
        grid=(grid,),
        out_shape=outs,
        in_specs=[ins.get(i, whole(value)) for i, value in enumerate(args)],
        out_specs=[out_specs.get(i, whole(value)) for i, value in enumerate(outs)],
        scratch_shapes=list(scratch),
        compiler_params=pltpu.CompilerParams(vmem_limit_bytes=56 * MIB),
        cost_estimate=pl.CostEstimate(flops=0, bytes_accessed=0, transcendentals=0),
    )(*args)


ROW = ("z", "y_lo")
COL = ("y_hi", "x", "core")


SWAP = [(0, 1), (1, 0)]


def together(*values):
    return lax.optimization_barrier(values)


def send(blocks, axes):
    return lax.all_to_all(blocks, axes, 0, 0)


def gather(own, axes, count):
    return send(jnp.broadcast_to(own[None], (count,) + own.shape), axes)


def shift(values, axis, step):
    return lax.ppermute(values, axis, [(i, (i - step) % 4) for i in range(4)])


def in_order(own, other, axis):
    first = lax.axis_index(axis) == 0
    return jnp.where(first, jnp.stack([own, other]), jnp.stack([other, own]))


def swap_halves(values, axis):
    first = lax.axis_index(axis) == 0
    kept = jnp.where(first, values[0], values[1])
    given = jnp.where(first, values[1], values[0])
    return kept.astype(F32) + lax.ppermute(given, axis, SWAP).astype(F32)


def ring_sum(blocks, axis):
    result = blocks[0].astype(F32)
    for k in range(1, 4):
        result = result + shift(blocks[k], axis, -k).astype(F32)
    return result


def from_here(values, axis, dim):
    here = lax.axis_index(axis)
    return [lax.dynamic_index_in_dim(values, (here + k) % 4, dim, False) for k in range(4)]


def beside(values, whole_sums):
    lines = values.reshape(-1, values.shape[-1])
    high = whole_sums.astype(BF)
    return jnp.concatenate([lines, high, (whole_sums - high.astype(F32)).astype(BF)], axis=0)


def apart(message, dims):
    count = 1
    for size in dims[:-1]:
        count *= size
    rest = message[count:]
    half = rest.shape[0] // 2
    return message[:count].reshape(dims), rest[:half] + rest[half:]


def swap_both(values, sums, axis):
    first = lax.axis_index(axis) == 0
    kept = jnp.where(first, values[0], values[1])
    given = jnp.where(first, values[1], values[0])
    got = lax.ppermute(beside(given, sums), axis, SWAP).astype(F32)
    got, more = apart(got, kept.shape)
    return kept.astype(F32) + got, sums + more


def ring_both(blocks, sums, axis):
    result, dims = blocks[0].astype(F32), blocks[0].shape
    added = sums
    for k in range(1, 4):
        got, more = apart(shift(beside(blocks[k], sums), axis, -k).astype(F32), dims)
        result, added = result + got, added + more
    return result, added


def swapped(own, axis):
    return in_order(own, lax.ppermute(own, axis, SWAP), axis)


def lane_ids(rows):
    return lax.broadcasted_iota(jnp.int32, (rows, 2 * HD), 1)


def half_mean(values, lanes):
    low = jnp.sum(jnp.where(lanes < HD, values, 0.0), axis=-1, keepdims=True)
    high = jnp.sum(jnp.where(lanes < HD, 0.0, values), axis=-1, keepdims=True)
    return jnp.where(lanes < HD, low, high) * (1.0 / HD)


def turn(values, cosine, sine, lanes):
    swapped = jnp.where(
        (lanes & (HD - 1)) < HD // 2,
        pltpu.roll(values, 2 * HD - HD // 2, 1),
        pltpu.roll(values, HD // 2, 1),
    )
    return values * cosine + swapped * sine


def turn_tables():
    frequency = np.float32(10000.0) ** (np.arange(HD // 2, dtype=np.float32) * np.float32(-2 / HD))
    angles = np.arange(LEN, dtype=np.float32)[:, None] * frequency[None, :].astype(np.float32)
    cosine, sine = np.cos(angles), np.sin(angles)
    return (
        np.concatenate([cosine] * 4, axis=1).astype(np.float32),
        np.concatenate([-sine, sine] * 2, axis=1).astype(np.float32),
    )


def attend_kernel(*refs):
    place, tokens, here, there, query_gain, key_gain, cosine, sine = refs[:8]
    pre, query, keyval, out, part, weight, out_weight, router = refs[8:16]
    key_low, key_high, val_low, val_high = refs[16:]
    size = here.shape[2]
    for core, ring in enumerate((here, there)):
        for k in range(4):
            for y in range(2):
                block = y * 8 + ((place[1] + k) & 3) * 2 + (place[2] ^ core)
                rows = pl.ds(pl.multiple_of(block * size, size), size)
                weight[rows, :] = ring[k, y, :, : 4 * HD]
                out_weight[rows, :] = ring[k, y, :, 4 * HD : 6 * HD]
                router[rows, :] = ring[k, y, :, 6 * HD :]
    lanes = lane_ids(BLK)
    for j in range(ROWS):
        rows = pl.ds(j * BLK, BLK)
        block = dot(tokens[j], weight[...])
        pre[rows, :] = block
        cos_rows, sin_rows = cosine[rows, :], sine[rows, :]
        q_pre, kv_pre = block[:, : 2 * HD], block[:, 2 * HD :]
        q_scale = lax.rsqrt(half_mean(q_pre * q_pre, lanes) + EPS)
        turned = turn(q_pre * q_scale * query_gain[...], cos_rows, sin_rows, lanes)
        query[rows, :] = turned.astype(BF) * HD ** (-0.5)
        k_scale = lax.rsqrt(half_mean(kv_pre * kv_pre, lanes) + EPS)
        turned = turn(kv_pre * k_scale * key_gain[...], cos_rows, sin_rows, lanes)
        key = jnp.where(lanes < HD, turned, 0.0)
        val = jnp.where(lanes < HD, 0.0, kv_pre)
        keyval[rows, :] = (key + val).astype(BF)
        key_low[rows, :] = key.astype(BF)
        key_high[rows, :] = pltpu.roll(key, HD, 1).astype(BF)
        val_low[rows, :] = pltpu.roll(val, HD, 1).astype(BF)
        val_high[rows, :] = val.astype(BF)
    prefix = place[0]
    size = 2 * BLK
    key_at = lax.broadcasted_iota(jnp.int32, (size, LEN), 1)

    def step(index, carry):
        rows = pl.ds(pl.multiple_of(index * size, size), size)
        q_rows = query[rows, :]
        at = lax.broadcasted_iota(jnp.int32, (size, 1), 0) + index * size
        visible = key_at < jnp.maximum(at + 1, prefix)
        mixed = jnp.zeros((size, 2 * HD), F32)
        for keys, vals in ((key_low, val_low), (key_high, val_high)):
            weights = jnp.where(visible, jnp.exp(dot_nt(q_rows, keys[...])), 0.0)
            inverse = 1.0 / jnp.sum(weights, axis=-1, keepdims=True)
            mixed += dot((weights * inverse).astype(BF), vals[...])
        mixed = mixed.astype(BF)
        out[rows, :] = mixed
        share = dot_nt(mixed, out_weight[...]).astype(BF)
        part[pl.ds(index * 2, 2)] = share.reshape(2, BLK, -1)
        return carry

    lax.fori_loop(0, LEN // size, step, 0, unroll=True)


def put_blocks(sums, which, value):
    size = value.shape[0] // COLS
    for block in range(COLS):
        sums[block % 2, which, block // 8, block // 2 % 4] = value[block * size : (block + 1) * size]


def attend_back_kernel(*refs):
    place, middle, out_weight, tokens, weight, query_gain, key_gain, cosine, sine = refs[:9]
    pre, query, keyval, heads, router_sums = refs[9:14]
    part, sums, pre_sum, gain_sum = refs[14:18]
    key_low, key_high, val_low, val_high, key_t, grads, q_grad, kv_grad, low = refs[18:]
    lanes = lane_ids(BLK)
    for j in range(ROWS):
        rows = pl.ds(j * BLK, BLK)
        both = keyval[rows, :].astype(F32)
        key = jnp.where(lanes < HD, both, 0.0)
        val = jnp.where(lanes < HD, 0.0, both)
        key_two = pltpu.roll(key, HD, 1)
        key_low[rows, :] = key.astype(BF)
        key_high[rows, :] = key_two.astype(BF)
        val_low[rows, :] = pltpu.roll(val, HD, 1).astype(BF)
        val_high[rows, :] = val.astype(BF)
        key_t[:, j * BLK : (j + 1) * BLK] = (key + key_two).T.astype(BF)
        grads[rows, :] = dot(middle[j], out_weight[...]).astype(BF)
    kv_grad[...] = jnp.zeros_like(kv_grad)
    prefix = place[0]
    size = 2 * BLK
    key_at = lax.broadcasted_iota(jnp.int32, (LEN, size), 0)
    wide = lane_ids(size)

    def step(index, carry):
        rows = pl.ds(pl.multiple_of(index * size, size), size)
        q_rows, g_rows = query[rows, :], grads[rows, :]
        q_wide, g_wide = q_rows.astype(F32), g_rows.astype(F32)
        row_at = lax.broadcasted_iota(jnp.int32, (1, size), 1) + index * size
        visible = key_at < jnp.maximum(row_at + 1, prefix)
        q_t = []
        for head, (keys, vals) in enumerate(((key_low, val_low), (key_high, val_high))):
            weights = jnp.where(visible, jnp.exp(dot_nt(keys[...], q_rows)), 0.0)
            probs = weights * (1.0 / jnp.sum(weights, axis=0, keepdims=True))
            back = dot_nt(vals[...], g_rows)
            delta = jnp.sum(probs * back, axis=0, keepdims=True)
            score = (probs * (back - delta)).astype(BF)
            q_t.append(dot(key_t[head * HD : (head + 1) * HD, :], score))
            q_side = q_wide if head == 0 else pltpu.roll(q_wide, HD, 1)
            g_side = pltpu.roll(g_wide, HD, 1) if head == 0 else g_wide
            q_side = jnp.where(wide < HD, q_side, 0.0).astype(BF)
            g_side = jnp.where(wide < HD, 0.0, g_side).astype(BF)
            kv_grad[...] += dot(score, q_side) + dot(probs.astype(BF), g_side)
        q_grad[rows, :] = jnp.concatenate(q_t, axis=0).T * HD ** (-0.5)
        return carry

    lax.fori_loop(0, LEN // size, step, 0, unroll=True)
    q_gain, k_gain = query_gain[...], key_gain[...]
    q_terms = jnp.zeros((1, 2 * HD), F32)
    k_terms = jnp.zeros((1, 2 * HD), F32)
    for j in range(ROWS):
        rows = pl.ds(j * BLK, BLK)
        cos_rows, sin_rows = cosine[rows, :], -sine[rows, :]
        block = pre[rows, :]
        q_pre, kv_pre = block[:, : 2 * HD], block[:, 2 * HD :]
        q_scale = lax.rsqrt(half_mean(q_pre * q_pre, lanes) + EPS)
        q_hat = q_pre * q_scale
        turned = turn(q_grad[rows, :], cos_rows, sin_rows, lanes)
        q_terms += jnp.sum(q_hat * turned, axis=0, keepdims=True)
        inner = turned * q_gain
        q_back = q_scale * (inner - q_hat * half_mean(inner * q_hat, lanes))
        low[rows, : 2 * HD] = q_back.astype(BF)
        k_scale = lax.rsqrt(half_mean(kv_pre * kv_pre, lanes) + EPS)
        k_hat = kv_pre * k_scale
        both = kv_grad[rows, :]
        turned = turn(both, cos_rows, sin_rows, lanes)
        k_terms += jnp.sum(k_hat * turned, axis=0, keepdims=True)
        inner = turned * k_gain
        k_back = k_scale * (inner - k_hat * half_mean(inner * k_hat, lanes))
        low[rows, 2 * HD :] = jnp.where(lanes < HD, k_back, both).astype(BF)
    column = jnp.zeros((1, tokens.shape[2]), F32)
    count = LEN // 4
    for j in range(4):
        share = dot_nt(low[pl.ds(j * count, count), :], weight[...])
        part[j] = share.astype(BF).reshape(part.shape[1:])
        held = tokens[pl.ds(2 * j, 2)].reshape(count, -1).astype(F32)
        column += jnp.sum(held * share, axis=0, keepdims=True)
    pre_sum[...] = column
    gain_sum[...] = jnp.concatenate([q_terms, k_terms], axis=0)
    tall = tokens[...].reshape(LEN, -1)
    put_blocks(sums, 0, dot_tn(tall, low[:, : 2 * HD]).astype(BF))
    put_blocks(sums, 1, dot_tn(tall, low[:, 2 * HD :]).astype(BF))
    put_blocks(sums, 2, dot_tn(middle[...].reshape(LEN, -1), heads[...]).astype(BF))
    put_blocks(sums, 3, router_sums[...])


def norm_kernel(x_in, gain, copies):
    value = x_in[...].astype(F32)
    scale = lax.rsqrt(jnp.mean(value * value, axis=-1, keepdims=True) + EPS)
    normed = (value * scale * gain[...]).astype(BF)
    for k in range(ROWS):
        copies[k] = normed


def middle_kernel(x_in, gain, parts, middle, copies):
    value = x_in[...].astype(F32)
    for k in range(ROWS):
        value += parts[k].astype(F32)
    middle[...] = value
    scale = lax.rsqrt(jnp.mean(value * value, axis=-1, keepdims=True) + EPS)
    normed = (value * scale * gain[...]).astype(BF)
    for k in range(ROWS):
        copies[k] = normed


def middle_back_kernel(middle_in, gain, upstream, parts, grad, copies, gain_sum):
    value = middle_in[...]
    back = parts[0].astype(F32)
    for k in range(1, ROWS):
        back += parts[k].astype(F32)
    scale = lax.rsqrt(jnp.mean(value * value, axis=-1, keepdims=True) + EPS)
    hat = value * scale
    gain_sum[...] = jnp.sum(hat * back, axis=0, keepdims=True)
    inner = back * gain[...]
    result = upstream[...].astype(F32) + scale * (
        inner - hat * jnp.mean(inner * hat, axis=-1, keepdims=True)
    )
    grad[...] = result
    rounded = result.astype(BF)
    for k in range(ROWS):
        copies[k] = rounded


def pick_rows(slot_rows, expert):
    slots = slot_rows[pl.ds(expert, 1), :]
    return (lax.broadcasted_iota(jnp.int32, (CAP, LEN), 0) == slots).astype(BF)


def pick_tokens(slot_cols, rows, count):
    slots = slot_cols[rows, :]
    ids = lax.broadcasted_iota(jnp.int32, (count, BLK), 1)
    tiles = []
    for tile in range(LOCAL * CAP // BLK):
        first = tile * BLK
        hit = None
        for e in range(first // CAP, (first + BLK - 1) // CAP + 1):
            at = slots[:, e : e + 1]
            at = jnp.where(at < 0, at, at + (e * CAP - first))
            hit = ids == at if hit is None else hit | (ids == at)
        tiles.append(hit.astype(BF))
    return jnp.concatenate(tiles, axis=1)


def upstream_kernel(slot_rows, t_0, t_1, t_2, t_3, slot_up):
    choose = pick_rows(slot_rows, pl.program_id(0))
    size = 2 * BLK
    picked = jnp.zeros((CAP, t_0.shape[-1]), F32)
    for k, tokens in enumerate((t_0, t_1, t_2, t_3)):
        picked += dot(choose[:, k * size : (k + 1) * size], tokens[...].reshape(size, -1))
    slot_up[0] = picked.astype(BF)


def expert_kernel(
    slot_rows,
    slot_cols,
    tokens,
    router,
    router_t,
    weights,
    slot_up,
    sums,
    act_gated,
    part,
    logit_grad,
    probs,
    gate_rows,
    pre_grad,
    grads,
    gates,
):
    step = pl.program_id(0)
    inner = act_gated.shape[-1]
    size = tokens.shape[-1] // COLS

    def put(lanes, value):
        for block in range(COLS):
            rows = value[block * size : (block + 1) * size]
            sums[block % 8, block // 8, 0, :, lanes] = rows.astype(BF)

    @pl.when(step == 0)
    def _():
        lanes = lax.broadcasted_iota(jnp.int32, (LEN, BLK), 1)
        logits = jnp.where(lanes < EXPERTS, dot(tokens[...], router[...]), -1e30)
        exps = jnp.exp(logits - jnp.max(logits, axis=-1, keepdims=True))
        values = exps / jnp.sum(exps, axis=-1, keepdims=True)
        probs[...] = values
        gate_rows[...] = values.T[: 2 * LOCAL].astype(BF).astype(F32)

    @pl.when(step < LOCAL)
    def _():
        hit = lax.broadcasted_iota(jnp.int32, (CAP, LEN), 0) == slot_rows[pl.ds(step, 1), :]
        gate = jnp.sum(
            jnp.where(hit, gate_rows[pl.ds(step, 1), :], 0.0), axis=-1, keepdims=True
        )
        picked = dot(hit.astype(BF), tokens[...]).astype(BF)
        raw = dot(slot_up[0], weights[0, :, 2 * inner :])
        both = dot(picked, weights[0, :, : 2 * inner])
        gate_pre, up_pre = both[:, :inner], both[:, inner:]
        sigma = 1.0 / (1.0 + jnp.exp(-gate_pre))
        silu = gate_pre * sigma
        act = (silu * up_pre).astype(BF).astype(F32)
        gate_back = jnp.sum(act * raw, axis=-1, keepdims=True)
        act_gated[0] = (act * gate).astype(BF)
        act_grad = raw * gate
        pre_grad[:, :inner] = (
            act_grad * up_pre * sigma * (1.0 + gate_pre * (1.0 - sigma))
        ).astype(BF)
        pre_grad[:, inner:] = (act_grad * silu).astype(BF)
        rows = pl.ds(pl.multiple_of(step * CAP, CAP), CAP)
        grads[rows, :] = dot_nt(pre_grad[...], weights[0, :, : 2 * inner]).astype(BF)
        lanes = lax.broadcasted_iota(jnp.int32, (CAP, BLK), 1)
        gates[rows, :] = jnp.where(lanes == step, gate_back, 0.0).astype(BF)
        put(pl.ds(0, 2 * inner), dot_tn(picked, pre_grad[...]))
        put(pl.ds(2 * inner, inner), dot_tn(slot_up[0], act_gated[0]))

    @pl.when(step == LOCAL)
    def _():
        count = LEN // 4
        for j in range(LEN // count):
            rows = pl.ds(j * count, count)
            choose = pick_tokens(slot_cols, rows, count)
            gate_back = dot(choose, gates[...])
            own = probs[rows, :]
            weighted = own * gate_back
            logit = weighted - own * jnp.sum(weighted, axis=-1, keepdims=True)
            high = logit.astype(BF).astype(F32)
            both = (high + pltpu.roll(logit - high, EXPERTS, 1)).astype(BF)
            logit_grad[rows, :] = both
            value = (dot(choose, grads[...]) + dot(both, router_t[...])).astype(BF)
            for k in range(count // BLK):
                part[j * (count // BLK) + k] = value[k * BLK : (k + 1) * BLK]


def mix_kernel(
    at, slot_cols, tokens, logit_grad, weights, act_gated, m_0, m_1, m_2, m_3, router_sum, held
):
    step = pl.program_id(0)

    @pl.when(step == 0)
    def _():
        router_sum[...] = dot(logit_grad[...].astype(F32).T.astype(BF), tokens[...])

    @pl.when(step < LOCAL)
    def _():
        rows = pl.ds(pl.multiple_of(step * CAP, CAP), CAP)
        held[rows, :] = dot_nt(act_gated[0], weights[0]).astype(BF)

    @pl.when(step == LOCAL)
    def _():
        for k, mix in enumerate((m_0, m_1, m_2, m_3)):
            place = (at[0] + k) & 3
            rows = pl.ds(pl.multiple_of(place * 2 * BLK, 2 * BLK), 2 * BLK)
            value = dot(pick_tokens(slot_cols, rows, 2 * BLK), held[...]).astype(BF)
            mix[0] = value[:BLK]
            mix[1] = value[BLK:]


def shards(
    layer_input,
    prenorm,
    query_proj,
    key_proj,
    value_proj,
    querynorm,
    keynorm,
    out_proj,
    midnorm,
    router,
    gate_proj,
    up_proj,
    down_proj,
    routes,
    slot_ids,
    prefix,
    cotangent,
):
    width = layer_input.shape[-1]
    inner = gate_proj.shape[-1]
    row = lax.axis_index(ROW)
    z = lax.axis_index("z")
    at = z.reshape(1)
    col_rows = width // COLS

    x_low = layer_input[0]
    x = x_low.astype(F32)
    scale_one = lax.rsqrt(jnp.mean(x * x, axis=-1, keepdims=True) + EPS)
    copied = shape((ROWS, BLK, width), BF)
    (copies,) = call(norm_kernel, (copied,), x_low, prenorm[None, :])
    router_own = jnp.pad(router, ((0, 0), (0, BLK - EXPERTS)))
    small = swapped(
        jnp.concatenate([query_proj, key_proj, value_proj, out_proj.T, router_own], axis=1), "y_hi"
    )
    upstream = swapped(cotangent[0], "y_lo")
    copies, upstream, small = together(copies, upstream, small)
    upstream = [upstream] + [shift(upstream, "z", k) for k in range(1, 4)]
    tokens_one = send(copies, ROW)
    experts = lax.all_gather(
        jnp.concatenate([gate_proj, up_proj, down_proj.transpose(0, 2, 1)], axis=2),
        COL,
        axis=1,
        tiled=True,
    )
    small = jnp.stack([small] + [shift(small, "x", k) for k in range(1, 4)])
    small_there = lax.ppermute(small, "core", SWAP)

    cosine, sine = turn_tables()
    query_gain = jnp.concatenate([querynorm, querynorm])[None, :]
    key_gain = jnp.concatenate([keynorm, keynorm])[None, :]
    side = pltpu.VMEM((LEN, 2 * HD), BF)
    place = jnp.stack([prefix[0], lax.axis_index("x"), lax.axis_index("core")]).astype(jnp.int32)
    pre, query, keyval, attended, part_out, qkv_weight, out_weight, router_all = call(
        attend_kernel,
        (
            shape((LEN, 4 * HD), F32),
            shape((LEN, 2 * HD), BF),
            shape((LEN, 2 * HD), BF),
            shape((LEN, 2 * HD), BF),
            copied,
            shape((width, 4 * HD), BF),
            shape((width, 2 * HD), BF),
            shape((width, BLK), BF),
        ),
        place,
        tokens_one,
        small,
        small_there,
        query_gain,
        key_gain,
        cosine,
        sine,
        ins={0: SM},
        scratch=[side] * 4,
    )
    router_rel = lax.dynamic_slice_in_dim(
        jnp.concatenate([router_all[:, :EXPERTS]] * 2, axis=1), row * LOCAL, EXPERTS, 1
    )
    router_pad = jnp.pad(router_rel, ((0, 0), (0, BLK - EXPERTS)))
    router_t = jnp.pad(
        jnp.concatenate([router_rel.T, router_rel.T], axis=0), ((0, BLK - 2 * EXPERTS), (0, 0))
    )
    part_out, *upstream = together(part_out, *upstream)
    parts_out = send(part_out, ROW)
    middle, copies_two = call(
        middle_kernel,
        (shape((BLK, width), F32), copied),
        x_low,
        midnorm[None, :],
        parts_out,
    )

    ids = row * LOCAL + jnp.arange(2 * LOCAL, dtype=jnp.int32)
    mine = (routes[0][:, :, None] == ids) & (jnp.arange(2 * LOCAL) < LOCAL)
    slot_cols = jnp.sum(jnp.where(mine, slot_ids[0][:, :, None] + 1, 0), axis=1) - 1
    slot_rows = slot_cols.T
    turned_rows = lax.dynamic_slice_in_dim(
        jnp.concatenate([slot_rows, slot_rows], axis=1), z * 2 * BLK, LEN, 1
    )
    last = lambda e: jnp.minimum(e, LOCAL - 1)
    one = lambda *dims: pl.BlockSpec((1,) + dims, lambda e: (last(e),) + (0,) * len(dims))
    down_block = pl.BlockSpec((1, width, inner), lambda e: (last(e), 0, 2))
    tokens_two = send(copies_two, ROW).reshape(LEN, width)
    (slot_up,) = call(
        upstream_kernel,
        (shape((LOCAL, CAP, width), BF),),
        turned_rows,
        *upstream,
        grid=LOCAL,
        out_specs={0: one(CAP, width)},
    )
    sums, act_gated, part, logit_grad = call(
        expert_kernel,
        (
            shape((COLS // 2, 2, LOCAL, col_rows, 3 * inner), BF),
            shape((LOCAL, CAP, inner), BF),
            copied,
            shape((LEN, BLK), BF),
        ),
        slot_rows,
        slot_cols,
        tokens_two,
        router_pad,
        router_t,
        experts,
        slot_up,
        ins={5: one(width, 3 * inner), 6: one(CAP, width)},
        grid=LOCAL + 1,
        out_specs={
            0: pl.BlockSpec(
                (COLS // 2, 2, 1, col_rows, 3 * inner), lambda e: (0, 0, last(e), 0, 0)
            ),
            1: one(CAP, inner),
        },
        scratch=[
            pltpu.VMEM((LEN, BLK), F32),
            pltpu.VMEM((2 * LOCAL, LEN), F32),
            pltpu.VMEM((CAP, 2 * inner), BF),
            pltpu.VMEM((LOCAL * CAP, width), BF),
            pltpu.VMEM((LOCAL * CAP, BLK), BF),
        ],
    )
    parts_two = send(part, ROW)
    *mix, router_sum = call(
        mix_kernel,
        (*[shape((2, BLK, width), BF)] * 4, shape((BLK, width), F32)),
        at,
        slot_cols,
        tokens_two,
        logit_grad,
        experts,
        act_gated,
        ins={0: SM, 4: down_block, 5: one(CAP, inner)},
        grid=LOCAL + 1,
        scratch=[pltpu.VMEM((LOCAL * CAP, width), BF)],
    )
    halves = lax.psum_scatter(sums, ("x", "core"), scatter_dimension=0, tiled=False)
    router_rows = router_sum[:EXPERTS] + router_sum[EXPERTS : 2 * EXPERTS]
    router_rows = lax.dynamic_slice_in_dim(
        jnp.concatenate([router_rows, router_rows], axis=0), EXPERTS - row * LOCAL, EXPERTS, 0
    )
    router_sums = jnp.pad(router_rows, ((0, BLK - EXPERTS), (0, 0))).T.astype(BF)

    middle_grad, copies_mid, midnorm_part = call(
        middle_back_kernel,
        (shape((BLK, width), F32), copied, shape((1, width), F32)),
        middle,
        midnorm[None, :],
        cotangent[0],
        parts_two,
    )
    group_mid = send(copies_mid, ROW)
    group_mid, halves, *mix = together(group_mid, halves, *mix)
    mixed = ring_sum(mix, "z").astype(BF)
    y_hi = lax.axis_index("y_hi")
    kept = lax.dynamic_index_in_dim(halves, y_hi, 0, False).astype(F32)
    given = lax.dynamic_index_in_dim(halves, 1 - y_hi, 0, False)
    got = lax.ppermute(given, "y_hi", SWAP)
    part_one, sums_one, prenorm_part, gain_part = call(
        attend_back_kernel,
        (
            shape((4, 2, BLK, width), BF),
            shape((2, 4, 2, 4, col_rows, 2 * HD), BF),
            shape((1, width), F32),
            shape((2, 2 * HD), F32),
        ),
        prefix,
        group_mid,
        out_weight,
        tokens_one,
        qkv_weight,
        query_gain,
        key_gain,
        cosine,
        sine,
        pre,
        query,
        keyval,
        attended,
        router_sums,
        ins={0: SM},
        scratch=[side] * 4
        + [
            pltpu.VMEM((2 * HD, LEN), BF),
            side,
            pltpu.VMEM((LEN, 2 * HD), F32),
            pltpu.VMEM((LEN, 2 * HD), F32),
            pltpu.VMEM((LEN, 4 * HD), BF),
        ],
    )
    part_one, sums_one, mixed, got = together(part_one, sums_one, mixed, got)
    expert_grads = kept + got.astype(F32)
    parts_one = lax.all_to_all(part_one, "z", 0, 0)
    parts_one = jnp.sum(parts_one.astype(F32), axis=0).astype(BF)
    normed_one_grad = swap_halves(parts_one, "y_lo")

    lines = width // (2 * HD)
    late = jnp.concatenate(
        [
            (prenorm_part / prenorm).reshape(-1, 2 * HD),
            midnorm_part.reshape(-1, 2 * HD),
            gain_part,
            jnp.zeros((6, 2 * HD), F32),
        ],
        axis=0,
    )
    sums_one, late = swap_both(sums_one, late, "core")
    sums_one, late = ring_both(from_here(sums_one.astype(BF), "x", 2), late, "x")
    layer_output = (middle + swap_halves(mixed, "y_lo")).astype(BF)[None]
    sums_one, late = swap_both(jnp.moveaxis(sums_one.astype(BF), 1, 0), late, "y_hi")
    router_part = sums_one[3].astype(BF)
    router_part, late = swap_both(jnp.stack([router_part] * 2), late, "y_lo")
    router_part, late = ring_both([router_part.astype(BF)] * 4, late, "z")
    hat = x * scale_one
    weighted = normed_one_grad * prenorm
    input_grad = middle_grad + scale_one * (
        weighted - hat * jnp.mean(weighted * hat, axis=-1, keepdims=True)
    )
    query_terms, key_terms = late[2 * lines], late[2 * lines + 1]
    return (
        layer_output,
        input_grad[None],
        late[:lines].reshape(width),
        sums_one[0],
        sums_one[1][:, :HD],
        sums_one[1][:, HD:],
        query_terms[:HD] + query_terms[HD:],
        key_terms[:HD],
        sums_one[2].T,
        late[lines : 2 * lines].reshape(width),
        router_part[:, :EXPERTS],
        expert_grads[:, :, :inner],
        expert_grads[:, :, inner : 2 * inner],
        expert_grads[:, :, 2 * inner :].transpose(0, 2, 1),
    )


def solution(mesh):
    axes = ("z", "y_lo", "y_hi", "x", "core")
    return jax.shard_map(
        shards,
        mesh=jax.sharding.Mesh(mesh.devices.reshape(4, 2, 2, 4, 2), axes),
        in_specs=(
            P(COL, ROW, None),
            P(),
            P(COL, ROW),
            P(COL, ROW),
            P(COL, ROW),
            P(),
            P(),
            P(ROW, COL),
            P(),
            P(COL, None),
            P(ROW, COL, None),
            P(ROW, COL, None),
            P(ROW, None, COL),
            P(COL, None, None),
            P(COL, None, None),
            P(COL),
            P(COL, ROW, None),
        ),
        out_specs=(
            P(COL, ROW, None),
            P(COL, ROW, None),
            P(),
            P(COL, ROW),
            P(COL, ROW),
            P(COL, ROW),
            P(),
            P(),
            P(ROW, COL),
            P(),
            P(COL, None),
            P(ROW, COL, None),
            P(ROW, COL, None),
            P(ROW, None, COL),
        ),
        check_vma=False,
    )
```

```python
import jax
import jax.numpy as jnp
import numpy as np
from jax import lax
from jax.experimental import pallas as pl
from jax.experimental.pallas import tpu as pltpu
from jax.sharding import PartitionSpec as P

HD = 64
CAP = 448
ROWS = 8
COLS = 16
BLK = 128
LEN = ROWS * BLK
LOCAL = 4
EXPERTS = 32
EPS = 1e-06
BF = jnp.bfloat16
F32 = jnp.float32
SM = pl.BlockSpec(memory_space=pltpu.SMEM)
MIB = 1 << 20


def dot(a, b):
    return lax.dot_general(a, b, (((1,), (0,)), ((), ())), preferred_element_type=F32)


def dot_nt(a, b):
    return lax.dot_general(a, b, (((1,), (1,)), ((), ())), preferred_element_type=F32)


def dot_tn(a, b):
    return lax.dot_general(a, b, (((0,), (0,)), ((), ())), preferred_element_type=F32)


def shape(dims, kind):
    return jax.ShapeDtypeStruct(dims, kind)


def whole(value):
    dims = value.shape
    return pl.BlockSpec(dims, lambda i: (0,) * len(dims))


def call(body, outs, *args, grid=1, ins=None, out_specs=None, scratch=(), limit=56):
    ins, out_specs = ins or {}, out_specs or {}
    return pl.pallas_call(
        body,
        grid=(grid,),
        out_shape=outs,
        in_specs=[ins.get(i, whole(value)) for i, value in enumerate(args)],
        out_specs=[out_specs.get(i, whole(value)) for i, value in enumerate(outs)],
        scratch_shapes=list(scratch),
        compiler_params=pltpu.CompilerParams(vmem_limit_bytes=limit * MIB),
        cost_estimate=pl.CostEstimate(flops=0, bytes_accessed=0, transcendentals=0),
    )(*args)


ROW = ("z", "y_lo")
COL = ("y_hi", "x", "core")


SWAP = [(0, 1), (1, 0)]


def together(*values):
    return lax.optimization_barrier(values)


def send(blocks, axes):
    return lax.all_to_all(blocks, axes, 0, 0)


def gather(own, axes, count):
    return send(jnp.broadcast_to(own[None], (count,) + own.shape), axes)


def shift(values, axis, step):
    return lax.ppermute(values, axis, [(i, (i - step) % 4) for i in range(4)])


def in_order(own, other, axis, dim=0):
    first = lax.axis_index(axis) == 0
    return jnp.where(first, jnp.stack([own, other], dim), jnp.stack([other, own], dim))


def swap_halves(values, axis):
    first = lax.axis_index(axis) == 0
    kept = jnp.where(first, values[0], values[1])
    given = jnp.where(first, values[1], values[0])
    return kept.astype(F32) + lax.ppermute(given, axis, SWAP).astype(F32)


def ring_sum(blocks, axis):
    result = blocks[0].astype(F32)
    for k in range(1, 4):
        result = result + shift(blocks[k], axis, -k).astype(F32)
    return result


def from_here(values, axis, dim):
    here = lax.axis_index(axis)
    return [lax.dynamic_index_in_dim(values, (here + k) % 4, dim, False) for k in range(4)]


def beside(values, whole_sums):
    lines = values.reshape(-1, values.shape[-1])
    high = whole_sums.astype(BF)
    return jnp.concatenate([lines, high, (whole_sums - high.astype(F32)).astype(BF)], axis=0)


def apart(message, dims):
    count = 1
    for size in dims[:-1]:
        count *= size
    rest = message[count:]
    half = rest.shape[0] // 2
    return message[:count].reshape(dims), rest[:half] + rest[half:]


def kept_and_given(values, axis):
    here = lax.axis_index(axis)
    return (
        lax.dynamic_index_in_dim(values, here, 0, False),
        lax.dynamic_index_in_dim(values, 1 - here, 0, False),
    )


def swap_both(values, sums, axis):
    first = lax.axis_index(axis) == 0
    kept = jnp.where(first, values[0], values[1])
    given = jnp.where(first, values[1], values[0])
    got = lax.ppermute(beside(given, sums), axis, SWAP).astype(F32)
    got, more = apart(got, kept.shape)
    return kept.astype(F32) + got, sums + more


def ring_both(blocks, sums, axis):
    result, dims = blocks[0].astype(F32), blocks[0].shape
    added = sums
    for k in range(1, 4):
        got, more = apart(shift(beside(blocks[k], sums), axis, -k).astype(F32), dims)
        result, added = result + got, added + more
    return result, added


def swapped(own, axis):
    return in_order(own, lax.ppermute(own, axis, SWAP), axis)


def lane_ids(rows):
    return lax.broadcasted_iota(jnp.int32, (rows, 2 * HD), 1)


def half_mean(values, lanes):
    low = jnp.sum(jnp.where(lanes < HD, values, 0.0), axis=-1, keepdims=True)
    high = jnp.sum(jnp.where(lanes < HD, 0.0, values), axis=-1, keepdims=True)
    return jnp.where(lanes < HD, low, high) * (1.0 / HD)


def turn(values, cosine, sine, lanes):
    swapped = jnp.where(
        (lanes & (HD - 1)) < HD // 2,
        pltpu.roll(values, 2 * HD - HD // 2, 1),
        pltpu.roll(values, HD // 2, 1),
    )
    return values * cosine + swapped * sine


def turn_tables():
    frequency = np.float32(10000.0) ** (np.arange(HD // 2, dtype=np.float32) * np.float32(-2 / HD))
    angles = np.arange(LEN, dtype=np.float32)[:, None] * frequency[None, :].astype(np.float32)
    cosine, sine = np.cos(angles), np.sin(angles)
    return (
        np.concatenate([cosine] * 4, axis=1).astype(np.float32),
        np.concatenate([-sine, sine] * 2, axis=1).astype(np.float32),
    )


def attend_kernel(*refs):
    place, tokens, here, there, query_gain, key_gain, cosine, sine = refs[:8]
    pre, query, keyval, out, weight, out_weight, router = refs[8:15]
    key_low, key_high, val_low, val_high = refs[15:]
    size = here.shape[2]
    for core, ring in enumerate((here, there)):
        for k in range(4):
            for y in range(2):
                block = y * 8 + ((place[1] + k) & 3) * 2 + (place[2] ^ core)
                rows = pl.ds(pl.multiple_of(block * size, size), size)
                weight[rows, :] = ring[k, y, :, : 4 * HD]
                out_weight[rows, :] = ring[k, y, :, 4 * HD : 6 * HD]
                router[rows, :] = ring[k, y, :, 6 * HD :]
    lanes = lane_ids(BLK)
    for j in range(ROWS):
        rows = pl.ds(j * BLK, BLK)
        block = dot(tokens[j], weight[...])
        pre[rows, :] = block
        cos_rows, sin_rows = cosine[rows, :], sine[rows, :]
        q_pre, kv_pre = block[:, : 2 * HD], block[:, 2 * HD :]
        q_scale = lax.rsqrt(half_mean(q_pre * q_pre, lanes) + EPS)
        turned = turn(q_pre * q_scale * query_gain[...], cos_rows, sin_rows, lanes)
        query[rows, :] = turned.astype(BF) * HD ** (-0.5)
        k_scale = lax.rsqrt(half_mean(kv_pre * kv_pre, lanes) + EPS)
        turned = turn(kv_pre * k_scale * key_gain[...], cos_rows, sin_rows, lanes)
        key = jnp.where(lanes < HD, turned, 0.0)
        val = jnp.where(lanes < HD, 0.0, kv_pre)
        keyval[rows, :] = (key + val).astype(BF)
        key_low[rows, :] = key.astype(BF)
        key_high[rows, :] = pltpu.roll(key, HD, 1).astype(BF)
        val_low[rows, :] = pltpu.roll(val, HD, 1).astype(BF)
        val_high[rows, :] = val.astype(BF)
    prefix = place[0]
    size = 2 * BLK
    key_at = lax.broadcasted_iota(jnp.int32, (size, LEN), 1)

    def step(index, carry):
        rows = pl.ds(pl.multiple_of(index * size, size), size)
        q_rows = query[rows, :]
        at = lax.broadcasted_iota(jnp.int32, (size, 1), 0) + index * size
        visible = key_at < jnp.maximum(at + 1, prefix)
        mixed = jnp.zeros((size, 2 * HD), F32)
        for keys, vals in ((key_low, val_low), (key_high, val_high)):
            weights = jnp.where(visible, jnp.exp(dot_nt(q_rows, keys[...])), 0.0)
            inverse = 1.0 / jnp.sum(weights, axis=-1, keepdims=True)
            mixed += dot((weights * inverse).astype(BF), vals[...])
        mixed = mixed.astype(BF)
        out[0, index] = mixed[:BLK]
        out[1, index] = mixed[BLK:]
        return carry

    lax.fori_loop(0, LEN // size, step, 0, unroll=True)


def share_kernel(place, mine, other, weight, ring, part, there):
    size = ring.shape[3]
    for core in range(2):
        for k in range(4):
            for y in range(2):
                block = y * 8 + ((place[1] + k) & 3) * 2 + (place[2] ^ core)
                rows = pl.ds(pl.multiple_of(block * size, size), size)
                there[rows, :] = ring[core, k, y]
    value = dot_nt(mine[...].reshape(LEN // 2, -1), weight[...])
    value += dot_nt(other[...].reshape(LEN // 2, -1), there[...])
    part[...] = value.astype(BF).reshape(part.shape)


def put_blocks(sums, which, value):
    size = value.shape[0] // COLS
    for block in range(COLS):
        at = (which * 8 + block // 2) * size
        sums[block % 2, at : at + size, :] = value[block * size : (block + 1) * size]


def attend_back_kernel(*refs):
    place, middle, out_weight, tokens, weight, query_gain, key_gain, cosine, sine = refs[:9]
    pre, query, keyval, heads, router_sums, pre_gain, mid_sum = refs[9:16]
    part, sums, late = refs[16:19]
    key_low, key_high, val_low, val_high, key_t, grads, q_grad, kv_grad, low = refs[19:]
    lanes = lane_ids(BLK)
    for j in range(ROWS):
        rows = pl.ds(j * BLK, BLK)
        both = keyval[rows, :].astype(F32)
        key = jnp.where(lanes < HD, both, 0.0)
        val = jnp.where(lanes < HD, 0.0, both)
        key_two = pltpu.roll(key, HD, 1)
        key_low[rows, :] = key.astype(BF)
        key_high[rows, :] = key_two.astype(BF)
        val_low[rows, :] = pltpu.roll(val, HD, 1).astype(BF)
        val_high[rows, :] = val.astype(BF)
        key_t[:, j * BLK : (j + 1) * BLK] = (key + key_two).T.astype(BF)
        grads[rows, :] = dot(middle[j], out_weight[...]).astype(BF)
    kv_grad[...] = jnp.zeros_like(kv_grad)
    prefix = place[0]
    size = 2 * BLK
    key_at = lax.broadcasted_iota(jnp.int32, (LEN, size), 0)
    wide = lane_ids(size)

    def step(index, carry):
        rows = pl.ds(pl.multiple_of(index * size, size), size)
        q_rows, g_rows = query[rows, :], grads[rows, :]
        q_wide, g_wide = q_rows.astype(F32), g_rows.astype(F32)
        row_at = lax.broadcasted_iota(jnp.int32, (1, size), 1) + index * size
        visible = key_at < jnp.maximum(row_at + 1, prefix)
        q_t = []
        for head, (keys, vals) in enumerate(((key_low, val_low), (key_high, val_high))):
            weights = jnp.where(visible, jnp.exp(dot_nt(keys[...], q_rows)), 0.0)
            probs = weights * (1.0 / jnp.sum(weights, axis=0, keepdims=True))
            back = dot_nt(vals[...], g_rows)
            delta = jnp.sum(probs * back, axis=0, keepdims=True)
            score = (probs * (back - delta)).astype(BF)
            q_t.append(dot(key_t[head * HD : (head + 1) * HD, :], score))
            q_side = q_wide if head == 0 else pltpu.roll(q_wide, HD, 1)
            g_side = pltpu.roll(g_wide, HD, 1) if head == 0 else g_wide
            q_side = jnp.where(wide < HD, q_side, 0.0).astype(BF)
            g_side = jnp.where(wide < HD, 0.0, g_side).astype(BF)
            kv_grad[...] += dot(score, q_side) + dot(probs.astype(BF), g_side)
        q_grad[rows, :] = jnp.concatenate(q_t, axis=0).T * HD ** (-0.5)
        return carry

    lax.fori_loop(0, LEN // size, step, 0, unroll=True)
    q_gain, k_gain = query_gain[...], key_gain[...]
    q_terms = jnp.zeros((1, 2 * HD), F32)
    k_terms = jnp.zeros((1, 2 * HD), F32)
    for j in range(ROWS):
        rows = pl.ds(j * BLK, BLK)
        cos_rows, sin_rows = cosine[rows, :], -sine[rows, :]
        block = pre[rows, :]
        q_pre, kv_pre = block[:, : 2 * HD], block[:, 2 * HD :]
        q_scale = lax.rsqrt(half_mean(q_pre * q_pre, lanes) + EPS)
        q_hat = q_pre * q_scale
        turned = turn(q_grad[rows, :], cos_rows, sin_rows, lanes)
        q_terms += jnp.sum(q_hat * turned, axis=0, keepdims=True)
        inner = turned * q_gain
        q_back = q_scale * (inner - q_hat * half_mean(inner * q_hat, lanes))
        low[rows, : 2 * HD] = q_back.astype(BF)
        k_scale = lax.rsqrt(half_mean(kv_pre * kv_pre, lanes) + EPS)
        k_hat = kv_pre * k_scale
        both = kv_grad[rows, :]
        turned = turn(both, cos_rows, sin_rows, lanes)
        k_terms += jnp.sum(k_hat * turned, axis=0, keepdims=True)
        inner = turned * k_gain
        k_back = k_scale * (inner - k_hat * half_mean(inner * k_hat, lanes))
        low[rows, 2 * HD :] = jnp.where(lanes < HD, k_back, both).astype(BF)
    column = jnp.zeros((1, tokens.shape[2]), F32)
    count = LEN // 4
    for j in range(4):
        share = dot_nt(low[pl.ds(j * count, count), :], weight[...])
        part[j] = share.astype(BF).reshape(part.shape[1:])
        held = tokens[pl.ds(2 * j, 2)].reshape(count, -1).astype(F32)
        column += jnp.sum(held * share, axis=0, keepdims=True)
    column = column / pre_gain[...]
    tall = [column[:, k : k + 2 * HD] for k in range(0, column.shape[1], 2 * HD)]
    tall += [mid_sum[:, k : k + 2 * HD] for k in range(0, column.shape[1], 2 * HD)]
    tall += [q_terms, k_terms, jnp.zeros((6, 2 * HD), F32)]
    total = jnp.concatenate(tall, axis=0)
    high = total.astype(BF)
    late[...] = total
    for core in range(2):
        sums[core, -48:, :] = jnp.concatenate(
            [high, (total - high.astype(F32)).astype(BF)], axis=0
        )
    tall = tokens[...].reshape(LEN, -1)
    ordered = jnp.concatenate([heads[j % 2, j // 2] for j in range(ROWS)], axis=0)
    put_blocks(sums, 0, dot_tn(tall, low[:, : 2 * HD]).astype(BF))
    put_blocks(sums, 1, dot_tn(tall, low[:, 2 * HD :]).astype(BF))
    put_blocks(sums, 2, dot_tn(middle[...].reshape(LEN, -1), ordered).astype(BF))
    put_blocks(sums, 3, router_sums[...])


def norm_kernel(x_in, gain, copies):
    value = x_in[...].astype(F32)
    scale = lax.rsqrt(jnp.mean(value * value, axis=-1, keepdims=True) + EPS)
    normed = (value * scale * gain[...]).astype(BF)
    for k in range(ROWS):
        copies[k] = normed


def middle_kernel(x_in, gain, parts, middle, copies):
    value = x_in[...].astype(F32)
    for k in range(parts.shape[0]):
        value += parts[k].astype(F32)
    middle[...] = value
    scale = lax.rsqrt(jnp.mean(value * value, axis=-1, keepdims=True) + EPS)
    normed = (value * scale * gain[...]).astype(BF)
    for k in range(ROWS):
        copies[k] = normed


def middle_back_kernel(middle_in, gain, upstream, parts, grad, copies, gain_sum):
    value = middle_in[...]
    back = parts[0].astype(F32)
    for k in range(1, ROWS):
        back += parts[k].astype(F32)
    scale = lax.rsqrt(jnp.mean(value * value, axis=-1, keepdims=True) + EPS)
    hat = value * scale
    gain_sum[...] = jnp.sum(hat * back, axis=0, keepdims=True)
    inner = back * gain[...]
    result = upstream[...].astype(F32) + scale * (
        inner - hat * jnp.mean(inner * hat, axis=-1, keepdims=True)
    )
    grad[...] = result
    rounded = result.astype(BF)
    for k in range(ROWS):
        copies[k] = rounded


def pick_rows(slot_rows, expert):
    slots = slot_rows[pl.ds(expert, 1), :]
    return (lax.broadcasted_iota(jnp.int32, (CAP, LEN), 0) == slots).astype(BF)


def pick_tokens(slot_cols, rows, count):
    slots = slot_cols[rows, :]
    ids = lax.broadcasted_iota(jnp.int32, (count, BLK), 1)
    tiles = []
    for tile in range(LOCAL * CAP // BLK):
        first = tile * BLK
        hit = None
        for e in range(first // CAP, (first + BLK - 1) // CAP + 1):
            at = slots[:, e : e + 1]
            at = jnp.where(at < 0, at, at + (e * CAP - first))
            hit = ids == at if hit is None else hit | (ids == at)
        tiles.append(hit.astype(BF))
    return jnp.concatenate(tiles, axis=1)


def upstream_kernel(slot_rows, t_0, t_1, t_2, t_3, slot_up):
    choose = pick_rows(slot_rows, pl.program_id(0))
    size = 2 * BLK
    picked = jnp.zeros((CAP, t_0.shape[-1]), F32)
    for k, tokens in enumerate((t_0, t_1, t_2, t_3)):
        picked += dot(choose[:, k * size : (k + 1) * size], tokens[...].reshape(size, -1))
    slot_up[0] = picked.astype(BF)


def expert_kernel(
    slot_rows,
    slot_cols,
    tokens,
    router,
    router_t,
    weights,
    slot_up,
    sums,
    act_gated,
    part,
    logit_grad,
    probs,
    gate_rows,
    pre_grad,
    grads,
    gates,
):
    step = pl.program_id(0)
    inner = act_gated.shape[-1]
    size = tokens.shape[-1] // COLS

    def put(lanes, value):
        for block in range(COLS):
            rows = value[block * size : (block + 1) * size]
            sums[block % 8, block // 8, 0, :, lanes] = rows.astype(BF)

    @pl.when(step == 0)
    def _():
        lanes = lax.broadcasted_iota(jnp.int32, (LEN, BLK), 1)
        logits = jnp.where(lanes < EXPERTS, dot(tokens[...], router[...]), -1e30)
        exps = jnp.exp(logits - jnp.max(logits, axis=-1, keepdims=True))
        values = exps / jnp.sum(exps, axis=-1, keepdims=True)
        probs[...] = values
        gate_rows[...] = values.T[: 2 * LOCAL].astype(BF).astype(F32)

    @pl.when(step < LOCAL)
    def _():
        hit = lax.broadcasted_iota(jnp.int32, (CAP, LEN), 0) == slot_rows[pl.ds(step, 1), :]
        gate = jnp.sum(
            jnp.where(hit, gate_rows[pl.ds(step, 1), :], 0.0), axis=-1, keepdims=True
        )
        picked = dot(hit.astype(BF), tokens[...]).astype(BF)
        raw = dot(slot_up[0], weights[0, :, 2 * inner :])
        both = dot(picked, weights[0, :, : 2 * inner])
        gate_pre, up_pre = both[:, :inner], both[:, inner:]
        sigma = 1.0 / (1.0 + jnp.exp(-gate_pre))
        silu = gate_pre * sigma
        act = (silu * up_pre).astype(BF).astype(F32)
        gate_back = jnp.sum(act * raw, axis=-1, keepdims=True)
        act_gated[0] = (act * gate).astype(BF)
        act_grad = raw * gate
        pre_grad[:, :inner] = (
            act_grad * up_pre * sigma * (1.0 + gate_pre * (1.0 - sigma))
        ).astype(BF)
        pre_grad[:, inner:] = (act_grad * silu).astype(BF)
        rows = pl.ds(pl.multiple_of(step * CAP, CAP), CAP)
        grads[rows, :] = dot_nt(pre_grad[...], weights[0, :, : 2 * inner]).astype(BF)
        lanes = lax.broadcasted_iota(jnp.int32, (CAP, BLK), 1)
        gates[rows, :] = jnp.where(lanes == step, gate_back, 0.0).astype(BF)
        put(pl.ds(0, 2 * inner), dot_tn(picked, pre_grad[...]))
        put(pl.ds(2 * inner, inner), dot_tn(slot_up[0], act_gated[0]))

    @pl.when(step == LOCAL)
    def _():
        count = LEN // 4
        for j in range(LEN // count):
            rows = pl.ds(j * count, count)
            choose = pick_tokens(slot_cols, rows, count)
            gate_back = dot(choose, gates[...])
            own = probs[rows, :]
            weighted = own * gate_back
            logit = weighted - own * jnp.sum(weighted, axis=-1, keepdims=True)
            high = logit.astype(BF).astype(F32)
            both = (high + pltpu.roll(logit - high, EXPERTS, 1)).astype(BF)
            logit_grad[rows, :] = both
            value = (dot(choose, grads[...]) + dot(both, router_t[...])).astype(BF)
            for k in range(count // BLK):
                part[j * (count // BLK) + k] = value[k * BLK : (k + 1) * BLK]


def mix_kernel(
    at, slot_cols, tokens, logit_grad, weights, act_gated, m_0, m_1, m_2, m_3, router_sum, held
):
    step = pl.program_id(0)

    @pl.when(step == 0)
    def _():
        router_sum[...] = dot(logit_grad[...].astype(F32).T.astype(BF), tokens[...])

    @pl.when(step < LOCAL)
    def _():
        rows = pl.ds(pl.multiple_of(step * CAP, CAP), CAP)
        held[rows, :] = dot_nt(act_gated[0], weights[0]).astype(BF)

    @pl.when(step == LOCAL)
    def _():
        for k, mix in enumerate((m_0, m_1, m_2, m_3)):
            place = (at[0] + k) & 3
            rows = pl.ds(pl.multiple_of(place * 2 * BLK, 2 * BLK), 2 * BLK)
            value = dot(pick_tokens(slot_cols, rows, 2 * BLK), held[...]).astype(BF)
            mix[0] = value[:BLK]
            mix[1] = value[BLK:]


def shards(
    layer_input,
    prenorm,
    query_proj,
    key_proj,
    value_proj,
    querynorm,
    keynorm,
    out_proj,
    midnorm,
    router,
    gate_proj,
    up_proj,
    down_proj,
    routes,
    slot_ids,
    prefix,
    cotangent,
):
    width = layer_input.shape[-1]
    inner = gate_proj.shape[-1]
    row = lax.axis_index(ROW)
    z = lax.axis_index("z")
    at = z.reshape(1)
    col_rows = width // COLS

    x_low = layer_input[0]
    x = x_low.astype(F32)
    scale_one = lax.rsqrt(jnp.mean(x * x, axis=-1, keepdims=True) + EPS)
    copied = shape((ROWS, BLK, width), BF)
    (copies,) = call(norm_kernel, (copied,), x_low, prenorm[None, :], limit=16)
    router_own = jnp.pad(router, ((0, 0), (0, BLK - EXPERTS)))
    small = swapped(
        jnp.concatenate([query_proj, key_proj, value_proj, out_proj.T, router_own], axis=1), "y_hi"
    )
    upstream = swapped(cotangent[0], "y_lo")
    copies, upstream, small = together(copies, upstream, small)
    upstream = [upstream] + [shift(upstream, "z", k) for k in range(1, 4)]
    tokens_one = send(copies, ROW)
    experts = lax.all_gather(
        jnp.concatenate([gate_proj, up_proj, down_proj.transpose(0, 2, 1)], axis=2),
        COL,
        axis=1,
        tiled=True,
    )
    small = jnp.stack([small] + [shift(small, "x", k) for k in range(1, 4)])
    small_there = lax.ppermute(small, "core", SWAP)
    out_there = jnp.stack([small, small_there])[..., 4 * HD : 6 * HD]
    out_there = lax.ppermute(out_there, "y_lo", SWAP)

    cosine, sine = turn_tables()
    query_gain = jnp.concatenate([querynorm, querynorm])[None, :]
    key_gain = jnp.concatenate([keynorm, keynorm])[None, :]
    side = pltpu.VMEM((LEN, 2 * HD), BF)
    place = jnp.stack([prefix[0], lax.axis_index("x"), lax.axis_index("core")]).astype(jnp.int32)
    pre, query, keyval, attended, qkv_weight, out_weight, router_all = call(
        attend_kernel,
        (
            shape((LEN, 4 * HD), F32),
            shape((LEN, 2 * HD), BF),
            shape((LEN, 2 * HD), BF),
            shape((2, 4, BLK, 2 * HD), BF),
            shape((width, 4 * HD), BF),
            shape((width, 2 * HD), BF),
            shape((width, BLK), BF),
        ),
        place,
        tokens_one,
        small,
        small_there,
        query_gain,
        key_gain,
        cosine,
        sine,
        ins={0: SM},
        scratch=[side] * 4,
        limit=32,
    )
    router_rel = lax.dynamic_slice_in_dim(
        jnp.concatenate([router_all[:, :EXPERTS]] * 2, axis=1), row * LOCAL, EXPERTS, 1
    )
    router_pad = jnp.pad(router_rel, ((0, 0), (0, BLK - EXPERTS)))
    router_t = jnp.pad(
        jnp.concatenate([router_rel.T, router_rel.T], axis=0), ((0, BLK - 2 * EXPERTS), (0, 0))
    )
    mine, given = kept_and_given(attended, "y_lo")
    (part_out,) = call(
        share_kernel,
        (shape((4, BLK, width), BF),),
        place,
        mine,
        lax.ppermute(given, "y_lo", SWAP),
        out_weight,
        out_there,
        ins={0: SM},
        scratch=[pltpu.VMEM((width, 2 * HD), BF)],
        limit=16,
    )
    part_out, *upstream = together(part_out, *upstream)
    parts_out = lax.all_to_all(part_out, "z", 0, 0)
    middle, copies_two = call(
        middle_kernel,
        (shape((BLK, width), F32), copied),
        x_low,
        midnorm[None, :],
        parts_out,
        limit=16,
    )

    ids = row * LOCAL + jnp.arange(2 * LOCAL, dtype=jnp.int32)
    mine = (routes[0][:, :, None] == ids) & (jnp.arange(2 * LOCAL) < LOCAL)
    slot_cols = jnp.sum(jnp.where(mine, slot_ids[0][:, :, None] + 1, 0), axis=1) - 1
    slot_rows = slot_cols.T
    turned_rows = lax.dynamic_slice_in_dim(
        jnp.concatenate([slot_rows, slot_rows], axis=1), z * 2 * BLK, LEN, 1
    )
    last = lambda e: jnp.minimum(e, LOCAL - 1)
    one = lambda *dims: pl.BlockSpec((1,) + dims, lambda e: (last(e),) + (0,) * len(dims))
    down_block = pl.BlockSpec((1, width, inner), lambda e: (last(e), 0, 2))
    tokens_two = send(copies_two, ROW).reshape(LEN, width)
    (slot_up,) = call(
        upstream_kernel,
        (shape((LOCAL, CAP, width), BF),),
        turned_rows,
        *upstream,
        grid=LOCAL,
        out_specs={0: one(CAP, width)},
        limit=24,
    )
    sums, act_gated, part, logit_grad = call(
        expert_kernel,
        (
            shape((COLS // 2, 2, LOCAL, col_rows, 3 * inner), BF),
            shape((LOCAL, CAP, inner), BF),
            copied,
            shape((LEN, BLK), BF),
        ),
        slot_rows,
        slot_cols,
        tokens_two,
        router_pad,
        router_t,
        experts,
        slot_up,
        ins={5: one(width, 3 * inner), 6: one(CAP, width)},
        grid=LOCAL + 1,
        out_specs={
            0: pl.BlockSpec(
                (COLS // 2, 2, 1, col_rows, 3 * inner), lambda e: (0, 0, last(e), 0, 0)
            ),
            1: one(CAP, inner),
        },
        scratch=[
            pltpu.VMEM((LEN, BLK), F32),
            pltpu.VMEM((2 * LOCAL, LEN), F32),
            pltpu.VMEM((CAP, 2 * inner), BF),
            pltpu.VMEM((LOCAL * CAP, width), BF),
            pltpu.VMEM((LOCAL * CAP, BLK), BF),
        ],
    )
    parts_two = send(part, ROW)
    *mix, router_sum = call(
        mix_kernel,
        (*[shape((2, BLK, width), BF)] * 4, shape((BLK, width), F32)),
        at,
        slot_cols,
        tokens_two,
        logit_grad,
        experts,
        act_gated,
        ins={0: SM, 4: down_block, 5: one(CAP, inner)},
        grid=LOCAL + 1,
        scratch=[pltpu.VMEM((LOCAL * CAP, width), BF)],
        limit=32,
    )
    halves = lax.psum_scatter(sums, ("x", "core"), scatter_dimension=0, tiled=False)
    router_rows = router_sum[:EXPERTS] + router_sum[EXPERTS : 2 * EXPERTS]
    router_rows = lax.dynamic_slice_in_dim(
        jnp.concatenate([router_rows, router_rows], axis=0), EXPERTS - row * LOCAL, EXPERTS, 0
    )
    router_sums = jnp.pad(router_rows, ((0, BLK - EXPERTS), (0, 0))).T.astype(BF)

    middle_grad, copies_mid, midnorm_part = call(
        middle_back_kernel,
        (shape((BLK, width), F32), copied, shape((1, width), F32)),
        middle,
        midnorm[None, :],
        cotangent[0],
        parts_two,
        limit=16,
    )
    group_mid = send(copies_mid, ROW)
    group_mid, *mix = together(group_mid, *mix)
    mix = mix[:1] + [shift(block, "z", -k) for k, block in enumerate(mix) if k]
    part_one, sums_one, late = call(
        attend_back_kernel,
        (
            shape((4, 2, BLK, width), BF),
            shape((2, 2 * width + 48, 2 * HD), BF),
            shape((24, 2 * HD), F32),
        ),
        prefix,
        group_mid,
        out_weight,
        tokens_one,
        qkv_weight,
        query_gain,
        key_gain,
        cosine,
        sine,
        pre,
        query,
        keyval,
        attended,
        router_sums,
        prenorm[None, :],
        midnorm_part,
        ins={0: SM},
        scratch=[side] * 4
        + [
            pltpu.VMEM((2 * HD, LEN), BF),
            side,
            pltpu.VMEM((LEN, 2 * HD), F32),
            pltpu.VMEM((LEN, 2 * HD), F32),
            pltpu.VMEM((LEN, 4 * HD), BF),
        ],
        limit=40,
    )
    part_one, sums_one, halves, *mix = together(part_one, sums_one, halves, *mix)
    kept, given = kept_and_given(halves, "y_hi")
    got = lax.ppermute(given, "y_hi", SWAP)
    parts_one = lax.all_to_all(part_one, "z", 0, 0)
    parts_one = jnp.sum(parts_one.astype(F32), axis=0).astype(BF)
    normed_one_grad = swap_halves(parts_one, "y_lo")

    lines = width // (2 * HD)
    mine, sent = kept_and_given(sums_one, "core")
    dims = (4, 2, 4, col_rows, 2 * HD)
    sums_one, more = apart(lax.ppermute(sent, "core", SWAP).astype(F32), dims)
    sums_one, late = mine[: 2 * width].astype(F32).reshape(dims) + sums_one, late + more
    sums_one, late, *mix = together(sums_one.astype(BF), late, *mix)
    mixed = sum(block.astype(F32) for block in mix).astype(BF)
    sums_one, late = ring_both(from_here(sums_one, "x", 2), late, "x")
    sums_one, late, got = together(sums_one, late, got)
    expert_grads = kept.astype(F32) + got.astype(F32)
    layer_output = (middle + swap_halves(mixed, "y_lo")).astype(BF)[None]
    sums_one, late = swap_both(jnp.moveaxis(sums_one.astype(BF), 1, 0), late, "y_hi")
    router_part = sums_one[3].astype(BF)
    router_part, late = swap_both(jnp.stack([router_part] * 2), late, "y_lo")
    router_part, late = ring_both([router_part.astype(BF)] * 4, late, "z")
    hat = x * scale_one
    weighted = normed_one_grad * prenorm
    input_grad = middle_grad + scale_one * (
        weighted - hat * jnp.mean(weighted * hat, axis=-1, keepdims=True)
    )
    query_terms, key_terms = late[2 * lines], late[2 * lines + 1]
    return (
        layer_output,
        input_grad[None],
        late[:lines].reshape(width),
        sums_one[0],
        sums_one[1][:, :HD],
        sums_one[1][:, HD:],
        query_terms[:HD] + query_terms[HD:],
        key_terms[:HD],
        sums_one[2].T,
        late[lines : 2 * lines].reshape(width),
        router_part[:, :EXPERTS],
        expert_grads[:, :, :inner],
        expert_grads[:, :, inner : 2 * inner],
        expert_grads[:, :, 2 * inner :].transpose(0, 2, 1),
    )


def solution(mesh):
    axes = ("z", "y_lo", "y_hi", "x", "core")
    return jax.shard_map(
        shards,
        mesh=jax.sharding.Mesh(mesh.devices.reshape(4, 2, 2, 4, 2), axes),
        in_specs=(
            P(COL, ROW, None),
            P(),
            P(COL, ROW),
            P(COL, ROW),
            P(COL, ROW),
            P(),
            P(),
            P(ROW, COL),
            P(),
            P(COL, None),
            P(ROW, COL, None),
            P(ROW, COL, None),
            P(ROW, None, COL),
            P(COL, None, None),
            P(COL, None, None),
            P(COL),
            P(COL, ROW, None),
        ),
        out_specs=(
            P(COL, ROW, None),
            P(COL, ROW, None),
            P(),
            P(COL, ROW),
            P(COL, ROW),
            P(COL, ROW),
            P(),
            P(),
            P(ROW, COL),
            P(),
            P(COL, None),
            P(ROW, COL, None),
            P(ROW, COL, None),
            P(ROW, None, COL),
        ),
        check_vma=False,
    )
```

```python
import jax
import jax.numpy as jnp
import numpy as np
from jax import lax
from jax.experimental import pallas as pl
from jax.experimental.pallas import tpu as pltpu
from jax.sharding import PartitionSpec as P

HD = 64
CAP = 448
ROWS = 8
COLS = 16
BLK = 128
LEN = ROWS * BLK
LOCAL = 4
EXPERTS = 32
EPS = 1e-06
BF = jnp.bfloat16
F32 = jnp.float32
SM = pl.BlockSpec(memory_space=pltpu.SMEM)
MIB = 1 << 20


def dot(a, b):
    return lax.dot_general(a, b, (((1,), (0,)), ((), ())), preferred_element_type=F32)


def dot_nt(a, b):
    return lax.dot_general(a, b, (((1,), (1,)), ((), ())), preferred_element_type=F32)


def dot_tn(a, b):
    return lax.dot_general(a, b, (((0,), (0,)), ((), ())), preferred_element_type=F32)


def shape(dims, kind):
    return jax.ShapeDtypeStruct(dims, kind)


def whole(value):
    dims = value.shape
    return pl.BlockSpec(dims, lambda i: (0,) * len(dims))


def call(body, outs, *args, grid=1, ins=None, out_specs=None, scratch=(), limit=56):
    ins, out_specs = ins or {}, out_specs or {}
    return pl.pallas_call(
        body,
        grid=(grid,),
        out_shape=outs,
        in_specs=[ins.get(i, whole(value)) for i, value in enumerate(args)],
        out_specs=[out_specs.get(i, whole(value)) for i, value in enumerate(outs)],
        scratch_shapes=list(scratch),
        compiler_params=pltpu.CompilerParams(vmem_limit_bytes=limit * MIB),
        cost_estimate=pl.CostEstimate(flops=0, bytes_accessed=0, transcendentals=0),
    )(*args)


ROW = ("z", "y_lo")
COL = ("y_hi", "x", "core")


SWAP = [(0, 1), (1, 0)]


def together(*values):
    return lax.optimization_barrier(values)


def send(blocks, axes):
    return lax.all_to_all(blocks, axes, 0, 0)


def gather(own, axes, count):
    return send(jnp.broadcast_to(own[None], (count,) + own.shape), axes)


def shift(values, axis, step):
    return lax.ppermute(values, axis, [(i, (i - step) % 4) for i in range(4)])


def in_order(own, other, axis, dim=0):
    first = lax.axis_index(axis) == 0
    return jnp.where(first, jnp.stack([own, other], dim), jnp.stack([other, own], dim))


def swap_halves(values, axis):
    first = lax.axis_index(axis) == 0
    kept = jnp.where(first, values[0], values[1])
    given = jnp.where(first, values[1], values[0])
    return kept.astype(F32) + lax.ppermute(given, axis, SWAP).astype(F32)


def ring_sum(blocks, axis):
    result = blocks[0].astype(F32)
    for k in range(1, 4):
        result = result + shift(blocks[k], axis, -k).astype(F32)
    return result


def from_here(values, axis, dim):
    here = lax.axis_index(axis)
    return [lax.dynamic_index_in_dim(values, (here + k) % 4, dim, False) for k in range(4)]


def beside(values, whole_sums):
    lines = values.reshape(-1, values.shape[-1])
    high = whole_sums.astype(BF)
    return jnp.concatenate([lines, high, (whole_sums - high.astype(F32)).astype(BF)], axis=0)


def apart(message, dims):
    count = 1
    for size in dims[:-1]:
        count *= size
    rest = message[count:]
    half = rest.shape[0] // 2
    return message[:count].reshape(dims), rest[:half] + rest[half:]


def kept_and_given(values, axis):
    here = lax.axis_index(axis)
    return (
        lax.dynamic_index_in_dim(values, here, 0, False),
        lax.dynamic_index_in_dim(values, 1 - here, 0, False),
    )


def swap_both(values, sums, axis):
    first = lax.axis_index(axis) == 0
    kept = jnp.where(first, values[0], values[1])
    given = jnp.where(first, values[1], values[0])
    got = lax.ppermute(beside(given, sums), axis, SWAP).astype(F32)
    got, more = apart(got, kept.shape)
    return kept.astype(F32) + got, sums + more


def ring_both(blocks, sums, axis):
    result, dims = blocks[0].astype(F32), blocks[0].shape
    added = sums
    for k in range(1, 4):
        got, more = apart(shift(beside(blocks[k], sums), axis, -k).astype(F32), dims)
        result, added = result + got, added + more
    return result, added


def swapped(own, axis):
    return in_order(own, lax.ppermute(own, axis, SWAP), axis)


def lane_ids(rows):
    return lax.broadcasted_iota(jnp.int32, (rows, 2 * HD), 1)


def half_mean(values, lanes):
    low = jnp.sum(jnp.where(lanes < HD, values, 0.0), axis=-1, keepdims=True)
    high = jnp.sum(jnp.where(lanes < HD, 0.0, values), axis=-1, keepdims=True)
    return jnp.where(lanes < HD, low, high) * (1.0 / HD)


def turn(values, cosine, sine, lanes):
    swapped = jnp.where(
        (lanes & (HD - 1)) < HD // 2,
        pltpu.roll(values, 2 * HD - HD // 2, 1),
        pltpu.roll(values, HD // 2, 1),
    )
    return values * cosine + swapped * sine


def turn_tables():
    frequency = np.float32(10000.0) ** (np.arange(HD // 2, dtype=np.float32) * np.float32(-2 / HD))
    angles = np.arange(LEN, dtype=np.float32)[:, None] * frequency[None, :].astype(np.float32)
    cosine, sine = np.cos(angles), np.sin(angles)
    return (
        np.concatenate([cosine] * 4, axis=1).astype(np.float32),
        np.concatenate([-sine, sine] * 2, axis=1).astype(np.float32),
    )


def attend_kernel(*refs):
    place, tokens, here, there, query_gain, key_gain, cosine, sine = refs[:8]
    pre, query, keyval, out, weight, out_weight, router = refs[8:15]
    key_low, key_high, val_low, val_high = refs[15:]
    size = here.shape[2]
    for core, ring in enumerate((here, there)):
        for k in range(4):
            for y in range(2):
                block = y * 8 + ((place[1] + k) & 3) * 2 + (place[2] ^ core)
                rows = pl.ds(pl.multiple_of(block * size, size), size)
                weight[rows, :] = ring[k, y, :, : 4 * HD]
                out_weight[rows, :] = ring[k, y, :, 4 * HD : 6 * HD]
                router[rows, :] = ring[k, y, :, 6 * HD :]
    lanes = lane_ids(BLK)
    for j in range(ROWS):
        rows = pl.ds(j * BLK, BLK)
        block = dot(tokens[j], weight[...])
        pre[rows, :] = block
        cos_rows, sin_rows = cosine[rows, :], sine[rows, :]
        q_pre, kv_pre = block[:, : 2 * HD], block[:, 2 * HD :]
        q_scale = lax.rsqrt(half_mean(q_pre * q_pre, lanes) + EPS)
        turned = turn(q_pre * q_scale * query_gain[...], cos_rows, sin_rows, lanes)
        query[rows, :] = turned.astype(BF) * HD ** (-0.5)
        k_scale = lax.rsqrt(half_mean(kv_pre * kv_pre, lanes) + EPS)
        turned = turn(kv_pre * k_scale * key_gain[...], cos_rows, sin_rows, lanes)
        key = jnp.where(lanes < HD, turned, 0.0)
        val = jnp.where(lanes < HD, 0.0, kv_pre)
        keyval[rows, :] = (key + val).astype(BF)
        key_low[rows, :] = key.astype(BF)
        key_high[rows, :] = pltpu.roll(key, HD, 1).astype(BF)
        val_low[rows, :] = pltpu.roll(val, HD, 1).astype(BF)
        val_high[rows, :] = val.astype(BF)
    prefix = place[0]
    size = 2 * BLK
    key_at = lax.broadcasted_iota(jnp.int32, (size, LEN), 1)

    def step(index, carry):
        rows = pl.ds(pl.multiple_of(index * size, size), size)
        q_rows = query[rows, :]
        at = lax.broadcasted_iota(jnp.int32, (size, 1), 0) + index * size
        visible = key_at < jnp.maximum(at + 1, prefix)
        mixed = jnp.zeros((size, 2 * HD), F32)
        for keys, vals in ((key_low, val_low), (key_high, val_high)):
            weights = jnp.where(visible, jnp.exp(dot_nt(q_rows, keys[...])), 0.0)
            inverse = 1.0 / jnp.sum(weights, axis=-1, keepdims=True)
            mixed += dot((weights * inverse).astype(BF), vals[...])
        mixed = mixed.astype(BF)
        out[0, index] = mixed[:BLK]
        out[1, index] = mixed[BLK:]
        return carry

    lax.fori_loop(0, LEN // size, step, 0, unroll=True)


def share_kernel(mine, other, weight, there, part):
    value = dot_nt(mine[...].reshape(LEN // 2, -1), weight[...])
    value += dot_nt(other[...].reshape(LEN // 2, -1), there[...])
    part[...] = value.astype(BF).reshape(part.shape)


def order_kernel(place, ring, there):
    size = ring.shape[3]
    for core in range(2):
        for k in range(4):
            for y in range(2):
                block = y * 8 + ((place[1] + k) & 3) * 2 + (place[2] ^ core)
                rows = pl.ds(pl.multiple_of(block * size, size), size)
                there[rows, :] = ring[core, k, y]


def put_blocks(first, mine, given, which, value):
    size = value.shape[0] // COLS
    for block in range(COLS // 2):
        rows = pl.ds((which * 8 + block) * size, size)
        even = value[2 * block * size : (2 * block + 1) * size]
        odd = value[(2 * block + 1) * size : (2 * block + 2) * size]
        mine[rows, :] = jnp.where(first, even, odd)
        given[rows, :] = jnp.where(first, odd, even)


def attend_back_kernel(*refs):
    place, middle, out_weight, tokens, weight, query_gain, key_gain, cosine, sine = refs[:9]
    pre, query, keyval, heads, router_sums, pre_gain, mid_sum = refs[9:16]
    sent, mine, given, late = refs[16:20]
    key_low, key_high, val_low, val_high, key_t, grads, q_grad, kv_grad, low = refs[20:]
    lanes = lane_ids(BLK)
    for j in range(ROWS):
        rows = pl.ds(j * BLK, BLK)
        both = keyval[rows, :].astype(F32)
        key = jnp.where(lanes < HD, both, 0.0)
        val = jnp.where(lanes < HD, 0.0, both)
        key_two = pltpu.roll(key, HD, 1)
        key_low[rows, :] = key.astype(BF)
        key_high[rows, :] = key_two.astype(BF)
        val_low[rows, :] = pltpu.roll(val, HD, 1).astype(BF)
        val_high[rows, :] = val.astype(BF)
        key_t[:, j * BLK : (j + 1) * BLK] = (key + key_two).T.astype(BF)
        grads[rows, :] = dot(middle[j], out_weight[...]).astype(BF)
    kv_grad[...] = jnp.zeros_like(kv_grad)
    prefix = place[0]
    size = 2 * BLK
    key_at = lax.broadcasted_iota(jnp.int32, (LEN, size), 0)
    wide = lane_ids(size)

    def step(index, carry):
        rows = pl.ds(pl.multiple_of(index * size, size), size)
        q_rows, g_rows = query[rows, :], grads[rows, :]
        q_wide, g_wide = q_rows.astype(F32), g_rows.astype(F32)
        row_at = lax.broadcasted_iota(jnp.int32, (1, size), 1) + index * size
        visible = key_at < jnp.maximum(row_at + 1, prefix)
        q_t = []
        for head, (keys, vals) in enumerate(((key_low, val_low), (key_high, val_high))):
            weights = jnp.where(visible, jnp.exp(dot_nt(keys[...], q_rows)), 0.0)
            probs = weights * (1.0 / jnp.sum(weights, axis=0, keepdims=True))
            back = dot_nt(vals[...], g_rows)
            delta = jnp.sum(probs * back, axis=0, keepdims=True)
            score = (probs * (back - delta)).astype(BF)
            q_t.append(dot(key_t[head * HD : (head + 1) * HD, :], score))
            q_side = q_wide if head == 0 else pltpu.roll(q_wide, HD, 1)
            g_side = pltpu.roll(g_wide, HD, 1) if head == 0 else g_wide
            q_side = jnp.where(wide < HD, q_side, 0.0).astype(BF)
            g_side = jnp.where(wide < HD, 0.0, g_side).astype(BF)
            kv_grad[...] += dot(score, q_side) + dot(probs.astype(BF), g_side)
        q_grad[rows, :] = jnp.concatenate(q_t, axis=0).T * HD ** (-0.5)
        return carry

    lax.fori_loop(0, LEN // size, step, 0, unroll=True)
    q_gain, k_gain = query_gain[...], key_gain[...]
    q_terms = jnp.zeros((1, 2 * HD), F32)
    k_terms = jnp.zeros((1, 2 * HD), F32)
    for j in range(ROWS):
        rows = pl.ds(j * BLK, BLK)
        cos_rows, sin_rows = cosine[rows, :], -sine[rows, :]
        block = pre[rows, :]
        q_pre, kv_pre = block[:, : 2 * HD], block[:, 2 * HD :]
        q_scale = lax.rsqrt(half_mean(q_pre * q_pre, lanes) + EPS)
        q_hat = q_pre * q_scale
        turned = turn(q_grad[rows, :], cos_rows, sin_rows, lanes)
        q_terms += jnp.sum(q_hat * turned, axis=0, keepdims=True)
        inner = turned * q_gain
        q_back = q_scale * (inner - q_hat * half_mean(inner * q_hat, lanes))
        low[rows, : 2 * HD] = q_back.astype(BF)
        k_scale = lax.rsqrt(half_mean(kv_pre * kv_pre, lanes) + EPS)
        k_hat = kv_pre * k_scale
        both = kv_grad[rows, :]
        turned = turn(both, cos_rows, sin_rows, lanes)
        k_terms += jnp.sum(k_hat * turned, axis=0, keepdims=True)
        inner = turned * k_gain
        k_back = k_scale * (inner - k_hat * half_mean(inner * k_hat, lanes))
        low[rows, 2 * HD :] = jnp.where(lanes < HD, k_back, both).astype(BF)
    column = jnp.zeros((1, tokens.shape[2]), F32)
    count = LEN // 4
    for j in range(4):
        share = dot_nt(low[pl.ds(j * count, count), :], weight[...])
        sent[0, j] = low[pl.ds(j * count, BLK), :]
        sent[1, j] = low[pl.ds(j * count + BLK, BLK), :]
        held = tokens[pl.ds(2 * j, 2)].reshape(count, -1).astype(F32)
        column += jnp.sum(held * share, axis=0, keepdims=True)
    column = column / pre_gain[...]
    tall = [column[:, k : k + 2 * HD] for k in range(0, column.shape[1], 2 * HD)]
    tall += [mid_sum[:, k : k + 2 * HD] for k in range(0, column.shape[1], 2 * HD)]
    tall += [q_terms, k_terms, jnp.zeros((6, 2 * HD), F32)]
    total = jnp.concatenate(tall, axis=0)
    high = total.astype(BF)
    late[...] = total
    given[-48:, :] = jnp.concatenate([high, (total - high.astype(F32)).astype(BF)], axis=0)
    first = place[1] == 0
    tall = tokens[...].reshape(LEN, -1)
    ordered = jnp.concatenate([heads[j % 2, j // 2] for j in range(ROWS)], axis=0)
    put_blocks(first, mine, given, 0, dot_tn(tall, low[:, : 2 * HD]).astype(BF))
    put_blocks(first, mine, given, 1, dot_tn(tall, low[:, 2 * HD :]).astype(BF))
    put_blocks(first, mine, given, 2, dot_tn(middle[...].reshape(LEN, -1), ordered).astype(BF))
    put_blocks(first, mine, given, 3, router_sums[...])


def norm_kernel(x_in, gain, copies):
    value = x_in[...].astype(F32)
    scale = lax.rsqrt(jnp.mean(value * value, axis=-1, keepdims=True) + EPS)
    normed = (value * scale * gain[...]).astype(BF)
    for k in range(ROWS):
        copies[k] = normed


def middle_kernel(x_in, gain, parts, middle, copies):
    value = x_in[...].astype(F32)
    for k in range(parts.shape[0]):
        value += parts[k].astype(F32)
    middle[...] = value
    scale = lax.rsqrt(jnp.mean(value * value, axis=-1, keepdims=True) + EPS)
    normed = (value * scale * gain[...]).astype(BF)
    for k in range(ROWS):
        copies[k] = normed


def middle_back_kernel(middle_in, gain, upstream, parts, grad, copies, gain_sum):
    value = middle_in[...]
    back = parts[0].astype(F32)
    for k in range(1, ROWS):
        back += parts[k].astype(F32)
    scale = lax.rsqrt(jnp.mean(value * value, axis=-1, keepdims=True) + EPS)
    hat = value * scale
    gain_sum[...] = jnp.sum(hat * back, axis=0, keepdims=True)
    inner = back * gain[...]
    result = upstream[...].astype(F32) + scale * (
        inner - hat * jnp.mean(inner * hat, axis=-1, keepdims=True)
    )
    grad[...] = result
    rounded = result.astype(BF)
    for k in range(ROWS):
        copies[k] = rounded


def pick_rows(slot_rows, expert):
    slots = slot_rows[pl.ds(expert, 1), :]
    return (lax.broadcasted_iota(jnp.int32, (CAP, LEN), 0) == slots).astype(BF)


def pick_tokens(slot_cols, rows, count):
    slots = slot_cols[rows, :]
    ids = lax.broadcasted_iota(jnp.int32, (count, BLK), 1)
    tiles = []
    for tile in range(LOCAL * CAP // BLK):
        first = tile * BLK
        hit = None
        for e in range(first // CAP, (first + BLK - 1) // CAP + 1):
            at = slots[:, e : e + 1]
            at = jnp.where(at < 0, at, at + (e * CAP - first))
            hit = ids == at if hit is None else hit | (ids == at)
        tiles.append(hit.astype(BF))
    return jnp.concatenate(tiles, axis=1)


def upstream_kernel(slot_rows, t_0, t_1, t_2, t_3, slot_up):
    choose = pick_rows(slot_rows, pl.program_id(0))
    size = 2 * BLK
    picked = jnp.zeros((CAP, t_0.shape[-1]), F32)
    for k, tokens in enumerate((t_0, t_1, t_2, t_3)):
        picked += dot(choose[:, k * size : (k + 1) * size], tokens[...].reshape(size, -1))
    slot_up[0] = picked.astype(BF)


def expert_kernel(
    slot_rows,
    slot_cols,
    tokens,
    router,
    router_t,
    weights,
    slot_up,
    sums,
    act_gated,
    part,
    logit_grad,
    probs,
    gate_rows,
    pre_grad,
    grads,
    gates,
):
    step = pl.program_id(0)
    inner = act_gated.shape[-1]
    size = tokens.shape[-1] // COLS

    def put(lanes, value):
        for block in range(COLS):
            rows = value[block * size : (block + 1) * size]
            sums[block % 8, block // 8, 0, :, lanes] = rows.astype(BF)

    @pl.when(step == 0)
    def _():
        lanes = lax.broadcasted_iota(jnp.int32, (LEN, BLK), 1)
        logits = jnp.where(lanes < EXPERTS, dot(tokens[...], router[...]), -1e30)
        exps = jnp.exp(logits - jnp.max(logits, axis=-1, keepdims=True))
        values = exps / jnp.sum(exps, axis=-1, keepdims=True)
        probs[...] = values
        gate_rows[...] = values.T[: 2 * LOCAL].astype(BF).astype(F32)

    @pl.when(step < LOCAL)
    def _():
        hit = lax.broadcasted_iota(jnp.int32, (CAP, LEN), 0) == slot_rows[pl.ds(step, 1), :]
        gate = jnp.sum(
            jnp.where(hit, gate_rows[pl.ds(step, 1), :], 0.0), axis=-1, keepdims=True
        )
        picked = dot(hit.astype(BF), tokens[...]).astype(BF)
        raw = dot(slot_up[0], weights[0, :, 2 * inner :])
        both = dot(picked, weights[0, :, : 2 * inner])
        gate_pre, up_pre = both[:, :inner], both[:, inner:]
        sigma = 1.0 / (1.0 + jnp.exp(-gate_pre))
        silu = gate_pre * sigma
        act = (silu * up_pre).astype(BF).astype(F32)
        gate_back = jnp.sum(act * raw, axis=-1, keepdims=True)
        act_gated[0] = (act * gate).astype(BF)
        act_grad = raw * gate
        pre_grad[:, :inner] = (
            act_grad * up_pre * sigma * (1.0 + gate_pre * (1.0 - sigma))
        ).astype(BF)
        pre_grad[:, inner:] = (act_grad * silu).astype(BF)
        rows = pl.ds(pl.multiple_of(step * CAP, CAP), CAP)
        grads[rows, :] = dot_nt(pre_grad[...], weights[0, :, : 2 * inner]).astype(BF)
        lanes = lax.broadcasted_iota(jnp.int32, (CAP, BLK), 1)
        gates[rows, :] = jnp.where(lanes == step, gate_back, 0.0).astype(BF)
        put(pl.ds(0, 2 * inner), dot_tn(picked, pre_grad[...]))
        put(pl.ds(2 * inner, inner), dot_tn(slot_up[0], act_gated[0]))

    @pl.when(step == LOCAL)
    def _():
        count = LEN // 4
        for j in range(LEN // count):
            rows = pl.ds(j * count, count)
            choose = pick_tokens(slot_cols, rows, count)
            gate_back = dot(choose, gates[...])
            own = probs[rows, :]
            weighted = own * gate_back
            logit = weighted - own * jnp.sum(weighted, axis=-1, keepdims=True)
            high = logit.astype(BF).astype(F32)
            both = (high + pltpu.roll(logit - high, EXPERTS, 1)).astype(BF)
            logit_grad[rows, :] = both
            value = (dot(choose, grads[...]) + dot(both, router_t[...])).astype(BF)
            for k in range(count // BLK):
                part[j * (count // BLK) + k] = value[k * BLK : (k + 1) * BLK]


def mix_kernel(
    at, slot_cols, tokens, logit_grad, weights, act_gated, m_0, m_1, m_2, m_3, router_sum, held
):
    step = pl.program_id(0)

    @pl.when(step == 0)
    def _():
        value = dot(logit_grad[...].astype(F32).T.astype(BF), tokens[...])
        given = lax.broadcasted_iota(jnp.int32, (BLK, BLK), 0)
        taken = lax.broadcasted_iota(jnp.int32, (BLK, BLK), 1)
        moved = (given + LOCAL * at[1]) & (EXPERTS - 1)
        order = ((moved == taken) & (given < 2 * EXPERTS)).astype(BF)
        router_sum[...] = dot(value.T.astype(BF), order).astype(BF)

    @pl.when(step < LOCAL)
    def _():
        rows = pl.ds(pl.multiple_of(step * CAP, CAP), CAP)
        held[rows, :] = dot_nt(act_gated[0], weights[0]).astype(BF)

    @pl.when(step == LOCAL)
    def _():
        for k, mix in enumerate((m_0, m_1, m_2, m_3)):
            place = (at[0] + k) & 3
            rows = pl.ds(pl.multiple_of(place * 2 * BLK, 2 * BLK), 2 * BLK)
            value = dot(pick_tokens(slot_cols, rows, 2 * BLK), held[...]).astype(BF)
            mix[0] = value[:BLK]
            mix[1] = value[BLK:]


def shards(
    layer_input,
    prenorm,
    query_proj,
    key_proj,
    value_proj,
    querynorm,
    keynorm,
    out_proj,
    midnorm,
    router,
    gate_proj,
    up_proj,
    down_proj,
    routes,
    slot_ids,
    prefix,
    cotangent,
):
    width = layer_input.shape[-1]
    inner = gate_proj.shape[-1]
    row = lax.axis_index(ROW)
    z = lax.axis_index("z")
    at = jnp.stack([z, row]).astype(jnp.int32)
    col_rows = width // COLS

    x_low = layer_input[0]
    x = x_low.astype(F32)
    scale_one = lax.rsqrt(jnp.mean(x * x, axis=-1, keepdims=True) + EPS)
    copied = shape((ROWS, BLK, width), BF)
    (copies,) = call(norm_kernel, (copied,), x_low, prenorm[None, :], limit=16)
    router_own = jnp.pad(router, ((0, 0), (0, BLK - EXPERTS)))
    small = swapped(
        jnp.concatenate([query_proj, key_proj, value_proj, out_proj.T, router_own], axis=1), "y_hi"
    )
    upstream = swapped(cotangent[0], "y_lo")
    copies, upstream, small = together(copies, upstream, small)
    upstream = [upstream] + [shift(upstream, "z", k) for k in range(1, 4)]
    tokens_one = send(copies, ROW)
    experts = lax.all_gather(
        jnp.concatenate([gate_proj, up_proj, down_proj.transpose(0, 2, 1)], axis=2),
        COL,
        axis=1,
        tiled=True,
    )
    small = jnp.stack([small] + [shift(small, "x", k) for k in range(1, 4)])
    small_there = lax.ppermute(small, "core", SWAP)
    out_there = jnp.stack([small, small_there])[..., 4 * HD : 6 * HD]
    out_there = lax.ppermute(out_there, "y_lo", SWAP)

    cosine, sine = turn_tables()
    query_gain = jnp.concatenate([querynorm, querynorm])[None, :]
    key_gain = jnp.concatenate([keynorm, keynorm])[None, :]
    side = pltpu.VMEM((LEN, 2 * HD), BF)
    place = jnp.stack([prefix[0], lax.axis_index("x"), lax.axis_index("core")]).astype(jnp.int32)
    pre, query, keyval, attended, qkv_weight, out_weight, router_all = call(
        attend_kernel,
        (
            shape((LEN, 4 * HD), F32),
            shape((LEN, 2 * HD), BF),
            shape((LEN, 2 * HD), BF),
            shape((2, 4, BLK, 2 * HD), BF),
            shape((width, 4 * HD), BF),
            shape((width, 2 * HD), BF),
            shape((width, BLK), BF),
        ),
        place,
        tokens_one,
        small,
        small_there,
        query_gain,
        key_gain,
        cosine,
        sine,
        ins={0: SM},
        scratch=[side] * 4,
        limit=32,
    )
    router_rel = lax.dynamic_slice_in_dim(
        jnp.concatenate([router_all[:, :EXPERTS]] * 2, axis=1), row * LOCAL, EXPERTS, 1
    )
    router_pad = jnp.pad(router_rel, ((0, 0), (0, BLK - EXPERTS)))
    router_t = jnp.pad(
        jnp.concatenate([router_rel.T, router_rel.T], axis=0), ((0, BLK - 2 * EXPERTS), (0, 0))
    )
    mine, given = kept_and_given(attended, "y_lo")
    (out_there,) = call(
        order_kernel,
        (shape((width, 2 * HD), BF),),
        place,
        out_there,
        ins={0: SM},
        limit=16,
    )
    (part_out,) = call(
        share_kernel,
        (shape((4, BLK, width), BF),),
        mine,
        lax.ppermute(given, "y_lo", SWAP),
        out_weight,
        out_there,
        limit=16,
    )
    part_out, *upstream = together(part_out, *upstream)
    parts_out = lax.all_to_all(part_out, "z", 0, 0)
    middle, copies_two = call(
        middle_kernel,
        (shape((BLK, width), F32), copied),
        x_low,
        midnorm[None, :],
        parts_out,
        limit=16,
    )

    ids = row * LOCAL + jnp.arange(2 * LOCAL, dtype=jnp.int32)
    mine = (routes[0][:, :, None] == ids) & (jnp.arange(2 * LOCAL) < LOCAL)
    slot_cols = jnp.sum(jnp.where(mine, slot_ids[0][:, :, None] + 1, 0), axis=1) - 1
    slot_rows = slot_cols.T
    turned_rows = lax.dynamic_slice_in_dim(
        jnp.concatenate([slot_rows, slot_rows], axis=1), z * 2 * BLK, LEN, 1
    )
    last = lambda e: jnp.minimum(e, LOCAL - 1)
    one = lambda *dims: pl.BlockSpec((1,) + dims, lambda e: (last(e),) + (0,) * len(dims))
    down_block = pl.BlockSpec((1, width, inner), lambda e: (last(e), 0, 2))
    tokens_two = send(copies_two, ROW).reshape(LEN, width)
    (slot_up,) = call(
        upstream_kernel,
        (shape((LOCAL, CAP, width), BF),),
        turned_rows,
        *upstream,
        grid=LOCAL,
        out_specs={0: one(CAP, width)},
        limit=24,
    )
    sums, act_gated, part, logit_grad = call(
        expert_kernel,
        (
            shape((COLS // 2, 2, LOCAL, col_rows, 3 * inner), BF),
            shape((LOCAL, CAP, inner), BF),
            copied,
            shape((LEN, BLK), BF),
        ),
        slot_rows,
        slot_cols,
        tokens_two,
        router_pad,
        router_t,
        experts,
        slot_up,
        ins={5: one(width, 3 * inner), 6: one(CAP, width)},
        grid=LOCAL + 1,
        out_specs={
            0: pl.BlockSpec(
                (COLS // 2, 2, 1, col_rows, 3 * inner), lambda e: (0, 0, last(e), 0, 0)
            ),
            1: one(CAP, inner),
        },
        scratch=[
            pltpu.VMEM((LEN, BLK), F32),
            pltpu.VMEM((2 * LOCAL, LEN), F32),
            pltpu.VMEM((CAP, 2 * inner), BF),
            pltpu.VMEM((LOCAL * CAP, width), BF),
            pltpu.VMEM((LOCAL * CAP, BLK), BF),
        ],
    )
    parts_two = send(part, ROW)
    *mix, router_sums = call(
        mix_kernel,
        (*[shape((2, BLK, width), BF)] * 4, shape((width, BLK), BF)),
        at,
        slot_cols,
        tokens_two,
        logit_grad,
        experts,
        act_gated,
        ins={0: SM, 4: down_block, 5: one(CAP, inner)},
        grid=LOCAL + 1,
        scratch=[pltpu.VMEM((LOCAL * CAP, width), BF)],
        limit=32,
    )
    halves = lax.psum_scatter(sums, ("x", "core"), scatter_dimension=0, tiled=False)

    middle_grad, copies_mid, midnorm_part = call(
        middle_back_kernel,
        (shape((BLK, width), F32), copied, shape((1, width), F32)),
        middle,
        midnorm[None, :],
        cotangent[0],
        parts_two,
        limit=16,
    )
    group_mid = send(copies_mid, ROW)
    group_mid, qkv_weight, *mix = together(group_mid, qkv_weight, *mix)
    qkv_there = lax.ppermute(qkv_weight, "y_lo", SWAP)
    mix = mix[:1] + [shift(block, "z", -k) for k, block in enumerate(mix) if k]
    low, mine, given, late = call(
        attend_back_kernel,
        (
            shape((2, 4, BLK, 4 * HD), BF),
            shape((2 * width, 2 * HD), BF),
            shape((2 * width + 48, 2 * HD), BF),
            shape((24, 2 * HD), F32),
        ),
        jnp.stack([prefix[0], lax.axis_index("core")]).astype(jnp.int32),
        group_mid,
        out_weight,
        tokens_one,
        qkv_weight,
        query_gain,
        key_gain,
        cosine,
        sine,
        pre,
        query,
        keyval,
        attended,
        router_sums,
        prenorm[None, :],
        midnorm_part,
        ins={0: SM},
        scratch=[side] * 4
        + [
            pltpu.VMEM((2 * HD, LEN), BF),
            side,
            pltpu.VMEM((LEN, 2 * HD), F32),
            pltpu.VMEM((LEN, 2 * HD), F32),
            pltpu.VMEM((LEN, 4 * HD), BF),
        ],
    )
    low, given, halves, qkv_there, *mix = together(low, given, halves, qkv_there, *mix)

    lines = width // (2 * HD)
    dims = (4, 2, 4, col_rows, 2 * HD)
    sums_one, more = apart(lax.ppermute(given, "core", SWAP).astype(F32), dims)
    sums_one, late = mine.astype(F32).reshape(dims) + sums_one, late + more
    sums_one, late, low, *mix = together(sums_one.astype(BF), late, low, *mix)
    low_mine, low_given = kept_and_given(low, "y_lo")
    (part_one,) = call(
        share_kernel,
        (shape((4, BLK, width), BF),),
        low_mine,
        lax.ppermute(low_given, "y_lo", SWAP),
        qkv_weight,
        qkv_there,
        limit=16,
    )
    parts_one = lax.all_to_all(part_one, "z", 0, 0)
    normed_one_grad = jnp.sum(parts_one.astype(F32), axis=0)
    mixed = sum(block.astype(F32) for block in mix).astype(BF)
    sums_one, late = ring_both(from_here(sums_one, "x", 2), late, "x")
    layer_output = (middle + swap_halves(mixed, "y_lo")).astype(BF)[None]
    sums_one, late = swap_both(jnp.moveaxis(sums_one.astype(BF), 1, 0), late, "y_hi")
    router_part = sums_one[3].astype(BF)
    router_part, late = swap_both(jnp.stack([router_part] * 2), late, "y_lo")
    router_part, late, halves = together(router_part.astype(BF), late, halves)
    expert_grads = swap_halves(halves, "y_hi")
    router_part, late = ring_both([router_part] * 4, late, "z")
    hat = x * scale_one
    weighted = normed_one_grad * prenorm
    input_grad = middle_grad + scale_one * (
        weighted - hat * jnp.mean(weighted * hat, axis=-1, keepdims=True)
    )
    query_terms, key_terms = late[2 * lines], late[2 * lines + 1]
    return (
        layer_output,
        input_grad[None],
        late[:lines].reshape(width),
        sums_one[0],
        sums_one[1][:, :HD],
        sums_one[1][:, HD:],
        query_terms[:HD] + query_terms[HD:],
        key_terms[:HD],
        sums_one[2].T,
        late[lines : 2 * lines].reshape(width),
        router_part[:, :EXPERTS],
        expert_grads[:, :, :inner],
        expert_grads[:, :, inner : 2 * inner],
        expert_grads[:, :, 2 * inner :].transpose(0, 2, 1),
    )


def solution(mesh):
    axes = ("z", "y_lo", "y_hi", "x", "core")
    return jax.shard_map(
        shards,
        mesh=jax.sharding.Mesh(mesh.devices.reshape(4, 2, 2, 4, 2), axes),
        in_specs=(
            P(COL, ROW, None),
            P(),
            P(COL, ROW),
            P(COL, ROW),
            P(COL, ROW),
            P(),
            P(),
            P(ROW, COL),
            P(),
            P(COL, None),
            P(ROW, COL, None),
            P(ROW, COL, None),
            P(ROW, None, COL),
            P(COL, None, None),
            P(COL, None, None),
            P(COL),
            P(COL, ROW, None),
        ),
        out_specs=(
            P(COL, ROW, None),
            P(COL, ROW, None),
            P(),
            P(COL, ROW),
            P(COL, ROW),
            P(COL, ROW),
            P(),
            P(),
            P(ROW, COL),
            P(),
            P(COL, None),
            P(ROW, COL, None),
            P(ROW, COL, None),
            P(ROW, None, COL),
        ),
        check_vma=False,
    )
```

```python
import jax
import jax.numpy as jnp
import numpy as np
from jax import lax
from jax.experimental import pallas as pl
from jax.experimental.pallas import tpu as pltpu
from jax.sharding import PartitionSpec as P

HD = 64
CAP = 448
ROWS = 8
COLS = 16
BLK = 128
LEN = ROWS * BLK
LOCAL = 4
EXPERTS = 32
EPS = 1e-06
BF = jnp.bfloat16
F32 = jnp.float32
SM = pl.BlockSpec(memory_space=pltpu.SMEM)
MIB = 1 << 20


def dot(a, b):
    return lax.dot_general(a, b, (((1,), (0,)), ((), ())), preferred_element_type=F32)


def dot_nt(a, b):
    return lax.dot_general(a, b, (((1,), (1,)), ((), ())), preferred_element_type=F32)


def dot_tn(a, b):
    return lax.dot_general(a, b, (((0,), (0,)), ((), ())), preferred_element_type=F32)


def shape(dims, kind):
    return jax.ShapeDtypeStruct(dims, kind)


def whole(value):
    dims = value.shape
    return pl.BlockSpec(dims, lambda i: (0,) * len(dims))


def call(body, outs, *args, grid=1, ins=None, out_specs=None, scratch=(), limit=56):
    ins, out_specs = ins or {}, out_specs or {}
    return pl.pallas_call(
        body,
        grid=(grid,),
        out_shape=outs,
        in_specs=[ins.get(i, whole(value)) for i, value in enumerate(args)],
        out_specs=[out_specs.get(i, whole(value)) for i, value in enumerate(outs)],
        scratch_shapes=list(scratch),
        compiler_params=pltpu.CompilerParams(vmem_limit_bytes=limit * MIB),
        cost_estimate=pl.CostEstimate(flops=0, bytes_accessed=0, transcendentals=0),
    )(*args)


ROW = ("z", "y_lo")
COL = ("y_hi", "x", "core")


SWAP = [(0, 1), (1, 0)]


def together(*values):
    return lax.optimization_barrier(values)


def send(blocks, axes):
    return lax.all_to_all(blocks, axes, 0, 0)


def gather(own, axes, count):
    return send(jnp.broadcast_to(own[None], (count,) + own.shape), axes)


def shift(values, axis, step):
    return lax.ppermute(values, axis, [(i, (i - step) % 4) for i in range(4)])


def in_order(own, other, axis, dim=0):
    first = lax.axis_index(axis) == 0
    return jnp.where(first, jnp.stack([own, other], dim), jnp.stack([other, own], dim))


def swap_halves(values, axis):
    first = lax.axis_index(axis) == 0
    kept = jnp.where(first, values[0], values[1])
    given = jnp.where(first, values[1], values[0])
    return kept.astype(F32) + lax.ppermute(given, axis, SWAP).astype(F32)


def ring_sum(blocks, axis):
    result = blocks[0].astype(F32)
    for k in range(1, 4):
        result = result + shift(blocks[k], axis, -k).astype(F32)
    return result


def from_here(values, axis, dim):
    here = lax.axis_index(axis)
    return [lax.dynamic_index_in_dim(values, (here + k) % 4, dim, False) for k in range(4)]


def beside(values, whole_sums):
    lines = values.reshape(-1, values.shape[-1])
    high = whole_sums.astype(BF)
    return jnp.concatenate([lines, high, (whole_sums - high.astype(F32)).astype(BF)], axis=0)


def apart(message, dims):
    count = 1
    for size in dims[:-1]:
        count *= size
    rest = message[count:]
    half = rest.shape[0] // 2
    return message[:count].reshape(dims), rest[:half] + rest[half:]


def kept_and_given(values, axis):
    here = lax.axis_index(axis)
    return (
        lax.dynamic_index_in_dim(values, here, 0, False),
        lax.dynamic_index_in_dim(values, 1 - here, 0, False),
    )


def swap_both(values, sums, axis):
    first = lax.axis_index(axis) == 0
    kept = jnp.where(first, values[0], values[1])
    given = jnp.where(first, values[1], values[0])
    got = lax.ppermute(beside(given, sums), axis, SWAP).astype(F32)
    got, more = apart(got, kept.shape)
    return kept.astype(F32) + got, sums + more


def ring_both(blocks, sums, axis):
    result, dims = blocks[0].astype(F32), blocks[0].shape
    added = sums
    for k in range(1, 4):
        got, more = apart(shift(beside(blocks[k], sums), axis, -k).astype(F32), dims)
        result, added = result + got, added + more
    return result, added


def swapped(own, axis):
    return in_order(own, lax.ppermute(own, axis, SWAP), axis)


def lane_ids(rows):
    return lax.broadcasted_iota(jnp.int32, (rows, 2 * HD), 1)


def half_mean(values, lanes):
    low = jnp.sum(jnp.where(lanes < HD, values, 0.0), axis=-1, keepdims=True)
    high = jnp.sum(jnp.where(lanes < HD, 0.0, values), axis=-1, keepdims=True)
    return jnp.where(lanes < HD, low, high) * (1.0 / HD)


def turn(values, cosine, sine, lanes):
    swapped = jnp.where(
        (lanes & (HD - 1)) < HD // 2,
        pltpu.roll(values, 2 * HD - HD // 2, 1),
        pltpu.roll(values, HD // 2, 1),
    )
    return values * cosine + swapped * sine


def turn_tables():
    frequency = np.float32(10000.0) ** (np.arange(HD // 2, dtype=np.float32) * np.float32(-2 / HD))
    angles = np.arange(LEN, dtype=np.float32)[:, None] * frequency[None, :].astype(np.float32)
    cosine, sine = np.cos(angles), np.sin(angles)
    return (
        np.concatenate([cosine] * 4, axis=1).astype(np.float32),
        np.concatenate([-sine, sine] * 2, axis=1).astype(np.float32),
    )


def attend_kernel(*refs):
    place, tokens, here, there, query_gain, key_gain, cosine, sine = refs[:8]
    pre, query, keyval, out, weight, out_weight, router = refs[8:15]
    key_low, key_high, val_low, val_high = refs[15:]
    size = here.shape[2]
    for core, ring in enumerate((here, there)):
        for k in range(4):
            for y in range(2):
                block = y * 8 + ((place[1] + k) & 3) * 2 + (place[2] ^ core)
                rows = pl.ds(pl.multiple_of(block * size, size), size)
                weight[rows, :] = ring[k, y, :, : 4 * HD]
                out_weight[rows, :] = ring[k, y, :, 4 * HD : 6 * HD]
                router[rows, :] = ring[k, y, :, 6 * HD :]
    lanes = lane_ids(BLK)
    for j in range(ROWS):
        rows = pl.ds(j * BLK, BLK)
        block = dot(tokens[j], weight[...])
        pre[rows, :] = block
        cos_rows, sin_rows = cosine[rows, :], sine[rows, :]
        q_pre, kv_pre = block[:, : 2 * HD], block[:, 2 * HD :]
        q_scale = lax.rsqrt(half_mean(q_pre * q_pre, lanes) + EPS)
        turned = turn(q_pre * q_scale * query_gain[...], cos_rows, sin_rows, lanes)
        query[rows, :] = turned.astype(BF) * HD ** (-0.5)
        k_scale = lax.rsqrt(half_mean(kv_pre * kv_pre, lanes) + EPS)
        turned = turn(kv_pre * k_scale * key_gain[...], cos_rows, sin_rows, lanes)
        key = jnp.where(lanes < HD, turned, 0.0)
        val = jnp.where(lanes < HD, 0.0, kv_pre)
        keyval[rows, :] = (key + val).astype(BF)
        key_low[rows, :] = key.astype(BF)
        key_high[rows, :] = pltpu.roll(key, HD, 1).astype(BF)
        val_low[rows, :] = pltpu.roll(val, HD, 1).astype(BF)
        val_high[rows, :] = val.astype(BF)
    prefix = place[0]
    size = 2 * BLK
    key_at = lax.broadcasted_iota(jnp.int32, (size, LEN), 1)

    def step(index, carry):
        rows = pl.ds(pl.multiple_of(index * size, size), size)
        q_rows = query[rows, :]
        at = lax.broadcasted_iota(jnp.int32, (size, 1), 0) + index * size
        visible = key_at < jnp.maximum(at + 1, prefix)
        mixed = jnp.zeros((size, 2 * HD), F32)
        for keys, vals in ((key_low, val_low), (key_high, val_high)):
            weights = jnp.where(visible, jnp.exp(dot_nt(q_rows, keys[...])), 0.0)
            inverse = 1.0 / jnp.sum(weights, axis=-1, keepdims=True)
            mixed += dot((weights * inverse).astype(BF), vals[...])
        mixed = mixed.astype(BF)
        out[0, index] = mixed[:BLK]
        out[1, index] = mixed[BLK:]
        return carry

    lax.fori_loop(0, LEN // size, step, 0, unroll=True)


def share_kernel(mine, other, weight, there, part):
    value = dot_nt(mine[...].reshape(LEN // 2, -1), weight[...])
    value += dot_nt(other[...].reshape(LEN // 2, -1), there[...])
    part[...] = value.astype(BF).reshape(part.shape)


def order_kernel(place, ring, there):
    size = ring.shape[3]
    for core in range(2):
        for k in range(4):
            for y in range(2):
                block = y * 8 + ((place[1] + k) & 3) * 2 + (place[2] ^ core)
                rows = pl.ds(pl.multiple_of(block * size, size), size)
                there[rows, :] = ring[core, k, y]


def put_blocks(first, mine, given, which, value):
    size = value.shape[0] // COLS
    for block in range(COLS // 2):
        rows = pl.ds((which * 8 + block) * size, size)
        even = value[2 * block * size : (2 * block + 1) * size]
        odd = value[(2 * block + 1) * size : (2 * block + 2) * size]
        mine[rows, :] = jnp.where(first, even, odd)
        given[rows, :] = jnp.where(first, odd, even)


def attend_back_kernel(*refs):
    place, middle, out_weight, tokens, weight, query_gain, key_gain, cosine, sine = refs[:9]
    pre, query, keyval, heads, router_sums, pre_gain, mid_sum = refs[9:16]
    sent, mine, given, late = refs[16:20]
    key_low, key_high, val_low, val_high, key_t, grads, q_grad, kv_grad, low = refs[20:]
    lanes = lane_ids(BLK)
    for j in range(ROWS):
        rows = pl.ds(j * BLK, BLK)
        both = keyval[rows, :].astype(F32)
        key = jnp.where(lanes < HD, both, 0.0)
        val = jnp.where(lanes < HD, 0.0, both)
        key_two = pltpu.roll(key, HD, 1)
        key_low[rows, :] = key.astype(BF)
        key_high[rows, :] = key_two.astype(BF)
        val_low[rows, :] = pltpu.roll(val, HD, 1).astype(BF)
        val_high[rows, :] = val.astype(BF)
        key_t[:, j * BLK : (j + 1) * BLK] = (key + key_two).T.astype(BF)
        grads[rows, :] = dot(middle[j], out_weight[...]).astype(BF)
    kv_grad[...] = jnp.zeros_like(kv_grad)
    prefix = place[0]
    size = 2 * BLK
    key_at = lax.broadcasted_iota(jnp.int32, (LEN, size), 0)
    wide = lane_ids(size)

    def step(index, carry):
        rows = pl.ds(pl.multiple_of(index * size, size), size)
        q_rows, g_rows = query[rows, :], grads[rows, :]
        q_wide, g_wide = q_rows.astype(F32), g_rows.astype(F32)
        row_at = lax.broadcasted_iota(jnp.int32, (1, size), 1) + index * size
        visible = key_at < jnp.maximum(row_at + 1, prefix)
        q_t = []
        for head, (keys, vals) in enumerate(((key_low, val_low), (key_high, val_high))):
            weights = jnp.where(visible, jnp.exp(dot_nt(keys[...], q_rows)), 0.0)
            probs = weights * (1.0 / jnp.sum(weights, axis=0, keepdims=True))
            back = dot_nt(vals[...], g_rows)
            delta = jnp.sum(probs * back, axis=0, keepdims=True)
            score = (probs * (back - delta)).astype(BF)
            q_t.append(dot(key_t[head * HD : (head + 1) * HD, :], score))
            q_side = q_wide if head == 0 else pltpu.roll(q_wide, HD, 1)
            g_side = pltpu.roll(g_wide, HD, 1) if head == 0 else g_wide
            q_side = jnp.where(wide < HD, q_side, 0.0).astype(BF)
            g_side = jnp.where(wide < HD, 0.0, g_side).astype(BF)
            kv_grad[...] += dot(score, q_side) + dot(probs.astype(BF), g_side)
        q_grad[rows, :] = jnp.concatenate(q_t, axis=0).T * HD ** (-0.5)
        return carry

    lax.fori_loop(0, LEN // size, step, 0, unroll=True)
    q_gain, k_gain = query_gain[...], key_gain[...]
    q_terms = jnp.zeros((1, 2 * HD), F32)
    k_terms = jnp.zeros((1, 2 * HD), F32)
    for j in range(ROWS):
        rows = pl.ds(j * BLK, BLK)
        cos_rows, sin_rows = cosine[rows, :], -sine[rows, :]
        block = pre[rows, :]
        q_pre, kv_pre = block[:, : 2 * HD], block[:, 2 * HD :]
        q_scale = lax.rsqrt(half_mean(q_pre * q_pre, lanes) + EPS)
        q_hat = q_pre * q_scale
        turned = turn(q_grad[rows, :], cos_rows, sin_rows, lanes)
        q_terms += jnp.sum(q_hat * turned, axis=0, keepdims=True)
        inner = turned * q_gain
        q_back = q_scale * (inner - q_hat * half_mean(inner * q_hat, lanes))
        low[rows, : 2 * HD] = q_back.astype(BF)
        k_scale = lax.rsqrt(half_mean(kv_pre * kv_pre, lanes) + EPS)
        k_hat = kv_pre * k_scale
        both = kv_grad[rows, :]
        turned = turn(both, cos_rows, sin_rows, lanes)
        k_terms += jnp.sum(k_hat * turned, axis=0, keepdims=True)
        inner = turned * k_gain
        k_back = k_scale * (inner - k_hat * half_mean(inner * k_hat, lanes))
        low[rows, 2 * HD :] = jnp.where(lanes < HD, k_back, both).astype(BF)
    column = jnp.zeros((1, tokens.shape[2]), F32)
    count = LEN // 4
    for j in range(4):
        share = dot_nt(low[pl.ds(j * count, count), :], weight[...])
        sent[0, j] = low[pl.ds(j * count, BLK), :]
        sent[1, j] = low[pl.ds(j * count + BLK, BLK), :]
        held = tokens[pl.ds(2 * j, 2)].reshape(count, -1).astype(F32)
        column += jnp.sum(held * share, axis=0, keepdims=True)
    column = column / pre_gain[...]
    tall = [column[:, k : k + 2 * HD] for k in range(0, column.shape[1], 2 * HD)]
    tall += [mid_sum[:, k : k + 2 * HD] for k in range(0, column.shape[1], 2 * HD)]
    tall += [q_terms, k_terms, jnp.zeros((6, 2 * HD), F32)]
    total = jnp.concatenate(tall, axis=0)
    high = total.astype(BF)
    late[...] = total
    given[-48:, :] = jnp.concatenate([high, (total - high.astype(F32)).astype(BF)], axis=0)
    first = place[1] == 0
    tall = tokens[...].reshape(LEN, -1)
    ordered = jnp.concatenate([heads[j % 2, j // 2] for j in range(ROWS)], axis=0)
    put_blocks(first, mine, given, 0, dot_tn(tall, low[:, : 2 * HD]).astype(BF))
    put_blocks(first, mine, given, 1, dot_tn(tall, low[:, 2 * HD :]).astype(BF))
    put_blocks(first, mine, given, 2, dot_tn(middle[...].reshape(LEN, -1), ordered).astype(BF))
    put_blocks(first, mine, given, 3, router_sums[...])


def norm_kernel(x_in, gain, copies):
    value = x_in[...].astype(F32)
    scale = lax.rsqrt(jnp.mean(value * value, axis=-1, keepdims=True) + EPS)
    normed = (value * scale * gain[...]).astype(BF)
    for k in range(ROWS):
        copies[k] = normed


def middle_kernel(x_in, gain, parts, middle, copies):
    value = x_in[...].astype(F32)
    for k in range(parts.shape[0]):
        value += parts[k].astype(F32)
    middle[...] = value
    scale = lax.rsqrt(jnp.mean(value * value, axis=-1, keepdims=True) + EPS)
    normed = (value * scale * gain[...]).astype(BF)
    for k in range(ROWS):
        copies[k] = normed


def middle_back_kernel(middle_in, gain, upstream, parts, grad, copies, gain_sum):
    value = middle_in[...]
    back = parts[0].astype(F32)
    for k in range(1, ROWS):
        back += parts[k].astype(F32)
    scale = lax.rsqrt(jnp.mean(value * value, axis=-1, keepdims=True) + EPS)
    hat = value * scale
    gain_sum[...] = jnp.sum(hat * back, axis=0, keepdims=True)
    inner = back * gain[...]
    result = upstream[...].astype(F32) + scale * (
        inner - hat * jnp.mean(inner * hat, axis=-1, keepdims=True)
    )
    grad[...] = result
    rounded = result.astype(BF)
    for k in range(ROWS):
        copies[k] = rounded


def pick_rows(slot_rows, expert):
    slots = slot_rows[pl.ds(expert, 1), :]
    return (lax.broadcasted_iota(jnp.int32, (CAP, LEN), 0) == slots).astype(BF)


def pick_tokens(slot_cols, rows, count):
    slots = slot_cols[rows, :]
    ids = lax.broadcasted_iota(jnp.int32, (count, BLK), 1)
    tiles = []
    for tile in range(LOCAL * CAP // BLK):
        first = tile * BLK
        hit = None
        for e in range(first // CAP, (first + BLK - 1) // CAP + 1):
            at = slots[:, e : e + 1]
            at = jnp.where(at < 0, at, at + (e * CAP - first))
            hit = ids == at if hit is None else hit | (ids == at)
        tiles.append(hit.astype(BF))
    return jnp.concatenate(tiles, axis=1)


def upstream_kernel(slot_rows, t_0, t_1, t_2, t_3, slot_up):
    choose = pick_rows(slot_rows, pl.program_id(0))
    size = 2 * BLK
    picked = jnp.zeros((CAP, t_0.shape[-1]), F32)
    for k, tokens in enumerate((t_0, t_1, t_2, t_3)):
        picked += dot(choose[:, k * size : (k + 1) * size], tokens[...].reshape(size, -1))
    slot_up[0] = picked.astype(BF)


def expert_kernel(
    slot_rows,
    slot_cols,
    tokens,
    router,
    router_t,
    weights,
    slot_up,
    sums,
    act_gated,
    part,
    logit_grad,
    probs,
    gate_rows,
    pre_grad,
    grads,
    gates,
):
    step = pl.program_id(0)
    inner = act_gated.shape[-1]
    size = tokens.shape[-1] // COLS

    def put(lanes, value):
        for block in range(COLS):
            rows = value[block * size : (block + 1) * size]
            sums[block % 8, block // 8, 0, :, lanes] = rows.astype(BF)

    @pl.when(step == 0)
    def _():
        lanes = lax.broadcasted_iota(jnp.int32, (LEN, BLK), 1)
        logits = jnp.where(lanes < EXPERTS, dot(tokens[...], router[...]), -1e30)
        exps = jnp.exp(logits - jnp.max(logits, axis=-1, keepdims=True))
        values = exps / jnp.sum(exps, axis=-1, keepdims=True)
        probs[...] = values
        gate_rows[...] = values.T[: 2 * LOCAL].astype(BF).astype(F32)

    @pl.when(step < LOCAL)
    def _():
        hit = lax.broadcasted_iota(jnp.int32, (CAP, LEN), 0) == slot_rows[pl.ds(step, 1), :]
        gate = jnp.sum(
            jnp.where(hit, gate_rows[pl.ds(step, 1), :], 0.0), axis=-1, keepdims=True
        )
        picked = dot(hit.astype(BF), tokens[...]).astype(BF)
        raw = dot(slot_up[0], weights[0, :, 2 * inner :])
        both = dot(picked, weights[0, :, : 2 * inner])
        gate_pre, up_pre = both[:, :inner], both[:, inner:]
        sigma = 1.0 / (1.0 + jnp.exp(-gate_pre))
        silu = gate_pre * sigma
        act = (silu * up_pre).astype(BF).astype(F32)
        gate_back = jnp.sum(act * raw, axis=-1, keepdims=True)
        act_gated[0] = (act * gate).astype(BF)
        act_grad = raw * gate
        pre_grad[:, :inner] = (
            act_grad * up_pre * sigma * (1.0 + gate_pre * (1.0 - sigma))
        ).astype(BF)
        pre_grad[:, inner:] = (act_grad * silu).astype(BF)
        rows = pl.ds(pl.multiple_of(step * CAP, CAP), CAP)
        grads[rows, :] = dot_nt(pre_grad[...], weights[0, :, : 2 * inner]).astype(BF)
        lanes = lax.broadcasted_iota(jnp.int32, (CAP, BLK), 1)
        gates[rows, :] = jnp.where(lanes == step, gate_back, 0.0).astype(BF)
        put(pl.ds(0, 2 * inner), dot_tn(picked, pre_grad[...]))
        put(pl.ds(2 * inner, inner), dot_tn(slot_up[0], act_gated[0]))

    @pl.when(step == LOCAL)
    def _():
        count = LEN // 4
        for j in range(LEN // count):
            rows = pl.ds(j * count, count)
            choose = pick_tokens(slot_cols, rows, count)
            gate_back = dot(choose, gates[...])
            own = probs[rows, :]
            weighted = own * gate_back
            logit = weighted - own * jnp.sum(weighted, axis=-1, keepdims=True)
            high = logit.astype(BF).astype(F32)
            both = (high + pltpu.roll(logit - high, EXPERTS, 1)).astype(BF)
            logit_grad[rows, :] = both
            value = (dot(choose, grads[...]) + dot(both, router_t[...])).astype(BF)
            for k in range(count // BLK):
                part[j * (count // BLK) + k] = value[k * BLK : (k + 1) * BLK]


def mix_kernel(
    at, slot_cols, tokens, logit_grad, weights, act_gated, m_0, m_1, m_2, m_3, router_sum, held
):
    step = pl.program_id(0)

    @pl.when(step == 0)
    def _():
        value = dot(logit_grad[...].astype(F32).T.astype(BF), tokens[...])
        given = lax.broadcasted_iota(jnp.int32, (BLK, BLK), 0)
        taken = lax.broadcasted_iota(jnp.int32, (BLK, BLK), 1)
        moved = (given + LOCAL * at[1]) & (EXPERTS - 1)
        order = ((moved == taken) & (given < 2 * EXPERTS)).astype(BF)
        router_sum[...] = dot(value.T.astype(BF), order).astype(BF)

    @pl.when(step < LOCAL)
    def _():
        rows = pl.ds(pl.multiple_of(step * CAP, CAP), CAP)
        held[rows, :] = dot_nt(act_gated[0], weights[0]).astype(BF)

    @pl.when(step == LOCAL)
    def _():
        for k, mix in enumerate((m_0, m_1, m_2, m_3)):
            place = (at[0] + k) & 3
            rows = pl.ds(pl.multiple_of(place * 2 * BLK, 2 * BLK), 2 * BLK)
            value = dot(pick_tokens(slot_cols, rows, 2 * BLK), held[...]).astype(BF)
            mix[0] = value[:BLK]
            mix[1] = value[BLK:]


def shards(
    layer_input,
    prenorm,
    query_proj,
    key_proj,
    value_proj,
    querynorm,
    keynorm,
    out_proj,
    midnorm,
    router,
    gate_proj,
    up_proj,
    down_proj,
    routes,
    slot_ids,
    prefix,
    cotangent,
):
    width = layer_input.shape[-1]
    inner = gate_proj.shape[-1]
    row = lax.axis_index(ROW)
    z = lax.axis_index("z")
    at = jnp.stack([z, row]).astype(jnp.int32)
    col_rows = width // COLS

    x_low = layer_input[0]
    x = x_low.astype(F32)
    scale_one = lax.rsqrt(jnp.mean(x * x, axis=-1, keepdims=True) + EPS)
    copied = shape((ROWS, BLK, width), BF)
    (copies,) = call(norm_kernel, (copied,), x_low, prenorm[None, :], limit=16)
    router_own = jnp.pad(router, ((0, 0), (0, BLK - EXPERTS)))
    small = swapped(
        jnp.concatenate([query_proj, key_proj, value_proj, out_proj.T, router_own], axis=1), "y_hi"
    )
    upstream = swapped(cotangent[0], "y_lo")
    copies, upstream, small = together(copies, upstream, small)
    upstream = [upstream] + [shift(upstream, "z", k) for k in range(1, 4)]
    tokens_one = send(copies, ROW)
    experts = lax.all_gather(
        jnp.concatenate([gate_proj, up_proj, down_proj.transpose(0, 2, 1)], axis=2),
        COL,
        axis=1,
        tiled=True,
    )
    small = jnp.stack([small] + [shift(small, "x", k) for k in range(1, 4)])
    small_there = lax.ppermute(small, "core", SWAP)
    out_there = jnp.stack([small, small_there])[..., 4 * HD : 6 * HD]
    out_there = lax.ppermute(out_there, "y_lo", SWAP)

    cosine, sine = turn_tables()
    query_gain = jnp.concatenate([querynorm, querynorm])[None, :]
    key_gain = jnp.concatenate([keynorm, keynorm])[None, :]
    side = pltpu.VMEM((LEN, 2 * HD), BF)
    place = jnp.stack([prefix[0], lax.axis_index("x"), lax.axis_index("core")]).astype(jnp.int32)
    pre, query, keyval, attended, qkv_weight, out_weight, router_all = call(
        attend_kernel,
        (
            shape((LEN, 4 * HD), F32),
            shape((LEN, 2 * HD), BF),
            shape((LEN, 2 * HD), BF),
            shape((2, 4, BLK, 2 * HD), BF),
            shape((width, 4 * HD), BF),
            shape((width, 2 * HD), BF),
            shape((width, BLK), BF),
        ),
        place,
        tokens_one,
        small,
        small_there,
        query_gain,
        key_gain,
        cosine,
        sine,
        ins={0: SM},
        scratch=[side] * 4,
        limit=32,
    )
    router_rel = lax.dynamic_slice_in_dim(
        jnp.concatenate([router_all[:, :EXPERTS]] * 2, axis=1), row * LOCAL, EXPERTS, 1
    )
    router_pad = jnp.pad(router_rel, ((0, 0), (0, BLK - EXPERTS)))
    router_t = jnp.pad(
        jnp.concatenate([router_rel.T, router_rel.T], axis=0), ((0, BLK - 2 * EXPERTS), (0, 0))
    )
    mine, given = kept_and_given(attended, "y_lo")
    (out_there,) = call(
        order_kernel,
        (shape((width, 2 * HD), BF),),
        place,
        out_there,
        ins={0: SM},
        limit=16,
    )
    (part_out,) = call(
        share_kernel,
        (shape((4, BLK, width), BF),),
        mine,
        lax.ppermute(given, "y_lo", SWAP),
        out_weight,
        out_there,
        limit=16,
    )
    part_out, *upstream = together(part_out, *upstream)
    parts_out = lax.all_to_all(part_out, "z", 0, 0)
    middle, copies_two = call(
        middle_kernel,
        (shape((BLK, width), F32), copied),
        x_low,
        midnorm[None, :],
        parts_out,
        limit=16,
    )

    ids = row * LOCAL + jnp.arange(2 * LOCAL, dtype=jnp.int32)
    mine = (routes[0][:, :, None] == ids) & (jnp.arange(2 * LOCAL) < LOCAL)
    slot_cols = jnp.sum(jnp.where(mine, slot_ids[0][:, :, None] + 1, 0), axis=1) - 1
    slot_rows = slot_cols.T
    turned_rows = lax.dynamic_slice_in_dim(
        jnp.concatenate([slot_rows, slot_rows], axis=1), z * 2 * BLK, LEN, 1
    )
    last = lambda e: jnp.minimum(e, LOCAL - 1)
    one = lambda *dims: pl.BlockSpec((1,) + dims, lambda e: (last(e),) + (0,) * len(dims))
    down_block = pl.BlockSpec((1, width, inner), lambda e: (last(e), 0, 2))
    tokens_two = send(copies_two, ROW).reshape(LEN, width)
    (slot_up,) = call(
        upstream_kernel,
        (shape((LOCAL, CAP, width), BF),),
        turned_rows,
        *upstream,
        grid=LOCAL,
        out_specs={0: one(CAP, width)},
        limit=24,
    )
    sums, act_gated, part, logit_grad = call(
        expert_kernel,
        (
            shape((COLS // 2, 2, LOCAL, col_rows, 3 * inner), BF),
            shape((LOCAL, CAP, inner), BF),
            copied,
            shape((LEN, BLK), BF),
        ),
        slot_rows,
        slot_cols,
        tokens_two,
        router_pad,
        router_t,
        experts,
        slot_up,
        ins={5: one(width, 3 * inner), 6: one(CAP, width)},
        grid=LOCAL + 1,
        out_specs={
            0: pl.BlockSpec(
                (COLS // 2, 2, 1, col_rows, 3 * inner), lambda e: (0, 0, last(e), 0, 0)
            ),
            1: one(CAP, inner),
        },
        scratch=[
            pltpu.VMEM((LEN, BLK), F32),
            pltpu.VMEM((2 * LOCAL, LEN), F32),
            pltpu.VMEM((CAP, 2 * inner), BF),
            pltpu.VMEM((LOCAL * CAP, width), BF),
            pltpu.VMEM((LOCAL * CAP, BLK), BF),
        ],
        limit=50,
    )
    parts_two = send(part, ROW)
    *mix, router_sums = call(
        mix_kernel,
        (*[shape((2, BLK, width), BF)] * 4, shape((width, BLK), BF)),
        at,
        slot_cols,
        tokens_two,
        logit_grad,
        experts,
        act_gated,
        ins={0: SM, 4: down_block, 5: one(CAP, inner)},
        grid=LOCAL + 1,
        scratch=[pltpu.VMEM((LOCAL * CAP, width), BF)],
        limit=32,
    )
    halves = lax.psum_scatter(sums, ("x", "core"), scatter_dimension=0, tiled=False)

    middle_grad, copies_mid, midnorm_part = call(
        middle_back_kernel,
        (shape((BLK, width), F32), copied, shape((1, width), F32)),
        middle,
        midnorm[None, :],
        cotangent[0],
        parts_two,
        limit=16,
    )
    group_mid = send(copies_mid, ROW)
    group_mid, qkv_weight, *mix = together(group_mid, qkv_weight, *mix)
    qkv_there = lax.ppermute(qkv_weight, "y_lo", SWAP)
    mix = mix[:1] + [shift(block, "z", -k) for k, block in enumerate(mix) if k]
    low, mine, given, late = call(
        attend_back_kernel,
        (
            shape((2, 4, BLK, 4 * HD), BF),
            shape((2 * width, 2 * HD), BF),
            shape((2 * width + 48, 2 * HD), BF),
            shape((24, 2 * HD), F32),
        ),
        jnp.stack([prefix[0], lax.axis_index("core")]).astype(jnp.int32),
        group_mid,
        out_weight,
        tokens_one,
        qkv_weight,
        query_gain,
        key_gain,
        cosine,
        sine,
        pre,
        query,
        keyval,
        attended,
        router_sums,
        prenorm[None, :],
        midnorm_part,
        ins={0: SM},
        scratch=[side] * 4
        + [
            pltpu.VMEM((2 * HD, LEN), BF),
            side,
            pltpu.VMEM((LEN, 2 * HD), F32),
            pltpu.VMEM((LEN, 2 * HD), F32),
            pltpu.VMEM((LEN, 4 * HD), BF),
        ],
    )
    low, given, halves, qkv_there, *mix = together(low, given, halves, qkv_there, *mix)

    lines = width // (2 * HD)
    dims = (4, 2, 4, col_rows, 2 * HD)
    sums_one, more = apart(lax.ppermute(given, "core", SWAP).astype(F32), dims)
    sums_one, late = mine.astype(F32).reshape(dims) + sums_one, late + more
    sums_one, late, low, *mix = together(sums_one.astype(BF), late, low, *mix)
    low_mine, low_given = kept_and_given(low, "y_lo")
    (part_one,) = call(
        share_kernel,
        (shape((4, BLK, width), BF),),
        low_mine,
        lax.ppermute(low_given, "y_lo", SWAP),
        qkv_weight,
        qkv_there,
        limit=16,
    )
    parts_one = lax.all_to_all(part_one, "z", 0, 0)
    normed_one_grad = jnp.sum(parts_one.astype(F32), axis=0)
    mixed = sum(block.astype(F32) for block in mix).astype(BF)
    sums_one, late = ring_both(from_here(sums_one, "x", 2), late, "x")
    layer_output = (middle + swap_halves(mixed, "y_lo")).astype(BF)[None]
    sums_one, late = swap_both(jnp.moveaxis(sums_one.astype(BF), 1, 0), late, "y_hi")
    router_part = sums_one[3].astype(BF)
    router_part, late = swap_both(jnp.stack([router_part] * 2), late, "y_lo")
    router_part, late, halves = together(router_part.astype(BF), late, halves)
    expert_grads = swap_halves(halves, "y_hi")
    router_part, late = ring_both([router_part] * 4, late, "z")
    hat = x * scale_one
    weighted = normed_one_grad * prenorm
    input_grad = middle_grad + scale_one * (
        weighted - hat * jnp.mean(weighted * hat, axis=-1, keepdims=True)
    )
    query_terms, key_terms = late[2 * lines], late[2 * lines + 1]
    return (
        layer_output,
        input_grad[None],
        late[:lines].reshape(width),
        sums_one[0],
        sums_one[1][:, :HD],
        sums_one[1][:, HD:],
        query_terms[:HD] + query_terms[HD:],
        key_terms[:HD],
        sums_one[2].T,
        late[lines : 2 * lines].reshape(width),
        router_part[:, :EXPERTS],
        expert_grads[:, :, :inner],
        expert_grads[:, :, inner : 2 * inner],
        expert_grads[:, :, 2 * inner :].transpose(0, 2, 1),
    )


def solution(mesh):
    axes = ("z", "y_lo", "y_hi", "x", "core")
    return jax.shard_map(
        shards,
        mesh=jax.sharding.Mesh(mesh.devices.reshape(4, 2, 2, 4, 2), axes),
        in_specs=(
            P(COL, ROW, None),
            P(),
            P(COL, ROW),
            P(COL, ROW),
            P(COL, ROW),
            P(),
            P(),
            P(ROW, COL),
            P(),
            P(COL, None),
            P(ROW, COL, None),
            P(ROW, COL, None),
            P(ROW, None, COL),
            P(COL, None, None),
            P(COL, None, None),
            P(COL),
            P(COL, ROW, None),
        ),
        out_specs=(
            P(COL, ROW, None),
            P(COL, ROW, None),
            P(),
            P(COL, ROW),
            P(COL, ROW),
            P(COL, ROW),
            P(),
            P(),
            P(ROW, COL),
            P(),
            P(COL, None),
            P(ROW, COL, None),
            P(ROW, COL, None),
            P(ROW, None, COL),
        ),
        check_vma=False,
    )
```
